256 devices in a mesh: dom: 64 (over y, z, core), rep: 4 (over x).
Axes of the slice: x: 4, y: 4, z: 8, core: 2. Of those that a mesh axis runs over, the one named last changes fastest.
Arguments:
- features: bfloat16 [1048576, 128], P(('dom', 'rep')), may hold values from -6 to 6
- out_grad: bfloat16 [1048576, 256], P(('dom', 'rep')), may hold values from -6 to 6
- w_self: bfloat16 [128, 256], replicated, may hold values from -0.5 to 0.5
- w_nbr: bfloat16 [128, 256], replicated, may hold values from -0.5 to 0.5
- hub_rows: int32 [4096], P(('dom', 'rep')), may hold values from 0 to 4095
- send_rows: int32 [16384, 32], P(('dom', 'rep')), may hold values from 0 to 4095
- send_counts: int32 [16384], P(('dom', 'rep')), may hold values from 0 to 32
- tile_targets: int32 [32768], P(('dom', 'rep')), may hold values from 0 to 31, as said below
- tile_sources: int32 [32768], P(('dom', 'rep')), may hold values from 0 to 79
- tile_count: int32 [256], P(('dom', 'rep')), may hold values from 32 to 128, as said below
- tile_weights: bfloat16 [32768, 128, 128], P(('dom', 'rep')), may hold values from 0 to 1, as said below
Outputs:
- hidden_out: bfloat16 [1048576, 256], P(('dom', 'rep'))
- grad_features: float32 [1048576, 128], P(('dom', 'rep'))
- grad_w_self: float32 [128, 256], replicated
- grad_w_nbr: float32 [128, 256], replicated
The draws below stay inside these ranges and needn't reach their ends.
Inputs may be any that keep to these rules, and one draw needn't show every extreme that they name: `hub_rows`: rows of the device that owns the entry. `send_rows`: rows of the sending device; list q of a device goes to the device at dom index q with the same rep index. `tile_targets`: the first 32 slots of each device name its 32 target blocks in order. `tile_sources`: source blocks 0 to 31 are the device's own rows, then come the hub rows, then the halo slots. `tile_count`: some device uses all 128 slots and some only 32. `tile_weights`: Nonnegative; most entries are zero.
All inputs are finite; a program needn't handle non-finite values.
Results may differ from the reference program's by a relative error of at most 0.0051.
Values may be sent and summed in bfloat16 or wider, within the bound.
No kernel may reach another device: no remote copies, remote signals or barrier semaphores. Data moves between devices by JAX's collectives and lax.ppermute only.
A program may use at most 128 MiB of HBM per device.

```python
import math
import jax
import jax.numpy as jnp
from jax import lax

F = 128
H = 256
NODE_DEV = 4096
HUB_DEV = 16
CAP = 32
BLOCK = 128
NODES = 1048576
HUBS = 4096
HALO = 2048
PEER_LISTS = 16384
TB = 32
SB = 80
TILE_CAP = 128
N_DOM = 64
N_REP = 4
DEVICES = 256


def draw_tile_targets(key, part):
    key = jax.random.fold_in(key, 11)
    remainder = jax.random.randint(key, (DEVICES, TILE_CAP - TB), 0, TB, dtype=jnp.int32)
    leading = jnp.broadcast_to(jnp.arange(TB, dtype=jnp.int32)[None, :], (DEVICES, TB))
    return jnp.concatenate([leading, remainder], 1).reshape(DEVICES * TILE_CAP)


def draw_tile_count(key, part):
    key = jax.random.fold_in(key, 12)
    count_key, place_key = jax.random.split(key)
    counts = jax.random.randint(count_key, (DEVICES,), TB, TILE_CAP + 1, dtype=jnp.int32)
    fullest = jax.random.randint(place_key, (), 0, DEVICES, dtype=jnp.int32)
    emptiest = (fullest + 1) % DEVICES
    return counts.at[fullest].set(TILE_CAP).at[emptiest].set(TB)


def draw_tile_weights(key, part):
    key = jax.random.fold_in(key, 13)
    mask_key, value_key = jax.random.split(key)
    tile_shape = (DEVICES * TILE_CAP, BLOCK, BLOCK)
    edge_hits = jax.random.randint(mask_key, tile_shape, 0, 12, dtype=jnp.int32) == 0
    values = jnp.exp(jax.random.uniform(value_key, tile_shape, jnp.float32, math.log(0.05), 0.0))
    return jnp.where(edge_hits, values, 0.0).astype(jnp.bfloat16)


def set_ends(entries, stream_key, least, high):
    dims = entries.shape
    index_at = [jax.random.randint(jax.random.fold_in(stream_key, axis), (), 0, dims[axis]) for axis in range(len(dims))]
    entries = entries.at[tuple(index_at)].set(least)
    longest = dims.index(max(dims))
    index_at[longest] = (index_at[longest] + 1) % dims[longest]
    return entries.at[tuple(index_at)].set(high)


def level_of(key, dims, cuts, smallest, largest):
    loudness = 1.0
    for dim, shards_of in cuts:
        heights = jax.random.uniform(jax.random.fold_in(jax.random.fold_in(key, 6), dim), (shards_of,), jnp.float32, smallest / len(cuts), largest / len(cuts))
        loudness = loudness * jnp.repeat(jnp.exp(heights), dims[dim] // shards_of).reshape((-1,) + (1,) * (len(dims) - 1 - dim))
    return loudness


def bell_draw(stream_key, shape, deviation, most, cuts=(), held_as=jnp.bfloat16):
    array = deviation * jax.random.normal(stream_key, shape, jnp.float32)
    if cuts:
        array = array * level_of(stream_key, shape, cuts, -0.22, 0.18)
    return jnp.clip(array, -most, most).astype(held_as)


def setup_inputs(seed: int = 0) -> dict:
    keys = jax.random.split(jax.random.key(seed), 12)
    features = bell_draw(keys[0], (NODES, F), 1.0, 6.0, ((0, 256),))
    out_grad = bell_draw(keys[1], (NODES, H), 1.0, 6.0, ((0, 256),))
    w_self = bell_draw(keys[2], (F, H), F ** -0.5, 0.5)
    w_nbr = bell_draw(keys[3], (F, H), F ** -0.5, 0.5)
    hub_rows = set_ends(jax.random.randint(keys[4], (HUBS,), 0, NODE_DEV), jax.random.fold_in(keys[4], 1), 0, NODE_DEV - 1).astype(jnp.int32)
    send_rows = set_ends(jax.random.randint(keys[5], (PEER_LISTS, CAP), 0, NODE_DEV), jax.random.fold_in(keys[5], 1), 0, NODE_DEV - 1).astype(jnp.int32)
    send_counts = set_ends(jax.random.randint(keys[6], (PEER_LISTS,), 0, CAP + 1), jax.random.fold_in(keys[6], 1), 0, CAP).astype(jnp.int32)
    tile_targets = draw_tile_targets(jax.random.fold_in(keys[11], 71), 0)
    tile_sources = set_ends(jax.random.randint(keys[8], (DEVICES * TILE_CAP,), 0, SB), jax.random.fold_in(keys[8], 1), 0, SB - 1).astype(jnp.int32)
    tile_count = draw_tile_count(jax.random.fold_in(keys[11], 71), 0)
    tile_weights = draw_tile_weights(jax.random.fold_in(keys[11], 71), 0)
    return dict(features=features, out_grad=out_grad, w_self=w_self, w_nbr=w_nbr, hub_rows=hub_rows, send_rows=send_rows, send_counts=send_counts, tile_targets=tile_targets, tile_sources=tile_sources, tile_count=tile_count, tile_weights=tile_weights)


def silu_slope(preact):
    sigmoid = jax.nn.sigmoid(preact)
    return sigmoid * (1.0 + preact * (1.0 - sigmoid))

def rows_added(values, row_ids):
    return jax.ops.segment_sum(values, row_ids, num_segments=NODE_DEV)

def reference(features, out_grad, w_self, w_nbr, hub_rows, send_rows, send_counts, tile_targets, tile_sources, tile_count, tile_weights):
    highest = lax.Precision.HIGHEST
    feature_width = features.shape[1]
    hidden_width = w_self.shape[1]
    device_ids = jnp.arange(DEVICES, dtype=jnp.int32)
    node_blocks = features.reshape(DEVICES, NODE_DEV, feature_width)
    hub_ids = hub_rows.reshape(DEVICES, HUB_DEV)
    hub_feats = node_blocks[device_ids[:, None], hub_ids].reshape(HUBS, feature_width)
    send_lists = send_rows.reshape(DEVICES, N_DOM, CAP)
    slot_live = jnp.arange(CAP, dtype=jnp.int32)[None, None, :] < send_counts.reshape(DEVICES, N_DOM)[:, :, None]
    outgoing = node_blocks[device_ids[:, None, None], send_lists] * slot_live[:, :, :, None].astype(features.dtype)
    incoming = outgoing.reshape(N_DOM, N_REP, N_DOM, CAP, feature_width).transpose(2, 1, 0, 3, 4).reshape(DEVICES, HALO, feature_width)
    target_ids = jnp.arange(TB, dtype=jnp.int32)
    source_ids = jnp.arange(SB, dtype=jnp.int32)

    def device_pass(totals, slices):
        hub_grads, self_grads, nbr_grads = totals
        local_rows, local_grad, halo_feats, weights, targets, sources, count = slices
        source_rows = jnp.concatenate([local_rows, hub_feats, halo_feats], 0).reshape(SB, BLOCK, feature_width)
        picked = source_rows[sources]
        tile_live = jnp.arange(TILE_CAP, dtype=jnp.int32) < count
        target_hot = ((targets[:, None] == target_ids[None, :]) & tile_live[:, None]).astype(jnp.float32)
        wide_weights = weights.astype(jnp.float32)
        products = jnp.einsum('tij,tjf->tif', wide_weights, picked.astype(jnp.float32), precision=highest)
        numerator = jnp.einsum('tb,tif->bif', target_hot, products, precision=highest).reshape(NODE_DEV, feature_width)
        row_sums = jnp.einsum('tb,ti->bi', target_hot, lax.optimization_barrier(jnp.sum(wide_weights, 2)), precision=highest).reshape(NODE_DEV)
        denominator = jnp.maximum(row_sums, 1.0)
        aggregate = (numerator / denominator[:, None]).astype(jnp.bfloat16)
        preact = jnp.dot(local_rows, w_self, preferred_element_type=jnp.float32) + jnp.dot(aggregate, w_nbr, preferred_element_type=jnp.float32)
        hidden_out = jax.nn.silu(preact).astype(jnp.bfloat16)
        grad_preact = (local_grad.astype(jnp.float32) * silu_slope(preact)).astype(jnp.bfloat16)
        self_term = jnp.dot(local_rows.T, grad_preact, preferred_element_type=jnp.float32)
        nbr_term = jnp.dot(aggregate.T, grad_preact, preferred_element_type=jnp.float32)
        grad_agg = (jnp.dot(grad_preact, w_nbr.T, preferred_element_type=jnp.float32) / denominator[:, None]).astype(jnp.bfloat16)
        grad_tiles = grad_agg.reshape(TB, BLOCK, feature_width)[targets] * tile_live[:, None, None].astype(jnp.bfloat16)
        grad_products = jnp.einsum('tij,tif->tjf', wide_weights, grad_tiles.astype(jnp.float32), precision=highest)
        source_hot = (sources[:, None] == source_ids[None, :]).astype(jnp.float32)
        grad_sources = jnp.einsum('ts,tjf->sjf', source_hot, grad_products, precision=highest).reshape(SB * BLOCK, feature_width)
        grad_local = jnp.dot(grad_preact, w_self.T, preferred_element_type=jnp.float32) + grad_sources[:NODE_DEV]
        hub_term = grad_sources[NODE_DEV:NODE_DEV + HUBS]
        halo_term = grad_sources[NODE_DEV + HUBS:].reshape(N_DOM, CAP, feature_width)
        return ((hub_grads + hub_term, self_grads + self_term, nbr_grads + nbr_term), (hidden_out, grad_local, halo_term))
    start = (jnp.zeros((HUBS, feature_width), jnp.float32), jnp.zeros((feature_width, hidden_width), jnp.float32), jnp.zeros((feature_width, hidden_width), jnp.float32))
    slices = (node_blocks, out_grad.reshape(DEVICES, NODE_DEV, hidden_width), incoming, tile_weights.reshape(DEVICES, TILE_CAP, BLOCK, BLOCK), tile_targets.reshape(DEVICES, TILE_CAP), tile_sources.reshape(DEVICES, TILE_CAP), tile_count)
    totals, stacked = lax.scan(device_pass, start, slices)
    hub_grads, self_grads, nbr_grads = totals
    hidden_out, grad_local, halo_grads = stacked
    returned = halo_grads.reshape(N_DOM, N_REP, N_DOM, CAP, feature_width).transpose(2, 1, 0, 3, 4).reshape(DEVICES, N_DOM, CAP, feature_width)
    returned = returned * slot_live[:, :, :, None].astype(jnp.float32)
    halo_back = jax.vmap(rows_added)(returned.reshape(DEVICES, HALO, feature_width), send_lists.reshape(DEVICES, HALO))
    hub_back = jax.vmap(rows_added)(hub_grads.reshape(DEVICES, HUB_DEV, feature_width), hub_ids)
    grad_features = (grad_local + hub_back + halo_back).reshape(NODES, feature_width)
    grad_scale = 1.0 / math.sqrt(NODES)
    return (hidden_out.reshape(NODES, hidden_width), grad_features, self_grads * grad_scale, nbr_grads * grad_scale)
```

```python
import math

import jax
import jax.numpy as jnp
from jax import lax
from jax.experimental import pallas as pl
from jax.experimental.pallas import tpu as pltpu
from jax.sharding import PartitionSpec as P

BF16 = jnp.bfloat16
F32 = jnp.float32
UNROLL = 4
WEIGHT_CHUNK = 16
ROWS = 256


def smem():
    return pl.BlockSpec(memory_space=pltpu.SMEM)


def vmem():
    return pl.BlockSpec(memory_space=pltpu.VMEM)


def hbm():
    return pl.BlockSpec(memory_space=pl.ANY)


def params(mebibytes):
    return pltpu.CompilerParams(vmem_limit_bytes=mebibytes * 1024 * 1024)


def rows_at(index, size):
    return pl.ds(pl.multiple_of(index * size, size), size)


def pack_kernel(hub_rows, send_rows, send_counts, features, out, wide, staged):
    node_rows = features.shape[0]
    peers, slots = send_rows.shape
    hubs = hub_rows.shape[0]
    wide[:node_rows] = features[...].astype(F32)
    wide[node_rows:] = jnp.zeros((wide.shape[0] - node_rows, wide.shape[1]), F32)
    for h in range(hubs):
        staged[h : h + 1] = wide[pl.ds(hub_rows[h], 1)]
    own_hubs = staged[:hubs].astype(BF16)

    def peer(p, carry):
        live = send_counts[p]
        base = p * slots
        for k in range(slots):
            row = jnp.where(k < live, send_rows[p, k], node_rows)
            staged[pl.ds(base + k, 1)] = wide[pl.ds(row, 1)]
        return carry

    lax.fori_loop(0, peers, peer, 0)

    def emit(p, carry):
        out[p, :slots] = staged[rows_at(p, slots)].astype(BF16)
        out[p, slots:] = own_hubs
        return carry

    lax.fori_loop(0, peers, emit, 0)


def pack(hub_rows, send_rows, send_counts, features):
    peers, slots = send_rows.shape
    hubs = hub_rows.shape[0]
    node_rows, width = features.shape
    return pl.pallas_call(
        pack_kernel,
        out_shape=jax.ShapeDtypeStruct((peers, slots + hubs, width), BF16),
        in_specs=[smem(), smem(), smem(), vmem()],
        out_specs=vmem(),
        scratch_shapes=[
            pltpu.VMEM((node_rows + 8, width), F32),
            pltpu.VMEM((peers * slots, width), F32),
        ],
        compiler_params=params(24),
        name="pack",
    )(hub_rows, send_rows, send_counts, features)


def start_weights(weights, held, sems):
    copies = []
    for c in range(weights.shape[0] // WEIGHT_CHUNK):
        part = pl.ds(c * WEIGHT_CHUNK, WEIGHT_CHUNK)
        copies.append(pltpu.make_async_copy(weights.at[part], held.at[part], sems.at[c]))
        copies[-1].start()
    return copies


def forward_kernel(
    targets,
    sources,
    count,
    weights,
    features,
    received,
    hub1,
    hub2,
    hub3,
    out_grad,
    w_self,
    w_nbr,
    hidden,
    grad_agg,
    grad_self,
    grad_w,
    held,
    source_rows,
    totals,
    w_both,
    grad_total,
    weight_sems,
    feature_sem,
):
    block = weights.shape[1]
    node_rows, width = features.shape
    target_blocks = node_rows // block
    peers = received.shape[0]
    hubs = hub1.shape[1]
    slots = received.shape[1] - hubs
    reps = 4
    weight_copies = start_weights(weights, held, weight_sems)
    feature_copy = pltpu.make_async_copy(features, source_rows.at[pl.ds(0, node_rows)], feature_sem)
    feature_copy.start()
    rep = lax.axis_index("rep")
    hub_base = node_rows
    halo_base = node_rows + peers * reps * hubs

    def place(p, carry):
        source_rows[pl.ds(pl.multiple_of(halo_base + p * slots, slots), slots)] = received[p, :slots]
        for i, piece in enumerate((received, hub1, hub2, hub3)):
            from_rep = lax.rem(rep - i + reps, reps)
            at = pl.multiple_of(hub_base + (p * reps + from_rep) * hubs, hubs)
            source_rows[pl.ds(at, hubs)] = piece[p, slots:] if i == 0 else piece[p]
        return carry

    lax.fori_loop(0, peers, place, 0)
    w_both[: w_self.shape[0]] = w_self[...]
    w_both[w_self.shape[0] :] = w_nbr[...]
    ones = jnp.ones((block, width), BF16)

    def product(t):
        picked = jnp.concatenate([source_rows[rows_at(sources[t], block)], ones], 1)
        return jnp.dot(held[t], picked, preferred_element_type=F32)

    feature_copy.wait()
    leading = target_blocks // WEIGHT_CHUNK
    for copy in weight_copies[:leading]:
        copy.wait()

    def first(g, carry):
        for u in range(UNROLL):
            t = g * UNROLL + u
            totals[t] = product(t)
        return carry

    lax.fori_loop(0, target_blocks // UNROLL, first, 0)
    for copy in weight_copies[leading:]:
        copy.wait()
    live = count[0]

    def more(g, carry):
        slots_at = [target_blocks + g * UNROLL + u for u in range(UNROLL)]
        products = [product(t) for t in slots_at]
        for t, value in zip(slots_at, products):
            target = jnp.where(t < live, targets[t], target_blocks)
            totals[target] += value
        return carry

    lax.fori_loop(0, (live - target_blocks + UNROLL - 1) // UNROLL, more, 0)
    grad_total[...] = jnp.zeros_like(grad_total)
    per_chunk = ROWS // block

    def dense(c, carry):
        rows = rows_at(c, ROWS)
        total = totals[pl.ds(c * per_chunk, per_chunk)].reshape(ROWS, 2 * width)
        inverse = 1.0 / jnp.maximum(total[:, width:], 1.0)
        aggregate = (total[:, :width] * inverse).astype(BF16)
        both = jnp.concatenate([source_rows[rows], aggregate], 1)
        preact = jnp.dot(both, w_both[...], preferred_element_type=F32)
        sigmoid = 1.0 / (1.0 + jnp.exp(-preact))
        activated = preact * sigmoid
        hidden[rows] = activated.astype(BF16)
        slope = sigmoid + activated * (1.0 - sigmoid)
        grad_preact = (out_grad[rows].astype(F32) * slope).astype(BF16)
        grad_total[...] += lax.dot_general(
            both, grad_preact, (((0,), (0,)), ((), ())), preferred_element_type=F32
        )
        back = lax.dot_general(
            grad_preact, w_both[...], (((1,), (1,)), ((), ())), preferred_element_type=F32
        )
        grad_self[rows] = back[:, :width]
        grad_agg[rows] = (back[:, width:] * inverse).astype(BF16)
        return carry

    lax.fori_loop(0, node_rows // ROWS, dense, 0)
    half = grad_total.shape[1] // 2
    grad_w[: grad_total.shape[0]] = grad_total[:, :half]
    grad_w[grad_total.shape[0] :] = grad_total[:, half:]


def forward(targets, sources, count, weights, features, received, pieces, out_grad, w_self, w_nbr):
    node_rows, width = features.shape
    tiles, block, _ = weights.shape
    hidden_width = w_self.shape[1]
    peers = received.shape[0]
    hubs = pieces[0].shape[1]
    slots = received.shape[1] - hubs
    source_rows = node_rows + peers * 4 * hubs + peers * slots
    return pl.pallas_call(
        forward_kernel,
        out_shape=(
            jax.ShapeDtypeStruct((node_rows, hidden_width), BF16),
            jax.ShapeDtypeStruct((node_rows, width), BF16),
            jax.ShapeDtypeStruct((node_rows, width), F32),
            jax.ShapeDtypeStruct((4 * width, hidden_width // 2), F32),
        ),
        in_specs=[smem()] * 3 + [hbm()] * 2 + [vmem()] * 7,
        out_specs=(vmem(),) * 4,
        scratch_shapes=[
            pltpu.VMEM((tiles, block, block), BF16),
            pltpu.VMEM((source_rows, width), BF16),
            pltpu.VMEM((node_rows // block + 1, block, 2 * width), F32),
            pltpu.VMEM((2 * width, hidden_width), BF16),
            pltpu.VMEM((2 * width, hidden_width), F32),
            pltpu.SemaphoreType.DMA((tiles // WEIGHT_CHUNK,)),
            pltpu.SemaphoreType.DMA,
        ],
        compiler_params=params(40),
        name="forward",
    )(targets, sources, count, weights, features, received, *pieces, out_grad, w_self, w_nbr)


def backward_kernel(
    targets,
    sources,
    count,
    weights,
    grad_agg,
    grad_self,
    grad_own,
    halo,
    hub0,
    hub1,
    hub2,
    hub3,
    held,
    totals,
    weight_sems,
):
    block = weights.shape[1]
    node_rows, width = grad_agg.shape
    peers, hubs, _ = hub0.shape
    peers = peers - 1
    slots = halo.shape[1]
    reps = 4
    weight_copies = start_weights(weights, held, weight_sems)
    rep = lax.axis_index("rep")
    totals[:node_rows] = grad_self[...]
    totals[node_rows:] = jnp.zeros((totals.shape[0] - node_rows, width), F32)
    spare = totals.shape[0] // block - 1
    for copy in weight_copies:
        copy.wait()
    live = count[0]

    def step(g, carry):
        slots_at = [g * UNROLL + u for u in range(UNROLL)]
        products = [
            lax.dot_general(
                held[t],
                grad_agg[rows_at(targets[t], block)],
                (((0,), (0,)), ((), ())),
                preferred_element_type=F32,
            )
            for t in slots_at
        ]
        for t, value in zip(slots_at, products):
            source = jnp.where(t < live, sources[t], spare)
            totals[rows_at(source, block)] += value
        return carry

    lax.fori_loop(0, (live + UNROLL - 1) // UNROLL, step, 0)
    grad_own[...] = totals[:node_rows]
    hub_base = node_rows
    halo_base = node_rows + peers * reps * hubs

    def emit(p, carry):
        at = pl.multiple_of(halo_base + p * slots, slots)
        halo[p] = totals[pl.ds(at, slots)].astype(BF16)
        for i, piece in enumerate((hub0, hub1, hub2, hub3)):
            to_rep = lax.rem(rep + i, reps)
            at = pl.multiple_of(hub_base + (p * reps + to_rep) * hubs, hubs)
            piece[p] = totals[pl.ds(at, hubs)].astype(BF16)
        return carry

    lax.fori_loop(0, peers, emit, 0)
    for piece in (hub0, hub1, hub2, hub3):
        piece[peers] = jnp.zeros((hubs, width), BF16)


def backward(targets, sources, count, weights, grad_agg, grad_self, peers, slots, hubs):
    node_rows, width = grad_agg.shape
    tiles, block, _ = weights.shape
    total_rows = node_rows + peers * 4 * hubs + peers * slots + block
    piece = jax.ShapeDtypeStruct((peers + 1, hubs, width), BF16)
    return pl.pallas_call(
        backward_kernel,
        out_shape=(
            jax.ShapeDtypeStruct((node_rows, width), F32),
            jax.ShapeDtypeStruct((peers, slots, width), BF16),
            piece,
            piece,
            piece,
            piece,
        ),
        in_specs=[smem()] * 3 + [hbm()] + [vmem()] * 2,
        out_specs=(vmem(),) * 6,
        scratch_shapes=[
            pltpu.VMEM((tiles, block, block), BF16),
            pltpu.VMEM((total_rows, width), F32),
            pltpu.SemaphoreType.DMA((tiles // WEIGHT_CHUNK,)),
        ],
        compiler_params=params(40),
        name="backward",
    )(targets, sources, count, weights, grad_agg, grad_self)


def merge_kernel(halo, hub0, hub1, hub2, hub3, out, w_parts):
    peers, slots, width = halo.shape
    hubs = hub0.shape[1]
    half = hubs // 2
    reps = 4
    rep = lax.axis_index("rep")
    pieces = (hub0, hub1, hub2, hub3)
    for i, piece in enumerate(pieces):
        pair = piece[peers].astype(F32)
        w_parts[lax.rem(rep - i + reps, reps)] = pair[:half] + pair[half:]
    w_total = ((w_parts[0] + w_parts[1]) + w_parts[2]) + w_parts[3]
    high = w_total.astype(BF16)
    low = (w_total - high.astype(F32)).astype(BF16)
    w_rows = jnp.concatenate([high.astype(F32), low.astype(F32)], 0).astype(BF16)

    def peer(p, carry):
        out[p, :slots] = halo[p]
        total = (hub0[p].astype(F32) + hub1[p].astype(F32)) + (
            hub2[p].astype(F32) + hub3[p].astype(F32)
        )
        out[p, slots : slots + hubs] = total.astype(BF16)
        out[p, slots + hubs :] = w_rows
        return carry

    lax.fori_loop(0, peers, peer, 0)


def merge(halo, pieces):
    peers, slots, width = halo.shape
    hubs = pieces[0].shape[1]
    return pl.pallas_call(
        merge_kernel,
        out_shape=jax.ShapeDtypeStruct((peers, slots + 2 * hubs, width), BF16),
        in_specs=[vmem()] * 5,
        out_specs=vmem(),
        scratch_shapes=[pltpu.VMEM((4, hubs // 2, width), F32)],
        compiler_params=params(24),
        name="merge",
    )(halo, *pieces)


def finish_kernel(hub_rows, send_ids, received, grad_own, out, grad_w, rows, grad_scale):
    peers, message, width = received.shape
    hubs = hub_rows.shape[0]
    slots = message - 2 * hubs
    half = hubs // 2
    node_rows = out.shape[0]

    def place(p, carry):
        rows[rows_at(p, slots)] = received[p, :slots]
        pair = received[p, slots + hubs :].astype(F32)
        grad_w[rows_at(p, half)] = (pair[:half] + pair[half:]) * grad_scale
        return carry + received[p, slots : slots + hubs].astype(F32)

    hub_total = lax.fori_loop(0, peers, place, jnp.zeros((hubs, width), F32))

    def scatter(c, carry):
        at = rows_at(c, ROWS)
        ids = lax.broadcasted_iota(jnp.int32, (ROWS, peers * slots), 0) + c * ROWS
        hot = (ids == send_ids[...]).astype(F32).astype(BF16)
        out[at] = grad_own[at] + jnp.dot(hot, rows[...], preferred_element_type=F32)
        return carry

    lax.fori_loop(0, node_rows // ROWS, scatter, 0)
    for h in range(hubs):
        out[pl.ds(hub_rows[h], 1)] += hub_total[h : h + 1]


def finish(hub_rows, send_ids, received, grad_own, grad_scale):
    peers, message, width = received.shape
    hubs = hub_rows.shape[0]
    slots = message - 2 * hubs

    def body(*refs):
        finish_kernel(*refs, grad_scale)

    return pl.pallas_call(
        body,
        out_shape=(
            jax.ShapeDtypeStruct(grad_own.shape, F32),
            jax.ShapeDtypeStruct((peers * hubs // 2, width), F32),
        ),
        in_specs=[smem()] + [vmem()] * 3,
        out_specs=(vmem(),) * 2,
        scratch_shapes=[pltpu.VMEM((peers * slots, width), BF16)],
        compiler_params=params(40),
        name="finish",
    )(hub_rows, send_ids, received, grad_own)


def rep_shift(value, shift, size):
    return lax.ppermute(value, "rep", [(j, (j + shift) % size) for j in range(size)])


def shards(
    features,
    out_grad,
    w_self,
    w_nbr,
    hub_rows,
    send_rows,
    send_counts,
    tile_targets,
    tile_sources,
    tile_count,
    tile_weights,
):
    node_rows, width = features.shape
    dom_size = lax.axis_size("dom")
    rep_size = lax.axis_size("rep")
    peers, slots = send_rows.shape
    hubs = hub_rows.shape[0]
    outgoing = pack(hub_rows, send_rows, send_counts, features)
    received = lax.all_to_all(outgoing, "dom", split_axis=0, concat_axis=0, tiled=True)
    own_rep = received[:, slots:]
    pieces = [rep_shift(own_rep, i, rep_size) for i in range(1, rep_size)]
    hidden, grad_agg, grad_self, grad_w = forward(
        tile_targets, tile_sources, tile_count, tile_weights, features, received, pieces,
        out_grad, w_self, w_nbr,
    )
    w_slices = lax.all_to_all(
        grad_w.reshape(dom_size, -1, width), "dom", split_axis=0, concat_axis=0, tiled=True
    )
    grad_own, halo, *hub_pieces = backward(
        tile_targets, tile_sources, tile_count, tile_weights, grad_agg, grad_self, peers, slots, hubs
    )
    w_slice = jnp.sum(w_slices, 0)
    high = w_slice.astype(BF16)
    low = (w_slice - high.astype(F32)).astype(BF16)
    w_pair = jnp.concatenate([high, low], 0)
    hub_pieces = [piece.at[dom_size].set(w_pair) for piece in hub_pieces]
    hub_pieces = hub_pieces[:1] + [
        rep_shift(hub_pieces[i], i, rep_size) for i in range(1, rep_size)
    ]
    back = lax.all_to_all(merge(halo, hub_pieces), "dom", split_axis=0, concat_axis=0, tiled=True)
    slot_live = jnp.arange(slots, dtype=jnp.int32)[None, :] < send_counts[:, None]
    send_ids = jnp.where(slot_live, send_rows, node_rows).reshape(1, -1)
    grad_scale = 1.0 / math.sqrt(node_rows * dom_size * rep_size)
    grad_features, grad_w = finish(hub_rows, send_ids, back, grad_own, grad_scale)
    both = jnp.concatenate([grad_w[: 2 * width], grad_w[2 * width :]], 1)
    return (hidden, grad_features, both[:width], both[width:])


def solution(mesh):
    return jax.shard_map(
        shards,
        mesh=mesh,
        in_specs=(
            P(("dom", "rep"), None),
            P(("dom", "rep"), None),
            P(),
            P(),
            P(("dom", "rep")),
            P(("dom", "rep"), None),
            P(("dom", "rep")),
            P(("dom", "rep")),
            P(("dom", "rep")),
            P(("dom", "rep")),
            P(("dom", "rep"), None, None),
        ),
        out_specs=(P(("dom", "rep"), None), P(("dom", "rep"), None), P(), P()),
        check_vma=False,
    )
```

```python
import math

import jax
import jax.numpy as jnp
from jax import lax
from jax.experimental import pallas as pl
from jax.experimental.pallas import tpu as pltpu
from jax.sharding import Mesh
from jax.sharding import PartitionSpec as P

BF16 = jnp.bfloat16
F32 = jnp.float32
CHUNK = 16
ROWS = 1024
NEAR = 16
WHOLE = 60
REPS = 4
CORES = 2
GROUP = "group"
DOM = ("group", "core")


def smem():
    return pl.BlockSpec(memory_space=pltpu.SMEM)


def vmem():
    return pl.BlockSpec(memory_space=pltpu.VMEM)


def hbm():
    return pl.BlockSpec(memory_space=pl.ANY)


def params(mebibytes):
    return pltpu.CompilerParams(vmem_limit_bytes=mebibytes * 1024 * 1024)


def rows_at(index, size):
    return pl.ds(pl.multiple_of(index * size, size), size)


def hub_pack_kernel(hub_rows, features, out, near, wide, sems):
    hubs = hub_rows.shape[0]
    copies = []
    for h in range(hubs):
        start = pl.multiple_of(hub_rows[h] // NEAR * NEAR, NEAR)
        copies.append(
            pltpu.make_async_copy(
                features.at[pl.ds(start, NEAR)], near.at[pl.ds(h * NEAR, NEAR)], sems.at[h]
            )
        )
        copies[-1].start()
    for copy in copies:
        copy.wait()
    wide[hubs:] = near[...].astype(F32)
    for h in range(hubs):
        row = hubs + h * NEAR + hub_rows[h] % NEAR
        wide[h : h + 1] = wide[pl.ds(row, 1)]
    own_hubs = wide[:hubs].astype(BF16)

    def emit(p, carry):
        out[p] = own_hubs
        return carry

    lax.fori_loop(0, out.shape[0], emit, 0)


def hub_pack(hub_rows, features, peers):
    hubs = hub_rows.shape[0]
    width = features.shape[1]
    return pl.pallas_call(
        hub_pack_kernel,
        out_shape=jax.ShapeDtypeStruct((peers, hubs, width), BF16),
        in_specs=[smem(), hbm()],
        out_specs=vmem(),
        scratch_shapes=[
            pltpu.VMEM((hubs * NEAR, width), BF16),
            pltpu.VMEM((hubs + hubs * NEAR, width), F32),
            pltpu.SemaphoreType.DMA((hubs,)),
        ],
        compiler_params=params(WHOLE),
        name="hub_pack",
    )(hub_rows, features)


def halo_pack_kernel(send_slots, send_counts, features, out, wide, staged):
    slots, peers = send_slots.shape
    wide[...] = features[...].astype(F32)

    def peer(p, carry):
        for k in range(slots):
            staged[pl.ds(p * slots + k, 1)] = wide[pl.ds(send_slots[k, p], 1)]
        return carry

    lax.fori_loop(0, peers, peer, 0)
    slot = lax.broadcasted_iota(jnp.int32, (slots, out.shape[2]), 0)

    def emit(p, carry):
        rows = staged[rows_at(p, slots)]
        out[p] = jnp.where(slot < send_counts[p], rows, 0.0).astype(BF16)
        return carry

    lax.fori_loop(0, peers, emit, 0)


def halo_pack(send_rows, send_counts, features):
    peers, slots = send_rows.shape
    node_rows, width = features.shape
    return pl.pallas_call(
        halo_pack_kernel,
        out_shape=jax.ShapeDtypeStruct((peers, slots, width), BF16),
        in_specs=[smem(), smem(), vmem()],
        out_specs=vmem(),
        scratch_shapes=[
            pltpu.VMEM((node_rows, width), F32),
            pltpu.VMEM((peers * slots, width), F32),
        ],
        compiler_params=params(WHOLE),
        name="halo_pack",
    )(send_rows.T, send_counts, features)


def weight_copy(c, weights, held, sems):
    part = rows_at(c, CHUNK)
    return pltpu.make_async_copy(weights.at[part], held.at[part], sems.at[c])


def start_weights(chunks, weights, held, sems):
    def start(c, carry):
        weight_copy(c, weights, held, sems).start()
        return carry

    lax.fori_loop(0, chunks, start, 0)


def forward_kernel(
    targets,
    sources,
    count,
    weights,
    features,
    halo,
    *refs,
):
    hubs, refs = refs[: REPS * CORES], refs[REPS * CORES :]
    out_grad, w_self, w_nbr, hidden, grad_agg, grad_self, grad_w, *refs = refs
    held, source_rows, totals, w_both, grads_in, grad_total, hidden_all, *refs = refs
    agg_all, self_all, w_all, weight_sems, sems, out_sems = refs
    block = weights.shape[1]
    target_blocks, parts, part_rows, width = features.shape
    hub_blocks = hubs[0].shape[0]
    halo_blocks = halo.shape[0]
    node_rows = target_blocks * block
    rep = lax.axis_index("rep")
    core = lax.axis_index("core")
    pieces = [(features, source_rows.at[pl.ds(0, target_blocks)])]
    for c in range(CORES):
        for i in range(REPS):
            from_core = lax.rem(core + c, CORES)
            from_rep = lax.rem(rep - i + REPS, REPS)
            part = from_core * REPS + from_rep
            pieces.append(
                (hubs[c * REPS + i], source_rows.at[pl.ds(target_blocks, hub_blocks), part])
            )
    pieces.append((halo, source_rows.at[pl.ds(target_blocks + hub_blocks, halo_blocks)]))
    early = [pltpu.make_async_copy(x, y, sems.at[n]) for n, (x, y) in enumerate(pieces)]
    for copy in early:
        copy.start()
    live = count[0]
    chunks = (live + CHUNK - 1) // CHUNK
    start_weights(chunks, weights, held, weight_sems)
    late = [
        pltpu.make_async_copy(x, y, sems.at[len(pieces) + n])
        for n, (x, y) in enumerate(
            (
                (w_self, w_both.at[pl.ds(0, width)]),
                (w_nbr, w_both.at[pl.ds(width, width)]),
                (out_grad, grads_in),
            )
        )
    ]
    for copy in late:
        copy.start()
    ones = jnp.ones((block, width), BF16)

    def product(t):
        picked = source_rows[sources[t]].reshape(block, width)
        return jnp.dot(
            held[t], jnp.concatenate([picked, ones], 1), preferred_element_type=F32
        )

    for copy in early:
        copy.wait()
    leading = target_blocks // CHUNK

    def first(c, carry):
        weight_copy(c, weights, held, weight_sems).wait()
        for u in range(CHUNK):
            totals[c * CHUNK + u] = product(c * CHUNK + u)
        return carry

    lax.fori_loop(0, leading, first, 0)

    def more(c, carry):
        weight_copy(c, weights, held, weight_sems).wait()
        products = [product(c * CHUNK + u) for u in range(CHUNK)]
        for u, value in enumerate(products):
            t = c * CHUNK + u
            target = jnp.where(t < live, targets[t], target_blocks)
            totals[target] += value
        return carry

    lax.fori_loop(leading, chunks, more, 0)
    grad_total[...] = jnp.zeros_like(grad_total)
    per_chunk = ROWS // block
    for copy in late:
        copy.wait()

    def outs(c):
        rows = rows_at(c, ROWS)
        return [
            pltpu.make_async_copy(x.at[rows], y.at[rows], out_sems.at[n])
            for n, (x, y) in enumerate(
                ((hidden_all, hidden), (agg_all, grad_agg), (self_all, grad_self))
            )
        ]

    def dense(c, carry):
        rows = rows_at(c, ROWS)
        blocks_at = pl.ds(c * per_chunk, per_chunk)
        total = totals[blocks_at].reshape(ROWS, 2 * width)
        inverse = 1.0 / jnp.maximum(total[:, width:], 1.0)
        aggregate = (total[:, :width] * inverse).astype(BF16)
        own = source_rows[blocks_at].reshape(ROWS, width)
        both = jnp.concatenate([own, aggregate], 1)
        preact = jnp.dot(both, w_both[...], preferred_element_type=F32)
        sigmoid = 0.5 * jnp.tanh(0.5 * preact) + 0.5
        activated = preact * sigmoid
        hidden_all[rows] = activated.astype(BF16)
        slope = sigmoid + activated * (1.0 - sigmoid)
        grad_preact = (grads_in[rows].astype(F32) * slope).astype(BF16)
        grad_total[...] += lax.dot_general(
            both, grad_preact, (((0,), (0,)), ((), ())), preferred_element_type=F32
        )
        back = lax.dot_general(
            grad_preact, w_both[...], (((1,), (1,)), ((), ())), preferred_element_type=F32
        )
        self_all[rows] = back[:, :width]
        agg_all[rows] = (back[:, width:] * inverse).astype(BF16)
        for copy in outs(c):
            copy.start()
        return carry

    steps = node_rows // ROWS
    lax.fori_loop(0, steps, dense, 0)
    half = grad_total.shape[1] // 2
    w_all[: grad_total.shape[0]] = grad_total[:, :half]
    w_all[grad_total.shape[0] :] = grad_total[:, half:]
    w_copy = pltpu.make_async_copy(w_all, grad_w, sems.at[0])
    w_copy.start()

    def drain(c, carry):
        for copy in outs(c):
            copy.wait()
        return carry

    lax.fori_loop(0, steps, drain, 0)
    w_copy.wait()


def forward(targets, sources, count, weights, features, halo, hubs, out_grad, w_self, w_nbr):
    node_rows, width = features.shape
    tiles, block, _ = weights.shape
    hidden_width = w_self.shape[1]
    parts = REPS * CORES
    part_rows = block // parts
    in_blocks = lambda value: value.reshape(-1, parts, part_rows, width)
    features = in_blocks(features)
    halo = in_blocks(halo)
    source_blocks = features.shape[0] + hubs[0].shape[0] + halo.shape[0]
    shapes = (
        jax.ShapeDtypeStruct((node_rows, hidden_width), BF16),
        jax.ShapeDtypeStruct((node_rows, width), BF16),
        jax.ShapeDtypeStruct((node_rows, width), F32),
        jax.ShapeDtypeStruct((4 * width, hidden_width // 2), F32),
    )
    return pl.pallas_call(
        forward_kernel,
        out_shape=shapes,
        in_specs=[smem()] * 3 + [hbm()] * (6 + parts),
        out_specs=(hbm(),) * 4,
        scratch_shapes=[
            pltpu.VMEM((tiles, block, block), BF16),
            pltpu.VMEM((source_blocks, parts, part_rows, width), BF16),
            pltpu.VMEM((node_rows // block + 1, block, 2 * width), F32),
            pltpu.VMEM((2 * width, hidden_width), BF16),
            pltpu.VMEM((node_rows, hidden_width), BF16),
            pltpu.VMEM((2 * width, hidden_width), F32),
        ]
        + [pltpu.VMEM(shape.shape, shape.dtype) for shape in shapes]
        + [
            pltpu.SemaphoreType.DMA((tiles // CHUNK,)),
            pltpu.SemaphoreType.DMA((5 + parts,)),
            pltpu.SemaphoreType.DMA((3,)),
        ],
        compiler_params=params(WHOLE),
        name="forward",
    )(targets, sources, count, weights, features, halo, *hubs, out_grad, w_self, w_nbr)


def backward_kernel(
    targets,
    sources,
    count,
    weights,
    grad_agg,
    grad_self,
    grad_own,
    halo,
    near,
    far,
    held,
    agg,
    totals,
    weight_sems,
    sems,
):
    block = weights.shape[1]
    node_rows, width = grad_agg.shape
    peers, slots, _ = halo.shape
    _, groups, hubs, _ = near.shape
    agg_copy = pltpu.make_async_copy(grad_agg, agg, sems.at[0])
    self_copy = pltpu.make_async_copy(grad_self, totals.at[pl.ds(0, node_rows)], sems.at[1])
    agg_copy.start()
    self_copy.start()
    live = count[0]
    chunks = (live + CHUNK - 1) // CHUNK
    start_weights(chunks, weights, held, weight_sems)
    rep = lax.axis_index("rep")
    core = lax.axis_index("core")
    totals[node_rows:] = jnp.zeros((totals.shape[0] - node_rows, width), F32)
    spare = totals.shape[0] // block - 1
    agg_copy.wait()
    self_copy.wait()

    def step(c, carry):
        weight_copy(c, weights, held, weight_sems).wait()
        products = [
            lax.dot_general(
                held[c * CHUNK + u],
                agg[rows_at(targets[c * CHUNK + u], block)],
                (((0,), (0,)), ((), ())),
                preferred_element_type=F32,
            )
            for u in range(CHUNK)
        ]
        for u, value in enumerate(products):
            t = c * CHUNK + u
            source = jnp.where(t < live, sources[t], spare)
            totals[rows_at(source, block)] += value
        return carry

    lax.fori_loop(0, chunks, step, 0)
    own_copy = pltpu.make_async_copy(totals.at[pl.ds(0, node_rows)], grad_own, sems.at[0])
    own_copy.start()
    hub_base = node_rows
    halo_base = hub_base + groups * CORES * REPS * hubs

    def emit_halo(p, carry):
        at = pl.multiple_of(halo_base + p * slots, slots)
        halo[p] = totals[pl.ds(at, slots)].astype(BF16)
        return carry

    lax.fori_loop(0, peers, emit_halo, 0)

    def emit_hub(p, carry):
        for c, piece in enumerate((near, far)):
            to_core = lax.rem(core + c, CORES)
            for i in range(REPS):
                to_rep = lax.rem(rep + i, REPS)
                part = (p * CORES + to_core) * REPS + to_rep
                at = pl.multiple_of(hub_base + part * hubs, hubs)
                piece[i, p] = totals[pl.ds(at, hubs)].astype(BF16)
        return carry

    lax.fori_loop(0, groups, emit_hub, 0)
    own_copy.wait()


def backward(targets, sources, count, weights, grad_agg, grad_self, peers, slots, hubs):
    node_rows, width = grad_agg.shape
    tiles, block, _ = weights.shape
    groups = peers // CORES
    total_rows = node_rows + peers * REPS * hubs + peers * slots + block
    piece = jax.ShapeDtypeStruct((REPS, groups, hubs, width), BF16)
    return pl.pallas_call(
        backward_kernel,
        out_shape=(
            jax.ShapeDtypeStruct((node_rows, width), F32),
            jax.ShapeDtypeStruct((peers, slots, width), BF16),
            piece,
            piece,
        ),
        in_specs=[smem()] * 3 + [hbm()] * 3,
        out_specs=(hbm(), vmem(), vmem(), vmem()),
        scratch_shapes=[
            pltpu.VMEM((tiles, block, block), BF16),
            pltpu.VMEM((node_rows, width), BF16),
            pltpu.VMEM((total_rows, width), F32),
            pltpu.SemaphoreType.DMA((tiles // CHUNK,)),
            pltpu.SemaphoreType.DMA((2,)),
        ],
        compiler_params=params(WHOLE),
        name="backward",
    )(targets, sources, count, weights, grad_agg, grad_self)


def split_pair(total):
    high = total.astype(BF16)
    return high, (total - high.astype(F32)).astype(BF16)


def fold_kernel(slices, out):
    def peer(p, total):
        return total + slices[p]

    total = lax.fori_loop(0, slices.shape[0], peer, jnp.zeros(slices.shape[1:], F32))
    out[0], out[1] = split_pair(total)


def fold(slices):
    return pl.pallas_call(
        fold_kernel,
        out_shape=jax.ShapeDtypeStruct((2, *slices.shape[1:]), BF16),
        in_specs=[vmem()],
        out_specs=vmem(),
        compiler_params=params(8),
        name="fold",
    )(slices)


def join_kernel(near, far, w_near, w_far, *outs):
    groups = near.shape[1]
    total = (w_near[0].astype(F32) + w_near[1].astype(F32)) + (
        w_far[0].astype(F32) + w_far[1].astype(F32)
    )
    high, low = split_pair(total)
    for out in outs:
        out[groups] = high
        out[groups + 1] = low

    def group(p, carry):
        for i, out in enumerate(outs):
            out[p] = (near[i, p].astype(F32) + far[i, p].astype(F32)).astype(BF16)
        return carry

    lax.fori_loop(0, groups, group, 0)


def join(near, far, w_near, w_far):
    reps, groups, hubs, width = near.shape
    piece = jax.ShapeDtypeStruct((groups + 2, hubs, width), BF16)
    return pl.pallas_call(
        join_kernel,
        out_shape=(piece,) * reps,
        in_specs=[vmem()] * 4,
        out_specs=(vmem(),) * reps,
        compiler_params=params(8),
        name="join",
    )(near, far, w_near, w_far)


def merge_kernel(hub0, hub1, hub2, hub3, out, w_parts):
    groups, message, width = out.shape
    hubs = hub0.shape[1]
    rep = lax.axis_index("rep")
    for i, piece in enumerate((hub0, hub1, hub2, hub3)):
        w_parts[lax.rem(rep - i + REPS, REPS)] = piece[groups].astype(F32) + piece[
            groups + 1
        ].astype(F32)
    w_total = (((w_parts[0] + w_parts[1]) + w_parts[2]) + w_parts[3]).astype(BF16)

    def group(p, carry):
        total = (hub0[p].astype(F32) + hub1[p].astype(F32)) + (
            hub2[p].astype(F32) + hub3[p].astype(F32)
        )
        out[p, :hubs] = total.astype(BF16)
        out[p, hubs:] = w_total
        return carry

    lax.fori_loop(0, groups, group, 0)


def merge(pieces):
    groups, hubs, width = pieces[0].shape
    return pl.pallas_call(
        merge_kernel,
        out_shape=jax.ShapeDtypeStruct((groups - 2, 2 * hubs, width), BF16),
        in_specs=[vmem()] * 4,
        out_specs=vmem(),
        scratch_shapes=[pltpu.VMEM((REPS, hubs, width), F32)],
        compiler_params=params(8),
        name="merge",
    )(*pieces)


def scatter_kernel(send_ids, received, grad_own, out):
    peers, slots, width = received.shape
    rows = received[...].reshape(peers * slots, width)

    def scatter(c, carry):
        at = rows_at(c, ROWS)
        ids = lax.broadcasted_iota(jnp.int32, (ROWS, peers * slots), 0) + c * ROWS
        hot = (ids == send_ids[...]).astype(F32).astype(BF16)
        out[at] = grad_own[at] + jnp.dot(hot, rows, preferred_element_type=F32)
        return carry

    lax.fori_loop(0, out.shape[0] // ROWS, scatter, 0)


def scatter(send_ids, received, grad_own):
    return pl.pallas_call(
        scatter_kernel,
        out_shape=jax.ShapeDtypeStruct(grad_own.shape, F32),
        in_specs=[vmem()] * 3,
        out_specs=vmem(),
        compiler_params=params(32),
        name="scatter",
    )(send_ids, received, grad_own)


def finish(hub_rows, received, grad_nodes, hidden_width, grad_scale):
    peers, message, width = received.shape
    hubs = hub_rows.shape[0]
    half = message - hubs

    def body(hub_rows, received, grad_nodes, out, grad_self, grad_nbr, held):
        out[...] = grad_nodes[...]

        def place(p, total):
            held[rows_at(p, half)] = received[p, hubs:].astype(F32) * grad_scale
            return total + received[p, :hubs].astype(F32)

        total = lax.fori_loop(0, peers, place, jnp.zeros((hubs, width), F32))
        for h in range(hubs):
            out[pl.ds(hub_rows[h], 1)] += total[h : h + 1]
        for k in range(hidden_width // width):
            columns = pl.ds(k * width, width)
            grad_self[:, columns] = held[2 * k * width : (2 * k + 1) * width]
            grad_nbr[:, columns] = held[(2 * k + 1) * width : (2 * k + 2) * width]

    return pl.pallas_call(
        body,
        out_shape=(
            jax.ShapeDtypeStruct(grad_nodes.shape, F32),
            jax.ShapeDtypeStruct((width, hidden_width), F32),
            jax.ShapeDtypeStruct((width, hidden_width), F32),
        ),
        in_specs=[smem()] + [vmem()] * 2,
        out_specs=(vmem(),) * 3,
        scratch_shapes=[pltpu.VMEM((peers * half, width), F32)],
        compiler_params=params(24),
        name="finish",
    )(hub_rows, received, grad_nodes)


def rep_shift(value, shift):
    return lax.ppermute(value, "rep", [(j, (j + shift) % REPS) for j in range(REPS)])


def core_swap(value):
    return lax.ppermute(value, "core", [(0, 1), (1, 0)])


def swap(value, axes):
    return lax.all_to_all(value, axes, split_axis=0, concat_axis=0, tiled=True)


def shards(
    features,
    out_grad,
    w_self,
    w_nbr,
    hub_rows,
    send_rows,
    send_counts,
    tile_targets,
    tile_sources,
    tile_count,
    tile_weights,
):
    node_rows, width = features.shape
    peers, slots = send_rows.shape
    hubs = hub_rows.shape[0]
    groups = peers // CORES
    own_rep = swap(hub_pack(hub_rows, features, groups), GROUP)
    halo = swap(halo_pack(send_rows, send_counts, features), DOM)
    near = [own_rep] + [rep_shift(own_rep, i) for i in range(1, REPS)]
    far = [core_swap(piece) for piece in near]
    hidden, grad_agg, grad_self, grad_w = forward(
        tile_targets, tile_sources, tile_count, tile_weights, features, halo, near + far,
        out_grad, w_self, w_nbr,
    )
    w_slices = swap(grad_w.reshape(groups, -1, width), GROUP)
    grad_own, grad_halo, near, far = backward(
        tile_targets, tile_sources, tile_count, tile_weights, grad_agg, grad_self, peers, slots, hubs
    )
    returned = swap(grad_halo, DOM)
    w_pair = fold(w_slices)
    pieces = join(near, core_swap(far), w_pair, core_swap(w_pair))
    pieces = [pieces[0]] + [rep_shift(pieces[i], i) for i in range(1, REPS)]
    merged = swap(merge(pieces), GROUP)
    slot_live = jnp.arange(slots, dtype=jnp.int32)[None, :] < send_counts[:, None]
    send_ids = jnp.where(slot_live, send_rows, node_rows).reshape(1, -1)
    grad_nodes = scatter(send_ids, returned, grad_own)
    grad_scale = 1.0 / math.sqrt(node_rows * peers * REPS)
    grad_features, grad_w_self, grad_w_nbr = finish(
        hub_rows, merged, grad_nodes, w_self.shape[1], grad_scale
    )
    return (hidden, grad_features, grad_w_self, grad_w_nbr)


def solution(mesh):
    fine = Mesh(mesh.devices.reshape(-1, CORES, REPS), ("group", "core", "rep"))
    every = ("group", "core", "rep")
    return jax.shard_map(
        shards,
        mesh=fine,
        in_specs=(
            P(every, None),
            P(every, None),
            P(),
            P(),
            P(every),
            P(every, None),
            P(every),
            P(every),
            P(every),
            P(every),
            P(every, None, None),
        ),
        out_specs=(P(every, None), P(every, None), P(), P()),
        check_vma=False,
    )
```

```python
import math

import jax
import jax.numpy as jnp
from jax import lax
from jax.experimental import pallas as pl
from jax.experimental.pallas import tpu as pltpu
from jax.sharding import Mesh
from jax.sharding import PartitionSpec as P

BF16 = jnp.bfloat16
F32 = jnp.float32
CHUNK = 16
ROWS = 1024
NEAR = 16
PARTS = 4
WHOLE = 60
REPS = 4
CORES = 2
GROUP = "group"
DOM = ("group", "core")


def smem():
    return pl.BlockSpec(memory_space=pltpu.SMEM)


def vmem():
    return pl.BlockSpec(memory_space=pltpu.VMEM)


def hbm():
    return pl.BlockSpec(memory_space=pl.ANY)


def params(mebibytes):
    return pltpu.CompilerParams(vmem_limit_bytes=mebibytes * 1024 * 1024)


def rows_at(index, size):
    return pl.ds(pl.multiple_of(index * size, size), size)


def hub_pack_kernel(hub_rows, features, out, near, wide, sems):
    hubs = hub_rows.shape[0]
    copies = []
    for h in range(hubs):
        start = pl.multiple_of(hub_rows[h] // NEAR * NEAR, NEAR)
        copies.append(
            pltpu.make_async_copy(
                features.at[pl.ds(start, NEAR)], near.at[pl.ds(h * NEAR, NEAR)], sems.at[h]
            )
        )
        copies[-1].start()
    for copy in copies:
        copy.wait()
    wide[hubs:] = near[...].astype(F32)
    for h in range(hubs):
        row = hubs + h * NEAR + hub_rows[h] % NEAR
        wide[h : h + 1] = wide[pl.ds(row, 1)]
    own_hubs = wide[:hubs].astype(BF16)

    def emit(p, carry):
        out[p] = own_hubs
        return carry

    lax.fori_loop(0, out.shape[0], emit, 0)


def hub_pack(hub_rows, features, peers):
    hubs = hub_rows.shape[0]
    width = features.shape[1]
    return pl.pallas_call(
        hub_pack_kernel,
        out_shape=jax.ShapeDtypeStruct((peers, hubs, width), BF16),
        in_specs=[smem(), hbm()],
        out_specs=vmem(),
        scratch_shapes=[
            pltpu.VMEM((hubs * NEAR, width), BF16),
            pltpu.VMEM((hubs + hubs * NEAR, width), F32),
            pltpu.SemaphoreType.DMA((hubs,)),
        ],
        compiler_params=params(WHOLE),
        name="hub_pack",
    )(hub_rows, features)


def halo_pack_kernel(send_slots, send_counts, features, out, wide, staged):
    slots, peers = send_slots.shape
    wide[...] = features[...].astype(F32)

    def peer(p, carry):
        for k in range(slots):
            staged[pl.ds(p * slots + k, 1)] = wide[pl.ds(send_slots[k, p], 1)]
        return carry

    lax.fori_loop(0, peers, peer, 0)
    slot = lax.broadcasted_iota(jnp.int32, (slots, out.shape[2]), 0)

    def emit(p, carry):
        rows = staged[rows_at(p, slots)]
        out[p] = jnp.where(slot < send_counts[p], rows, 0.0).astype(BF16)
        return carry

    lax.fori_loop(0, peers, emit, 0)


def halo_pack(send_rows, send_counts, features):
    peers, slots = send_rows.shape
    node_rows, width = features.shape
    return pl.pallas_call(
        halo_pack_kernel,
        out_shape=jax.ShapeDtypeStruct((peers, slots, width), BF16),
        in_specs=[smem(), smem(), vmem()],
        out_specs=vmem(),
        scratch_shapes=[
            pltpu.VMEM((node_rows, width), F32),
            pltpu.VMEM((peers * slots, width), F32),
        ],
        compiler_params=params(WHOLE),
        name="halo_pack",
    )(send_rows.T, send_counts, features)


def weight_copy(c, weights, held, sems):
    part = rows_at(c, CHUNK)
    return pltpu.make_async_copy(weights.at[part], held.at[part], sems.at[c])


def start_weights(first, chunks, weights, held, sems):
    def start(c, carry):
        weight_copy(c, weights, held, sems).start()
        return carry

    lax.fori_loop(first, chunks, start, 0)


def forward_kernel(
    targets,
    sources,
    count,
    weights,
    features,
    halo,
    *refs,
):
    hubs, refs = refs[: REPS * CORES], refs[REPS * CORES :]
    out_grad, w_self, w_nbr, hidden, grad_agg, grad_self, grad_w, *refs = refs
    held, source_rows, totals, w_both, grads_in, grad_total, hidden_all, *refs = refs
    agg_all, self_all, w_all, weight_sems, sems, out_sems = refs
    block = weights.shape[1]
    target_blocks, parts, part_rows, width = features.shape
    hub_blocks = hubs[0].shape[0]
    halo_blocks = halo.shape[0]
    node_rows = target_blocks * block
    rep = lax.axis_index("rep")
    core = lax.axis_index("core")
    pieces = [(features, source_rows.at[pl.ds(0, target_blocks)])]
    for c in range(CORES):
        for i in range(REPS):
            from_core = lax.rem(core + c, CORES)
            from_rep = lax.rem(rep - i + REPS, REPS)
            part = from_core * REPS + from_rep
            pieces.append(
                (hubs[c * REPS + i], source_rows.at[pl.ds(target_blocks, hub_blocks), part])
            )
    pieces.append((halo, source_rows.at[pl.ds(target_blocks + hub_blocks, halo_blocks)]))
    early = [pltpu.make_async_copy(x, y, sems.at[n]) for n, (x, y) in enumerate(pieces)]
    for copy in early:
        copy.start()
    live = count[0]
    chunks = (live + CHUNK - 1) // CHUNK
    start_weights(0, chunks, weights, held, weight_sems)
    late = [
        pltpu.make_async_copy(x, y, sems.at[len(pieces) + n])
        for n, (x, y) in enumerate(
            (
                (w_self, w_both.at[pl.ds(0, width)]),
                (w_nbr, w_both.at[pl.ds(width, width)]),
                (out_grad, grads_in),
            )
        )
    ]
    for copy in late:
        copy.start()
    ones = jnp.ones((block, width), BF16)

    def product(t):
        picked = source_rows[sources[t]].reshape(block, width)
        return jnp.dot(
            held[t], jnp.concatenate([picked, ones], 1), preferred_element_type=F32
        )

    for copy in early:
        copy.wait()
    leading = target_blocks // CHUNK

    def first(c, carry):
        weight_copy(c, weights, held, weight_sems).wait()
        for u in range(CHUNK):
            totals[c * CHUNK + u] = product(c * CHUNK + u)
        return carry

    lax.fori_loop(0, leading, first, 0)

    def more(c, carry):
        weight_copy(c, weights, held, weight_sems).wait()
        products = [product(c * CHUNK + u) for u in range(CHUNK)]
        for u, value in enumerate(products):
            t = c * CHUNK + u
            target = jnp.where(t < live, targets[t], target_blocks)
            totals[target] += value
        return carry

    lax.fori_loop(leading, chunks, more, 0)
    grad_total[...] = jnp.zeros_like(grad_total)
    per_chunk = ROWS // block
    for copy in late:
        copy.wait()

    def outs(c):
        rows = rows_at(c, ROWS)
        return [
            pltpu.make_async_copy(x.at[rows], y.at[rows], out_sems.at[n])
            for n, (x, y) in enumerate(
                ((hidden_all, hidden), (agg_all, grad_agg), (self_all, grad_self))
            )
        ]

    def dense(c, carry):
        rows = rows_at(c, ROWS)
        blocks_at = pl.ds(c * per_chunk, per_chunk)
        total = totals[blocks_at].reshape(ROWS, 2 * width)
        inverse = 1.0 / jnp.maximum(total[:, width:], 1.0)
        aggregate = (total[:, :width] * inverse).astype(BF16)
        own = source_rows[blocks_at].reshape(ROWS, width)
        both = jnp.concatenate([own, aggregate], 1)
        preact = jnp.dot(both, w_both[...], preferred_element_type=F32)
        sigmoid = 0.5 * jnp.tanh(0.5 * preact) + 0.5
        activated = preact * sigmoid
        hidden_all[rows] = activated.astype(BF16)
        slope = sigmoid + activated * (1.0 - sigmoid)
        grad_preact = (grads_in[rows].astype(F32) * slope).astype(BF16)
        grad_total[...] += lax.dot_general(
            both, grad_preact, (((0,), (0,)), ((), ())), preferred_element_type=F32
        )
        back = lax.dot_general(
            grad_preact, w_both[...], (((1,), (1,)), ((), ())), preferred_element_type=F32
        )
        self_all[rows] = back[:, :width]
        agg_all[rows] = (back[:, width:] * inverse).astype(BF16)
        for copy in outs(c):
            copy.start()
        return carry

    steps = node_rows // ROWS
    lax.fori_loop(0, steps, dense, 0)
    half = grad_total.shape[1] // 2
    w_all[: grad_total.shape[0]] = grad_total[:, :half].astype(BF16)
    w_all[grad_total.shape[0] :] = grad_total[:, half:].astype(BF16)
    w_copy = pltpu.make_async_copy(w_all, grad_w, sems.at[0])
    w_copy.start()

    def drain(c, carry):
        for copy in outs(c):
            copy.wait()
        return carry

    lax.fori_loop(0, steps, drain, 0)
    w_copy.wait()


def forward(targets, sources, count, weights, features, halo, hubs, out_grad, w_self, w_nbr):
    node_rows, width = features.shape
    tiles, block, _ = weights.shape
    hidden_width = w_self.shape[1]
    parts = REPS * CORES
    part_rows = block // parts
    in_blocks = lambda value: value.reshape(-1, parts, part_rows, width)
    features = in_blocks(features)
    halo = in_blocks(halo)
    source_blocks = features.shape[0] + hubs[0].shape[0] + halo.shape[0]
    shapes = (
        jax.ShapeDtypeStruct((node_rows, hidden_width), BF16),
        jax.ShapeDtypeStruct((node_rows, width), BF16),
        jax.ShapeDtypeStruct((node_rows, width), F32),
        jax.ShapeDtypeStruct((4 * width, hidden_width // 2), BF16),
    )
    return pl.pallas_call(
        forward_kernel,
        out_shape=shapes,
        in_specs=[smem()] * 3 + [hbm()] * (6 + parts),
        out_specs=(hbm(),) * 4,
        scratch_shapes=[
            pltpu.VMEM((tiles, block, block), BF16),
            pltpu.VMEM((source_blocks, parts, part_rows, width), BF16),
            pltpu.VMEM((node_rows // block + 1, block, 2 * width), F32),
            pltpu.VMEM((2 * width, hidden_width), BF16),
            pltpu.VMEM((node_rows, hidden_width), BF16),
            pltpu.VMEM((2 * width, hidden_width), F32),
        ]
        + [pltpu.VMEM(shape.shape, shape.dtype) for shape in shapes]
        + [
            pltpu.SemaphoreType.DMA((tiles // CHUNK,)),
            pltpu.SemaphoreType.DMA((5 + parts,)),
            pltpu.SemaphoreType.DMA((3,)),
        ],
        compiler_params=params(WHOLE),
        name="forward",
    )(targets, sources, count, weights, features, halo, *hubs, out_grad, w_self, w_nbr)


def collect(live, wanted, order):
    def look(t, found):
        order[found] = t
        return found + wanted(t).astype(jnp.int32)

    found = lax.fori_loop(0, live, look, 0)
    for u in range(CHUNK):
        order[found + u] = 0
    return found


def add_tiles(found, order, chunks, targets, held, agg, totals, place, spare, arrived):
    block = held.shape[1]

    def step(c, waited):
        at = [order[c * CHUNK + u] for u in range(CHUNK)]
        last = order[jnp.minimum(c * CHUNK + CHUNK, found) - 1]
        needed = last // CHUNK + 1

        def wait(n, carry):
            arrived(n)
            return carry

        lax.fori_loop(waited, needed, wait, 0)
        products = [
            lax.dot_general(
                held[t],
                agg[rows_at(targets[t], block)],
                (((0,), (0,)), ((), ())),
                preferred_element_type=F32,
            )
            for t in at
        ]
        for u, value in enumerate(products):
            block_at = jnp.where(c * CHUNK + u < found, place(at[u]), spare)
            totals[rows_at(block_at, block)] += value
        return needed

    waited = lax.fori_loop(0, (found + CHUNK - 1) // CHUNK, step, 0)

    def rest(n, carry):
        arrived(n)
        return carry

    lax.fori_loop(waited, chunks, rest, 0)


def backward_far_kernel(
    targets,
    sources,
    count,
    weights,
    grad_agg,
    halo,
    near,
    far,
    order,
    held,
    agg,
    totals,
    halo_all,
    near_all,
    far_all,
    weight_sems,
    sems,
):
    block = weights.shape[1]
    node_rows, width = grad_agg.shape
    own_blocks = node_rows // block
    peers, slots, _ = halo.shape
    _, groups, hubs, _ = near.shape
    agg_copy = pltpu.make_async_copy(grad_agg, agg, sems.at[0])
    agg_copy.start()
    live = count[0]
    chunks = (live + CHUNK - 1) // CHUNK
    start_weights(0, chunks, weights, held, weight_sems)
    rep = lax.axis_index("rep")
    core = lax.axis_index("core")
    totals[...] = jnp.zeros_like(totals)
    found = collect(live, lambda t: sources[t] >= own_blocks, order)
    agg_copy.wait()
    add_tiles(
        found,
        order,
        chunks,
        targets,
        held,
        agg,
        totals,
        lambda t: sources[t] - own_blocks,
        totals.shape[0] // block - 1,
        lambda n: weight_copy(n, weights, held, weight_sems).wait(),
    )
    outs = [
        pltpu.make_async_copy(x, y, sems.at[n])
        for n, (x, y) in enumerate(((far_all, far), (halo_all, halo), (near_all, near)))
    ]
    halo_base = groups * CORES * REPS * hubs

    def emit_hub(piece, to_core):
        def emit(p, carry):
            for i in range(REPS):
                to_rep = lax.rem(rep + i, REPS)
                part = (p * CORES + to_core) * REPS + to_rep
                piece[i, p] = totals[rows_at(part, hubs)].astype(BF16)
            return carry

        lax.fori_loop(0, groups, emit, 0, unroll=4)

    def emit_halo(p, carry):
        at = pl.multiple_of(halo_base + p * slots, slots)
        halo_all[p] = totals[pl.ds(at, slots)].astype(BF16)
        return carry

    emit_hub(far_all, 1 - core)
    outs[0].start()
    lax.fori_loop(0, peers, emit_halo, 0, unroll=8)
    outs[1].start()
    emit_hub(near_all, core)
    outs[2].start()
    for copy in outs:
        copy.wait()


def backward_far(targets, sources, count, weights, grad_agg, peers, slots, hubs):
    node_rows, width = grad_agg.shape
    tiles, block, _ = weights.shape
    groups = peers // CORES
    total_rows = peers * REPS * hubs + peers * slots + block
    halo = jax.ShapeDtypeStruct((peers, slots, width), BF16)
    piece = jax.ShapeDtypeStruct((REPS, groups, hubs, width), BF16)
    return pl.pallas_call(
        backward_far_kernel,
        out_shape=(halo, piece, piece),
        in_specs=[smem()] * 3 + [hbm()] * 2,
        out_specs=(hbm(),) * 3,
        scratch_shapes=[
            pltpu.SMEM((tiles + CHUNK,), jnp.int32),
            pltpu.VMEM((tiles, block, block), BF16),
            pltpu.VMEM((node_rows, width), BF16),
            pltpu.VMEM((total_rows, width), F32),
            pltpu.VMEM(halo.shape, BF16),
            pltpu.VMEM(piece.shape, BF16),
            pltpu.VMEM(piece.shape, BF16),
            pltpu.SemaphoreType.DMA((tiles // CHUNK,)),
            pltpu.SemaphoreType.DMA((3,)),
        ],
        compiler_params=params(WHOLE),
        name="backward_far",
    )(targets, sources, count, weights, grad_agg)


def backward_own_kernel(
    targets,
    sources,
    count,
    weights,
    grad_agg,
    grad_self,
    after,
    grad_own,
    order,
    held,
    agg,
    totals,
    weight_sems,
    sems,
):
    block = weights.shape[1]
    node_rows, width = grad_agg.shape
    own_blocks = node_rows // block
    copies = [
        pltpu.make_async_copy(grad_agg, agg, sems.at[0]),
        pltpu.make_async_copy(grad_self, totals.at[pl.ds(0, node_rows)], sems.at[1]),
    ]
    for copy in copies:
        copy.start()
    live = count[0]
    chunks = (live + CHUNK - 1) // CHUNK
    start_weights(0, chunks, weights, held, weight_sems)
    totals[node_rows:] = jnp.zeros((block, width), F32)
    found = collect(live, lambda t: sources[t] < own_blocks, order)
    for copy in copies:
        copy.wait()
    add_tiles(
        found,
        order,
        chunks,
        targets,
        held,
        agg,
        totals,
        lambda t: sources[t],
        own_blocks,
        lambda n: weight_copy(n, weights, held, weight_sems).wait(),
    )
    out = pltpu.make_async_copy(totals.at[pl.ds(0, node_rows)], grad_own, sems.at[0])
    out.start()
    out.wait()


def backward_own(targets, sources, count, weights, grad_agg, grad_self, after):
    node_rows, width = grad_agg.shape
    tiles, block, _ = weights.shape
    return pl.pallas_call(
        backward_own_kernel,
        out_shape=jax.ShapeDtypeStruct((node_rows, width), F32),
        in_specs=[smem()] * 3 + [hbm()] * 4,
        out_specs=hbm(),
        scratch_shapes=[
            pltpu.SMEM((tiles + CHUNK,), jnp.int32),
            pltpu.VMEM((tiles, block, block), BF16),
            pltpu.VMEM((node_rows, width), BF16),
            pltpu.VMEM((node_rows + block, width), F32),
            pltpu.SemaphoreType.DMA((tiles // CHUNK,)),
            pltpu.SemaphoreType.DMA((2,)),
        ],
        compiler_params=params(40),
        name="backward_own",
    )(targets, sources, count, weights, grad_agg, grad_self, after)


def split_pair(total):
    high = total.astype(BF16)
    return high, (total - high.astype(F32)).astype(BF16)


def fold_kernel(slices, out):
    def peer(p, total):
        return total + slices[p].astype(F32)

    total = lax.fori_loop(0, slices.shape[0], peer, jnp.zeros(slices.shape[1:], F32))
    out[0], out[1] = split_pair(total)


def fold(slices):
    return pl.pallas_call(
        fold_kernel,
        out_shape=jax.ShapeDtypeStruct((2, *slices.shape[1:]), BF16),
        in_specs=[vmem()],
        out_specs=vmem(),
        compiler_params=params(8),
        name="fold",
    )(slices)


def join_kernel(near, far, w_near, w_far, *outs):
    groups = near.shape[1]
    total = (w_near[0].astype(F32) + w_near[1].astype(F32)) + (
        w_far[0].astype(F32) + w_far[1].astype(F32)
    )
    high, low = split_pair(total)
    for out in outs:
        out[groups] = high
        out[groups + 1] = low

    def group(p, carry):
        for i, out in enumerate(outs):
            out[p] = (near[i, p].astype(F32) + far[i, p].astype(F32)).astype(BF16)
        return carry

    lax.fori_loop(0, groups, group, 0)


def join(near, far, w_near, w_far):
    reps, groups, hubs, width = near.shape
    piece = jax.ShapeDtypeStruct((groups + 2, hubs, width), BF16)
    return pl.pallas_call(
        join_kernel,
        out_shape=(piece,) * reps,
        in_specs=[vmem()] * 4,
        out_specs=(vmem(),) * reps,
        compiler_params=params(8),
        name="join",
    )(near, far, w_near, w_far)


def merge_kernel(hub0, hub1, hub2, hub3, out, w_parts):
    groups, message, width = out.shape
    hubs = hub0.shape[1]
    rep = lax.axis_index("rep")
    for i, piece in enumerate((hub0, hub1, hub2, hub3)):
        w_parts[lax.rem(rep - i + REPS, REPS)] = piece[groups].astype(F32) + piece[
            groups + 1
        ].astype(F32)
    w_total = (((w_parts[0] + w_parts[1]) + w_parts[2]) + w_parts[3]).astype(BF16)

    def group(p, carry):
        total = (hub0[p].astype(F32) + hub1[p].astype(F32)) + (
            hub2[p].astype(F32) + hub3[p].astype(F32)
        )
        out[p, :hubs] = total.astype(BF16)
        out[p, hubs:] = w_total
        return carry

    lax.fori_loop(0, groups, group, 0)


def merge(pieces):
    groups, hubs, width = pieces[0].shape
    return pl.pallas_call(
        merge_kernel,
        out_shape=jax.ShapeDtypeStruct((groups - 2, 2 * hubs, width), BF16),
        in_specs=[vmem()] * 4,
        out_specs=vmem(),
        scratch_shapes=[pltpu.VMEM((REPS, hubs, width), F32)],
        compiler_params=params(8),
        name="merge",
    )(*pieces)


def scatter_kernel(send_ids, received, grad_own, out):
    peers, slots, width = received.shape
    rows = received[...].reshape(peers * slots, width)

    def scatter(c, carry):
        at = rows_at(c, ROWS)
        ids = lax.broadcasted_iota(jnp.int32, (ROWS, peers * slots), 0) + c * ROWS
        hot = (ids == send_ids[...]).astype(F32).astype(BF16)
        out[at] = grad_own[at] + jnp.dot(hot, rows, preferred_element_type=F32)
        return carry

    lax.fori_loop(0, out.shape[0] // ROWS, scatter, 0)


def scatter(send_ids, received, grad_own):
    return pl.pallas_call(
        scatter_kernel,
        out_shape=jax.ShapeDtypeStruct(grad_own.shape, F32),
        in_specs=[vmem()] * 3,
        out_specs=vmem(),
        compiler_params=params(32),
        name="scatter",
    )(send_ids, received, grad_own)


def finish(hub_rows, received, grad_nodes, hidden_width, grad_scale):
    peers, message, width = received.shape
    hubs = hub_rows.shape[0]
    half = message - hubs

    def body(hub_rows, received, grad_nodes, out, grad_self, grad_nbr, held):
        out[...] = grad_nodes[...]

        def place(p, total):
            held[rows_at(p, half)] = received[p, hubs:].astype(F32) * grad_scale
            return total + received[p, :hubs].astype(F32)

        total = lax.fori_loop(0, peers, place, jnp.zeros((hubs, width), F32))
        for h in range(hubs):
            out[pl.ds(hub_rows[h], 1)] += total[h : h + 1]
        for k in range(hidden_width // width):
            columns = pl.ds(k * width, width)
            grad_self[:, columns] = held[2 * k * width : (2 * k + 1) * width]
            grad_nbr[:, columns] = held[(2 * k + 1) * width : (2 * k + 2) * width]

    return pl.pallas_call(
        body,
        out_shape=(
            jax.ShapeDtypeStruct(grad_nodes.shape, F32),
            jax.ShapeDtypeStruct((width, hidden_width), F32),
            jax.ShapeDtypeStruct((width, hidden_width), F32),
        ),
        in_specs=[smem()] + [vmem()] * 2,
        out_specs=(vmem(),) * 3,
        scratch_shapes=[pltpu.VMEM((peers * half, width), F32)],
        compiler_params=params(24),
        name="finish",
    )(hub_rows, received, grad_nodes)


def rep_shift(value, shift):
    return lax.ppermute(value, "rep", [(j, (j + shift) % REPS) for j in range(REPS)])


def core_swap(value):
    return lax.ppermute(value, "core", [(0, 1), (1, 0)])


def swap(value, axes):
    return lax.all_to_all(value, axes, split_axis=0, concat_axis=0, tiled=True)


def shards(
    features,
    out_grad,
    w_self,
    w_nbr,
    hub_rows,
    send_rows,
    send_counts,
    tile_targets,
    tile_sources,
    tile_count,
    tile_weights,
):
    node_rows, width = features.shape
    peers, slots = send_rows.shape
    hubs = hub_rows.shape[0]
    groups = peers // CORES
    own_rep = swap(hub_pack(hub_rows, features, groups), GROUP)
    halo = swap(halo_pack(send_rows, send_counts, features), DOM)
    near = [own_rep] + [rep_shift(own_rep, i) for i in range(1, REPS)]
    far = [core_swap(piece) for piece in near]
    hidden, grad_agg, grad_self, grad_w = forward(
        tile_targets, tile_sources, tile_count, tile_weights, features, halo, near + far,
        out_grad, w_self, w_nbr,
    )
    w_slices = swap(grad_w.reshape(groups, -1, width), GROUP)
    grad_halo, near, far = backward_far(
        tile_targets, tile_sources, tile_count, tile_weights, grad_agg, peers, slots, hubs
    )
    returned = swap(grad_halo, DOM)
    w_pair = fold(w_slices)
    pieces = join(near, core_swap(far), w_pair, core_swap(w_pair))
    grad_own = backward_own(
        tile_targets, tile_sources, tile_count, tile_weights, grad_agg, grad_self, pieces[0]
    )
    pieces = [pieces[0]] + [rep_shift(pieces[i], i) for i in range(1, REPS)]
    merged = swap(merge(pieces), GROUP)
    slot_live = jnp.arange(slots, dtype=jnp.int32)[None, :] < send_counts[:, None]
    send_ids = jnp.where(slot_live, send_rows, node_rows).reshape(1, -1)
    grad_nodes = scatter(send_ids, returned, grad_own)
    grad_scale = 1.0 / math.sqrt(node_rows * peers * REPS)
    grad_features, grad_w_self, grad_w_nbr = finish(
        hub_rows, merged, grad_nodes, w_self.shape[1], grad_scale
    )
    return (hidden, grad_features, grad_w_self, grad_w_nbr)


def solution(mesh):
    fine = Mesh(mesh.devices.reshape(-1, CORES, REPS), ("group", "core", "rep"))
    every = ("group", "core", "rep")
    return jax.shard_map(
        shards,
        mesh=fine,
        in_specs=(
            P(every, None),
            P(every, None),
            P(),
            P(),
            P(every),
            P(every, None),
            P(every),
            P(every),
            P(every),
            P(every),
            P(every, None, None),
        ),
        out_specs=(P(every, None), P(every, None), P(), P()),
        check_vma=False,
    )
```

```python
import math

import jax
import jax.numpy as jnp
from jax import lax
from jax.experimental import pallas as pl
from jax.experimental.pallas import tpu as pltpu
from jax.sharding import Mesh
from jax.sharding import PartitionSpec as P

BF16 = jnp.bfloat16
F32 = jnp.float32
CHUNK = 16
ROWS = 1024
NEAR = 16
TILE = 8
PARTS = 4
WHOLE = 60
FORWARD = 60
SCATTER = 60
FINISH = 16
TOKEN = jax.ShapeDtypeStruct((8, 128), F32)
REPS = 4
CORES = 2
GROUP = "group"
DOM = ("group", "core")


def smem():
    return pl.BlockSpec(memory_space=pltpu.SMEM)


def vmem():
    return pl.BlockSpec(memory_space=pltpu.VMEM)


def hbm():
    return pl.BlockSpec(memory_space=pl.ANY)


def params(mebibytes):
    return pltpu.CompilerParams(vmem_limit_bytes=mebibytes * 1024 * 1024)


def rows_at(index, size):
    return pl.ds(pl.multiple_of(index * size, size), size)


def hub_pack_kernel(hub_rows, features, out, near, wide, sems):
    hubs = hub_rows.shape[0]
    copies = []
    for h in range(hubs):
        start = pl.multiple_of(hub_rows[h] // NEAR * NEAR, NEAR)
        copies.append(
            pltpu.make_async_copy(
                features.at[pl.ds(start, NEAR)], near.at[pl.ds(h * NEAR, NEAR)], sems.at[h]
            )
        )
        copies[-1].start()
    for copy in copies:
        copy.wait()
    wide[hubs:] = near[...].astype(F32)
    for h in range(hubs):
        row = hubs + h * NEAR + hub_rows[h] % NEAR
        wide[h : h + 1] = wide[pl.ds(row, 1)]
    own_hubs = wide[:hubs].astype(BF16)

    def emit(p, carry):
        out[p] = own_hubs
        return carry

    lax.fori_loop(0, out.shape[0], emit, 0)


def hub_pack(hub_rows, features, peers):
    hubs = hub_rows.shape[0]
    width = features.shape[1]
    return pl.pallas_call(
        hub_pack_kernel,
        out_shape=jax.ShapeDtypeStruct((peers, hubs, width), BF16),
        in_specs=[smem(), hbm()],
        out_specs=vmem(),
        scratch_shapes=[
            pltpu.VMEM((hubs * NEAR, width), BF16),
            pltpu.VMEM((hubs + hubs * NEAR, width), F32),
            pltpu.SemaphoreType.DMA((hubs,)),
        ],
        compiler_params=params(WHOLE),
        name="hub_pack",
    )(hub_rows, features)


def halo_pack_kernel(send_slots, send_counts, features, out, wide, staged):
    slots, peers = send_slots.shape
    wide[...] = features[...].astype(F32)

    def peer(p, carry):
        for k in range(slots):
            staged[pl.ds(p * slots + k, 1)] = wide[pl.ds(send_slots[k, p], 1)]
        return carry

    lax.fori_loop(0, peers, peer, 0)
    slot = lax.broadcasted_iota(jnp.int32, (slots, out.shape[2]), 0)

    def emit(p, carry):
        rows = staged[rows_at(p, slots)]
        out[p] = jnp.where(slot < send_counts[p], rows, 0.0).astype(BF16)
        return carry

    lax.fori_loop(0, peers, emit, 0)


def halo_pack(send_rows, send_counts, features):
    peers, slots = send_rows.shape
    node_rows, width = features.shape
    return pl.pallas_call(
        halo_pack_kernel,
        out_shape=jax.ShapeDtypeStruct((peers, slots, width), BF16),
        in_specs=[smem(), smem(), vmem()],
        out_specs=vmem(),
        scratch_shapes=[
            pltpu.VMEM((node_rows, width), F32),
            pltpu.VMEM((peers * slots, width), F32),
        ],
        compiler_params=params(WHOLE),
        name="halo_pack",
    )(send_rows.T, send_counts, features)


def weight_copy(c, weights, held, sems):
    part = rows_at(c, CHUNK)
    return pltpu.make_async_copy(weights.at[part], held.at[part], sems.at[c])


def start_weights(first, chunks, weights, held, sems):
    def start(c, carry):
        weight_copy(c, weights, held, sems).start()
        return carry

    lax.fori_loop(first, chunks, start, 0)


def forward_kernel(
    targets,
    sources,
    count,
    weights,
    features,
    halo,
    *refs,
):
    hubs, refs = refs[: REPS * CORES], refs[REPS * CORES :]
    out_grad, w_self, w_nbr, hidden, grad_agg, grad_self, grad_w, *refs = refs
    held, source_rows, totals, w_both, grads_in, grad_total, hidden_all, *refs = refs
    agg_all, self_all, w_all, weight_sems, sems, out_sems = refs
    block = weights.shape[1]
    target_blocks, parts, part_rows, width = features.shape
    hub_blocks = hubs[0].shape[0]
    halo_blocks = halo.shape[0]
    node_rows = target_blocks * block
    rep = lax.axis_index("rep")
    core = lax.axis_index("core")
    pieces = [(features, source_rows.at[pl.ds(0, target_blocks)])]
    for c in range(CORES):
        for i in range(REPS):
            from_core = lax.rem(core + c, CORES)
            from_rep = lax.rem(rep - i + REPS, REPS)
            part = from_core * REPS + from_rep
            pieces.append(
                (hubs[c * REPS + i], source_rows.at[pl.ds(target_blocks, hub_blocks), part])
            )
    pieces.append((halo, source_rows.at[pl.ds(target_blocks + hub_blocks, halo_blocks)]))
    early = [pltpu.make_async_copy(x, y, sems.at[n]) for n, (x, y) in enumerate(pieces)]
    for copy in early:
        copy.start()
    live = count[0]
    chunks = (live + CHUNK - 1) // CHUNK
    start_weights(0, chunks, weights, held, weight_sems)
    late = [
        pltpu.make_async_copy(x, y, sems.at[len(pieces) + n])
        for n, (x, y) in enumerate(
            (
                (w_self, w_both.at[pl.ds(0, width)]),
                (w_nbr, w_both.at[pl.ds(width, width)]),
                (out_grad, grads_in),
            )
        )
    ]
    for copy in late:
        copy.start()
    ones = jnp.ones((block, width), BF16)

    def product(t):
        picked = source_rows[sources[t]].reshape(block, width)
        return jnp.dot(
            held[t], jnp.concatenate([picked, ones], 1), preferred_element_type=F32
        )

    for copy in early:
        copy.wait()
    leading = target_blocks // CHUNK

    def first(c, carry):
        weight_copy(c, weights, held, weight_sems).wait()
        for u in range(CHUNK):
            totals[c * CHUNK + u] = product(c * CHUNK + u)
        return carry

    lax.fori_loop(0, leading, first, 0)

    def more(c, carry):
        weight_copy(c, weights, held, weight_sems).wait()
        products = [product(c * CHUNK + u) for u in range(CHUNK)]
        for u, value in enumerate(products):
            t = c * CHUNK + u
            target = jnp.where(t < live, targets[t], target_blocks)
            totals[target] += value
        return carry

    lax.fori_loop(leading, chunks, more, 0)
    grad_total[...] = jnp.zeros_like(grad_total)
    per_chunk = ROWS // block
    for copy in late:
        copy.wait()

    def outs(c):
        rows = rows_at(c, ROWS)
        return [
            pltpu.make_async_copy(x.at[rows], y.at[rows], out_sems.at[n])
            for n, (x, y) in enumerate(
                ((hidden_all, hidden), (agg_all, grad_agg), (self_all, grad_self))
            )
        ]

    def dense(c, carry):
        rows = rows_at(c, ROWS)
        blocks_at = pl.ds(c * per_chunk, per_chunk)
        total = totals[blocks_at].reshape(ROWS, 2 * width)
        inverse = 1.0 / jnp.maximum(total[:, width:], 1.0)
        aggregate = (total[:, :width] * inverse).astype(BF16)
        own = source_rows[blocks_at].reshape(ROWS, width)
        both = jnp.concatenate([own, aggregate], 1)
        preact = jnp.dot(both, w_both[...], preferred_element_type=F32)
        sigmoid = 0.5 * jnp.tanh(0.5 * preact) + 0.5
        activated = preact * sigmoid
        hidden_all[rows] = activated.astype(BF16)
        slope = sigmoid + activated * (1.0 - sigmoid)
        grad_preact = (grads_in[rows].astype(F32) * slope).astype(BF16)
        grad_total[...] += lax.dot_general(
            both, grad_preact, (((0,), (0,)), ((), ())), preferred_element_type=F32
        )
        back = lax.dot_general(
            grad_preact, w_both[...], (((1,), (1,)), ((), ())), preferred_element_type=F32
        )
        self_all[rows] = back[:, :width]
        agg_all[rows] = (back[:, width:] * inverse).astype(BF16)
        for copy in outs(c):
            copy.start()
        return carry

    steps = node_rows // ROWS
    lax.fori_loop(0, steps, dense, 0)
    half = grad_total.shape[1] // 2
    w_all[: grad_total.shape[0]] = grad_total[:, :half].astype(BF16)
    w_all[grad_total.shape[0] :] = grad_total[:, half:].astype(BF16)
    w_copy = pltpu.make_async_copy(w_all, grad_w, sems.at[0])
    w_copy.start()

    def drain(c, carry):
        for copy in outs(c):
            copy.wait()
        return carry

    lax.fori_loop(0, steps, drain, 0)
    w_copy.wait()


def forward(targets, sources, count, weights, features, halo, hubs, out_grad, w_self, w_nbr):
    node_rows, width = features.shape
    tiles, block, _ = weights.shape
    hidden_width = w_self.shape[1]
    parts = REPS * CORES
    part_rows = block // parts
    in_blocks = lambda value: value.reshape(-1, parts, part_rows, width)
    features = in_blocks(features)
    halo = in_blocks(halo)
    source_blocks = features.shape[0] + hubs[0].shape[0] + halo.shape[0]
    shapes = (
        jax.ShapeDtypeStruct((node_rows, hidden_width), BF16),
        jax.ShapeDtypeStruct((node_rows, width), BF16),
        jax.ShapeDtypeStruct((node_rows, width), F32),
        jax.ShapeDtypeStruct((4 * width, hidden_width // 2), BF16),
    )
    return pl.pallas_call(
        forward_kernel,
        out_shape=shapes,
        in_specs=[smem()] * 3 + [hbm()] * (6 + parts),
        out_specs=(hbm(),) * 4,
        scratch_shapes=[
            pltpu.VMEM((tiles, block, block), BF16),
            pltpu.VMEM((source_blocks, parts, part_rows, width), BF16),
            pltpu.VMEM((node_rows // block + 1, block, 2 * width), F32),
            pltpu.VMEM((2 * width, hidden_width), BF16),
            pltpu.VMEM((node_rows, hidden_width), BF16),
            pltpu.VMEM((2 * width, hidden_width), F32),
        ]
        + [pltpu.VMEM(shape.shape, shape.dtype) for shape in shapes]
        + [
            pltpu.SemaphoreType.DMA((tiles // CHUNK,)),
            pltpu.SemaphoreType.DMA((5 + parts,)),
            pltpu.SemaphoreType.DMA((3,)),
        ],
        compiler_params=params(FORWARD),
        name="forward",
    )(targets, sources, count, weights, features, halo, *hubs, out_grad, w_self, w_nbr)


def collect(live, wanted, order):
    def look(t, found):
        order[found] = t
        return found + wanted(t).astype(jnp.int32)

    found = lax.fori_loop(0, live, look, 0)
    for u in range(CHUNK):
        order[found + u] = 0
    return found


def add_tiles(found, order, chunks, targets, held, agg, totals, place, spare, arrived):
    block = held.shape[1]

    def step(c, waited):
        at = [order[c * CHUNK + u] for u in range(CHUNK)]
        last = order[jnp.minimum(c * CHUNK + CHUNK, found) - 1]
        needed = last // CHUNK + 1

        def wait(n, carry):
            arrived(n)
            return carry

        lax.fori_loop(waited, needed, wait, 0)
        products = [
            lax.dot_general(
                held[t],
                agg[rows_at(targets[t], block)],
                (((0,), (0,)), ((), ())),
                preferred_element_type=F32,
            )
            for t in at
        ]
        for u, value in enumerate(products):
            block_at = jnp.where(c * CHUNK + u < found, place(at[u]), spare)
            totals[rows_at(block_at, block)] += value
        return needed

    waited = lax.fori_loop(0, (found + CHUNK - 1) // CHUNK, step, 0)

    def rest(n, carry):
        arrived(n)
        return carry

    lax.fori_loop(waited, chunks, rest, 0)


def backward_far_kernel(
    targets,
    sources,
    count,
    weights,
    grad_agg,
    halo,
    near,
    far,
    order,
    held,
    agg,
    totals,
    halo_all,
    near_all,
    far_all,
    weight_sems,
    sems,
):
    block = weights.shape[1]
    node_rows, width = grad_agg.shape
    own_blocks = node_rows // block
    peers, slots, _ = halo.shape
    _, groups, hubs, _ = near.shape
    agg_copy = pltpu.make_async_copy(grad_agg, agg, sems.at[0])
    agg_copy.start()
    live = count[0]
    chunks = (live + CHUNK - 1) // CHUNK
    start_weights(0, chunks, weights, held, weight_sems)
    rep = lax.axis_index("rep")
    core = lax.axis_index("core")
    totals[...] = jnp.zeros_like(totals)
    found = collect(live, lambda t: sources[t] >= own_blocks, order)
    agg_copy.wait()
    add_tiles(
        found,
        order,
        chunks,
        targets,
        held,
        agg,
        totals,
        lambda t: sources[t] - own_blocks,
        totals.shape[0] // block - 1,
        lambda n: weight_copy(n, weights, held, weight_sems).wait(),
    )
    outs = [
        pltpu.make_async_copy(x, y, sems.at[n])
        for n, (x, y) in enumerate(((far_all, far), (halo_all, halo), (near_all, near)))
    ]
    halo_base = groups * CORES * REPS * hubs

    def emit_hub(piece, to_core):
        def emit(p, carry):
            for i in range(REPS):
                to_rep = lax.rem(rep + i, REPS)
                part = (p * CORES + to_core) * REPS + to_rep
                piece[i, p] = totals[rows_at(part, hubs)].astype(BF16)
            return carry

        lax.fori_loop(0, groups, emit, 0, unroll=4)

    def emit_halo(p, carry):
        at = pl.multiple_of(halo_base + p * slots, slots)
        halo_all[p] = totals[pl.ds(at, slots)].astype(BF16)
        return carry

    emit_hub(far_all, 1 - core)
    outs[0].start()
    lax.fori_loop(0, peers, emit_halo, 0, unroll=8)
    outs[1].start()
    emit_hub(near_all, core)
    outs[2].start()
    for copy in outs:
        copy.wait()


def backward_far(targets, sources, count, weights, grad_agg, peers, slots, hubs):
    node_rows, width = grad_agg.shape
    tiles, block, _ = weights.shape
    groups = peers // CORES
    total_rows = peers * REPS * hubs + peers * slots + block
    halo = jax.ShapeDtypeStruct((peers, slots, width), BF16)
    piece = jax.ShapeDtypeStruct((REPS, groups, hubs, width), BF16)
    return pl.pallas_call(
        backward_far_kernel,
        out_shape=(halo, piece, piece),
        in_specs=[smem()] * 3 + [hbm()] * 2,
        out_specs=(hbm(),) * 3,
        scratch_shapes=[
            pltpu.SMEM((tiles + CHUNK,), jnp.int32),
            pltpu.VMEM((tiles, block, block), BF16),
            pltpu.VMEM((node_rows, width), BF16),
            pltpu.VMEM((total_rows, width), F32),
            pltpu.VMEM(halo.shape, BF16),
            pltpu.VMEM(piece.shape, BF16),
            pltpu.VMEM(piece.shape, BF16),
            pltpu.SemaphoreType.DMA((tiles // CHUNK,)),
            pltpu.SemaphoreType.DMA((3,)),
        ],
        compiler_params=params(WHOLE),
        name="backward_far",
    )(targets, sources, count, weights, grad_agg)


def backward_own_kernel(
    targets,
    sources,
    count,
    weights,
    grad_agg,
    grad_self,
    after,
    grad_own,
    token,
    order,
    held,
    agg,
    totals,
    weight_sems,
    sems,
):
    block = weights.shape[1]
    node_rows, width = grad_agg.shape
    own_blocks = node_rows // block
    copies = [
        pltpu.make_async_copy(grad_agg, agg, sems.at[0]),
        pltpu.make_async_copy(grad_self, totals.at[pl.ds(0, node_rows)], sems.at[1]),
    ]
    for copy in copies:
        copy.start()
    live = count[0]
    chunks = (live + CHUNK - 1) // CHUNK
    start_weights(0, chunks, weights, held, weight_sems)
    totals[node_rows:] = jnp.zeros((block, width), F32)
    found = collect(live, lambda t: sources[t] < own_blocks, order)
    for copy in copies:
        copy.wait()
    add_tiles(
        found,
        order,
        chunks,
        targets,
        held,
        agg,
        totals,
        lambda t: sources[t],
        own_blocks,
        lambda n: weight_copy(n, weights, held, weight_sems).wait(),
    )
    out = pltpu.make_async_copy(totals.at[pl.ds(0, node_rows)], grad_own, sems.at[0])
    out.start()
    token[...] = jnp.zeros_like(token)
    out.wait()


def backward_own(targets, sources, count, weights, grad_agg, grad_self, after):
    node_rows, width = grad_agg.shape
    tiles, block, _ = weights.shape
    return pl.pallas_call(
        backward_own_kernel,
        out_shape=(jax.ShapeDtypeStruct((node_rows, width), F32), TOKEN),
        in_specs=[smem()] * 3 + [hbm()] * 4,
        out_specs=(hbm(), vmem()),
        scratch_shapes=[
            pltpu.SMEM((tiles + CHUNK,), jnp.int32),
            pltpu.VMEM((tiles, block, block), BF16),
            pltpu.VMEM((node_rows, width), BF16),
            pltpu.VMEM((node_rows + block, width), F32),
            pltpu.SemaphoreType.DMA((tiles // CHUNK,)),
            pltpu.SemaphoreType.DMA((2,)),
        ],
        compiler_params=params(WHOLE),
        name="backward_own",
    )(targets, sources, count, weights, grad_agg, grad_self, after)


def split_pair(total):
    high = total.astype(BF16)
    return high, (total - high.astype(F32)).astype(BF16)


def fold_kernel(slices, out):
    def peer(p, total):
        return total + slices[p].astype(F32)

    total = lax.fori_loop(0, slices.shape[0], peer, jnp.zeros(slices.shape[1:], F32))
    out[0], out[1] = split_pair(total)


def fold(slices):
    return pl.pallas_call(
        fold_kernel,
        out_shape=jax.ShapeDtypeStruct((2, *slices.shape[1:]), BF16),
        in_specs=[vmem()],
        out_specs=vmem(),
        compiler_params=params(8),
        name="fold",
    )(slices)


def join_kernel(near, far, w_near, w_far, *outs):
    *outs, token = outs
    token[...] = jnp.zeros_like(token)
    groups = near.shape[1]
    total = (w_near[0].astype(F32) + w_near[1].astype(F32)) + (
        w_far[0].astype(F32) + w_far[1].astype(F32)
    )
    high, low = split_pair(total)
    for out in outs:
        out[groups] = high
        out[groups + 1] = low

    def group(p, carry):
        for i, out in enumerate(outs):
            out[p] = (near[i, p].astype(F32) + far[i, p].astype(F32)).astype(BF16)
        return carry

    lax.fori_loop(0, groups, group, 0)


def join(near, far, w_near, w_far):
    reps, groups, hubs, width = near.shape
    piece = jax.ShapeDtypeStruct((groups + 2, hubs, width), BF16)
    return pl.pallas_call(
        join_kernel,
        out_shape=(piece,) * reps + (TOKEN,),
        in_specs=[vmem()] * 4,
        out_specs=(vmem(),) * (reps + 1),
        compiler_params=params(8),
        name="join",
    )(near, far, w_near, w_far)


def merge_kernel(hub0, hub1, hub2, hub3, after, out, w_parts):
    groups, message, width = out.shape
    hubs = hub0.shape[1]
    rep = lax.axis_index("rep")
    for i, piece in enumerate((hub0, hub1, hub2, hub3)):
        w_parts[lax.rem(rep - i + REPS, REPS)] = piece[groups].astype(F32) + piece[
            groups + 1
        ].astype(F32)
    w_total = (((w_parts[0] + w_parts[1]) + w_parts[2]) + w_parts[3]).astype(BF16)

    def group(p, carry):
        total = (hub0[p].astype(F32) + hub1[p].astype(F32)) + (
            hub2[p].astype(F32) + hub3[p].astype(F32)
        )
        out[p, :hubs] = total.astype(BF16)
        out[p, hubs:] = w_total
        return carry

    lax.fori_loop(0, groups, group, 0)


def merge(pieces, after):
    groups, hubs, width = pieces[0].shape
    return pl.pallas_call(
        merge_kernel,
        out_shape=jax.ShapeDtypeStruct((groups - 2, 2 * hubs, width), BF16),
        in_specs=[vmem()] * 4 + [hbm()],
        out_specs=vmem(),
        scratch_shapes=[pltpu.VMEM((REPS, hubs, width), F32)],
        compiler_params=params(8),
        name="merge",
    )(*pieces, after)


def scatter_kernel(send_ids, received, grad_own, out):
    peers, slots, width = received.shape
    rows = received[...].reshape(peers * slots, width)

    def scatter(c, carry):
        at = rows_at(c, ROWS)
        ids = lax.broadcasted_iota(jnp.int32, (ROWS, peers * slots), 0) + c * ROWS
        hot = (ids == send_ids[...]).astype(F32).astype(BF16)
        out[at] = grad_own[at] + jnp.dot(hot, rows, preferred_element_type=F32)
        return carry

    lax.fori_loop(0, out.shape[0] // ROWS, scatter, 0)


def scatter(send_ids, received, grad_own):
    return pl.pallas_call(
        scatter_kernel,
        out_shape=jax.ShapeDtypeStruct(grad_own.shape, F32),
        in_specs=[vmem()] * 3,
        out_specs=vmem(),
        compiler_params=params(SCATTER),
        name="scatter",
    )(send_ids, received, grad_own)


def finish(hub_rows, received, grad_nodes, hidden_width, grad_scale):
    groups, message, width = received.shape
    hubs = hub_rows.shape[0]
    w_rows = message - hubs

    def body(hub_rows, received, grad_nodes, out, grad_self, grad_nbr, near, held, sems):
        at = [hub_rows[h] // TILE for h in range(hubs)]
        for h in range(hubs):
            pltpu.make_async_copy(
                grad_nodes.at[rows_at(at[h], TILE)], near.at[pl.ds(h * TILE, TILE)], sems.at[h]
            ).start()

        def place(p, total):
            held[rows_at(p, w_rows)] = received[p, hubs:].astype(F32) * grad_scale
            return total + received[p, :hubs].astype(F32)

        total = lax.fori_loop(0, groups, place, jnp.zeros((hubs, width), F32), unroll=4)
        for k in range(hidden_width // width):
            columns = pl.ds(k * width, width)
            grad_self[:, columns] = held[2 * k * width : (2 * k + 1) * width]
            grad_nbr[:, columns] = held[(2 * k + 1) * width : (2 * k + 2) * width]
        for h in range(hubs):
            pltpu.make_async_copy(
                grad_nodes.at[rows_at(at[h], TILE)], near.at[pl.ds(h * TILE, TILE)], sems.at[h]
            ).wait()
        first = []
        for h in range(hubs):
            slot = jnp.int32(h)
            for j in reversed(range(h)):
                slot = jnp.where(at[j] == at[h], j, slot)
            first.append(slot)
            row = slot * TILE + hub_rows[h] % TILE
            near[pl.ds(row, 1)] += total[h : h + 1]

        def back(h):
            return pltpu.make_async_copy(
                near.at[pl.ds(h * TILE, TILE)], out.at[rows_at(at[h], TILE)], sems.at[h]
            )

        for h in range(hubs):
            pl.when(first[h] == h)(back(h).start)
        for h in range(hubs):
            pl.when(first[h] == h)(back(h).wait)

    return pl.pallas_call(
        body,
        out_shape=(
            jax.ShapeDtypeStruct(grad_nodes.shape, F32),
            jax.ShapeDtypeStruct((width, hidden_width), F32),
            jax.ShapeDtypeStruct((width, hidden_width), F32),
        ),
        in_specs=[smem(), vmem(), hbm()],
        out_specs=(hbm(), vmem(), vmem()),
        input_output_aliases={2: 0},
        scratch_shapes=[
            pltpu.VMEM((hubs * TILE, width), F32),
            pltpu.VMEM((groups * w_rows, width), F32),
            pltpu.SemaphoreType.DMA((hubs,)),
        ],
        compiler_params=params(FINISH),
        name="finish",
    )(hub_rows, received, grad_nodes)


def rep_shift(value, shift):
    return lax.ppermute(value, "rep", [(j, (j + shift) % REPS) for j in range(REPS)])


def core_swap(value):
    return lax.ppermute(value, "core", [(0, 1), (1, 0)])


def swap(value, axes):
    return lax.all_to_all(value, axes, split_axis=0, concat_axis=0, tiled=True)


def shards(
    features,
    out_grad,
    w_self,
    w_nbr,
    hub_rows,
    send_rows,
    send_counts,
    tile_targets,
    tile_sources,
    tile_count,
    tile_weights,
):
    node_rows, width = features.shape
    peers, slots = send_rows.shape
    hubs = hub_rows.shape[0]
    groups = peers // CORES
    own_rep = swap(hub_pack(hub_rows, features, groups), GROUP)
    halo = swap(halo_pack(send_rows, send_counts, features), DOM)
    near = [own_rep] + [rep_shift(own_rep, i) for i in range(1, REPS)]
    far = [core_swap(piece) for piece in near]
    hidden, grad_agg, grad_self, grad_w = forward(
        tile_targets, tile_sources, tile_count, tile_weights, features, halo, near + far,
        out_grad, w_self, w_nbr,
    )
    w_slices = swap(grad_w.reshape(groups, -1, width), GROUP)
    grad_halo, near, far = backward_far(
        tile_targets, tile_sources, tile_count, tile_weights, grad_agg, peers, slots, hubs
    )
    returned = swap(grad_halo, DOM)
    w_pair = fold(w_slices)
    *pieces, joined = join(near, core_swap(far), w_pair, core_swap(w_pair))
    grad_own, own_done = backward_own(
        tile_targets, tile_sources, tile_count, tile_weights, grad_agg, grad_self, joined
    )
    pieces = [pieces[0]] + [rep_shift(pieces[i], i) for i in range(1, REPS)]
    merged = swap(merge(pieces, own_done), GROUP)
    slot_live = jnp.arange(slots, dtype=jnp.int32)[None, :] < send_counts[:, None]
    send_ids = jnp.where(slot_live, send_rows, node_rows).reshape(1, -1)
    grad_nodes = scatter(send_ids, returned, grad_own)
    grad_scale = 1.0 / math.sqrt(node_rows * peers * REPS)
    grad_features, grad_w_self, grad_w_nbr = finish(
        hub_rows, merged, grad_nodes, w_self.shape[1], grad_scale
    )
    return (hidden, grad_features, grad_w_self, grad_w_nbr)


def solution(mesh):
    fine = Mesh(mesh.devices.reshape(-1, CORES, REPS), ("group", "core", "rep"))
    every = ("group", "core", "rep")
    return jax.shard_map(
        shards,
        mesh=fine,
        in_specs=(
            P(every, None),
            P(every, None),
            P(),
            P(),
            P(every),
            P(every, None),
            P(every),
            P(every),
            P(every),
            P(every),
            P(every, None, None),
        ),
        out_specs=(P(every, None), P(every, None), P(), P()),
        check_vma=False,
    )
```

```python
import math

import jax
import jax.numpy as jnp
from jax import lax
from jax.experimental import pallas as pl
from jax.experimental.pallas import tpu as pltpu
from jax.sharding import Mesh
from jax.sharding import PartitionSpec as P

BF16 = jnp.bfloat16
F32 = jnp.float32
CHUNK = 16
ROWS = 1024
NEAR = 16
TILE = 8
PARTS = 4
WHOLE = 60
FINISH = 16
FOLDS = 4
FOLD_ROWS = 512
REPS = 4
CORES = 2
GROUP = "group"
DOM = ("group", "core")


def smem():
    return pl.BlockSpec(memory_space=pltpu.SMEM)


def vmem():
    return pl.BlockSpec(memory_space=pltpu.VMEM)


def hbm():
    return pl.BlockSpec(memory_space=pl.ANY)


def params(mebibytes):
    return pltpu.CompilerParams(vmem_limit_bytes=mebibytes * 1024 * 1024)


def rows_at(index, size):
    return pl.ds(pl.multiple_of(index * size, size), size)


def hub_pack_kernel(hub_rows, features, out, near, wide, sems):
    hubs = hub_rows.shape[0]
    copies = []
    for h in range(hubs):
        start = pl.multiple_of(hub_rows[h] // NEAR * NEAR, NEAR)
        copies.append(
            pltpu.make_async_copy(
                features.at[pl.ds(start, NEAR)], near.at[pl.ds(h * NEAR, NEAR)], sems.at[h]
            )
        )
        copies[-1].start()
    for copy in copies:
        copy.wait()
    wide[hubs:] = near[...].astype(F32)
    for h in range(hubs):
        row = hubs + h * NEAR + hub_rows[h] % NEAR
        wide[h : h + 1] = wide[pl.ds(row, 1)]
    own_hubs = wide[:hubs].astype(BF16)

    def emit(p, carry):
        out[p] = own_hubs
        return carry

    lax.fori_loop(0, out.shape[0], emit, 0)


def hub_pack(hub_rows, features, peers):
    hubs = hub_rows.shape[0]
    width = features.shape[1]
    return pl.pallas_call(
        hub_pack_kernel,
        out_shape=jax.ShapeDtypeStruct((peers, hubs, width), BF16),
        in_specs=[smem(), hbm()],
        out_specs=vmem(),
        scratch_shapes=[
            pltpu.VMEM((hubs * NEAR, width), BF16),
            pltpu.VMEM((hubs + hubs * NEAR, width), F32),
            pltpu.SemaphoreType.DMA((hubs,)),
        ],
        compiler_params=params(WHOLE),
        name="hub_pack",
    )(hub_rows, features)


def halo_pack_kernel(send_slots, send_counts, features, out, wide, staged):
    slots, peers = send_slots.shape
    wide[...] = features[...].astype(F32)

    def peer(p, carry):
        for k in range(slots):
            staged[pl.ds(p * slots + k, 1)] = wide[pl.ds(send_slots[k, p], 1)]
        return carry

    lax.fori_loop(0, peers, peer, 0)
    slot = lax.broadcasted_iota(jnp.int32, (slots, out.shape[2]), 0)

    def emit(p, carry):
        rows = staged[rows_at(p, slots)]
        out[p] = jnp.where(slot < send_counts[p], rows, 0.0).astype(BF16)
        return carry

    lax.fori_loop(0, peers, emit, 0)


def halo_pack(send_rows, send_counts, features):
    peers, slots = send_rows.shape
    node_rows, width = features.shape
    return pl.pallas_call(
        halo_pack_kernel,
        out_shape=jax.ShapeDtypeStruct((peers, slots, width), BF16),
        in_specs=[smem(), smem(), vmem()],
        out_specs=vmem(),
        scratch_shapes=[
            pltpu.VMEM((node_rows, width), F32),
            pltpu.VMEM((peers * slots, width), F32),
        ],
        compiler_params=params(WHOLE),
        name="halo_pack",
    )(send_rows.T, send_counts, features)


def weight_copy(c, weights, held, sems):
    part = rows_at(c, CHUNK)
    return pltpu.make_async_copy(weights.at[part], held.at[part], sems.at[c])


def start_weights(first, chunks, weights, held, sems):
    def start(c, carry):
        weight_copy(c, weights, held, sems).start()
        return carry

    lax.fori_loop(first, chunks, start, 0)


def forward_kernel(
    targets,
    sources,
    count,
    weights,
    features,
    halo,
    *refs,
):
    hubs, refs = refs[: REPS * CORES], refs[REPS * CORES :]
    out_grad, w_self, w_nbr, hidden, grad_agg, grad_self, grad_w, *refs = refs
    held, source_rows, totals, w_both, grads_in, grad_total, hidden_all, *refs = refs
    agg_all, self_all, w_all, weight_sems, sems, out_sems = refs
    block = weights.shape[1]
    target_blocks, parts, part_rows, width = features.shape
    hub_blocks = hubs[0].shape[0]
    halo_blocks = halo.shape[0]
    node_rows = target_blocks * block
    rep = lax.axis_index("rep")
    core = lax.axis_index("core")
    pieces = [(features, source_rows.at[pl.ds(0, target_blocks)])]
    for c in range(CORES):
        for i in range(REPS):
            from_core = lax.rem(core + c, CORES)
            from_rep = lax.rem(rep - i + REPS, REPS)
            part = from_core * REPS + from_rep
            pieces.append(
                (hubs[c * REPS + i], source_rows.at[pl.ds(target_blocks, hub_blocks), part])
            )
    pieces.append((halo, source_rows.at[pl.ds(target_blocks + hub_blocks, halo_blocks)]))
    early = [pltpu.make_async_copy(x, y, sems.at[n]) for n, (x, y) in enumerate(pieces)]
    for copy in early:
        copy.start()
    live = count[0]
    chunks = (live + CHUNK - 1) // CHUNK
    start_weights(0, chunks, weights, held, weight_sems)
    late = [
        pltpu.make_async_copy(x, y, sems.at[len(pieces) + n])
        for n, (x, y) in enumerate(
            (
                (w_self, w_both.at[pl.ds(0, width)]),
                (w_nbr, w_both.at[pl.ds(width, width)]),
                (out_grad, grads_in),
            )
        )
    ]
    for copy in late:
        copy.start()
    ones = jnp.ones((block, width), BF16)

    def product(t):
        picked = source_rows[sources[t]].reshape(block, width)
        return jnp.dot(
            held[t], jnp.concatenate([picked, ones], 1), preferred_element_type=F32
        )

    for copy in early:
        copy.wait()
    leading = target_blocks // CHUNK

    def first(c, carry):
        weight_copy(c, weights, held, weight_sems).wait()
        for u in range(CHUNK):
            totals[c * CHUNK + u] = product(c * CHUNK + u)
        return carry

    lax.fori_loop(0, leading, first, 0)

    def more(c, carry):
        weight_copy(c, weights, held, weight_sems).wait()
        products = [product(c * CHUNK + u) for u in range(CHUNK)]
        for u, value in enumerate(products):
            t = c * CHUNK + u
            target = jnp.where(t < live, targets[t], target_blocks)
            totals[target] += value
        return carry

    lax.fori_loop(leading, chunks, more, 0)
    grad_total[...] = jnp.zeros_like(grad_total)
    per_chunk = ROWS // block
    for copy in late:
        copy.wait()

    def outs(c):
        rows = rows_at(c, ROWS)
        return [
            pltpu.make_async_copy(x.at[rows], y.at[rows], out_sems.at[n])
            for n, (x, y) in enumerate(
                ((hidden_all, hidden), (agg_all, grad_agg), (self_all, grad_self))
            )
        ]

    def dense(c, carry):
        rows = rows_at(c, ROWS)
        blocks_at = pl.ds(c * per_chunk, per_chunk)
        total = totals[blocks_at].reshape(ROWS, 2 * width)
        inverse = 1.0 / jnp.maximum(total[:, width:], 1.0)
        aggregate = (total[:, :width] * inverse).astype(BF16)
        own = source_rows[blocks_at].reshape(ROWS, width)
        both = jnp.concatenate([own, aggregate], 1)
        preact = jnp.dot(both, w_both[...], preferred_element_type=F32)
        sigmoid = 0.5 * jnp.tanh(0.5 * preact) + 0.5
        activated = preact * sigmoid
        hidden_all[rows] = activated.astype(BF16)
        slope = sigmoid + activated * (1.0 - sigmoid)
        grad_preact = (grads_in[rows].astype(F32) * slope).astype(BF16)
        grad_total[...] += lax.dot_general(
            both, grad_preact, (((0,), (0,)), ((), ())), preferred_element_type=F32
        )
        back = lax.dot_general(
            grad_preact, w_both[...], (((1,), (1,)), ((), ())), preferred_element_type=F32
        )
        self_all[rows] = back[:, :width]
        agg_all[rows] = (back[:, width:] * inverse).astype(BF16)
        for copy in outs(c):
            copy.start()
        return carry

    steps = node_rows // ROWS
    lax.fori_loop(0, steps, dense, 0)
    half = grad_total.shape[1] // 2
    w_all[: grad_total.shape[0]] = grad_total[:, :half].astype(BF16)
    w_all[grad_total.shape[0] :] = grad_total[:, half:].astype(BF16)
    w_copy = pltpu.make_async_copy(w_all, grad_w, sems.at[0])
    w_copy.start()

    def drain(c, carry):
        for copy in outs(c):
            copy.wait()
        return carry

    lax.fori_loop(0, steps, drain, 0)
    w_copy.wait()


def forward(targets, sources, count, weights, features, halo, hubs, out_grad, w_self, w_nbr):
    node_rows, width = features.shape
    tiles, block, _ = weights.shape
    hidden_width = w_self.shape[1]
    parts = REPS * CORES
    part_rows = block // parts
    in_blocks = lambda value: value.reshape(-1, parts, part_rows, width)
    features = in_blocks(features)
    halo = in_blocks(halo)
    source_blocks = features.shape[0] + hubs[0].shape[0] + halo.shape[0]
    shapes = (
        jax.ShapeDtypeStruct((node_rows, hidden_width), BF16),
        jax.ShapeDtypeStruct((node_rows, width), BF16),
        jax.ShapeDtypeStruct((node_rows, width), F32),
        jax.ShapeDtypeStruct((4 * width, hidden_width // 2), BF16),
    )
    return pl.pallas_call(
        forward_kernel,
        out_shape=shapes,
        in_specs=[smem()] * 3 + [hbm()] * (6 + parts),
        out_specs=(hbm(),) * 4,
        scratch_shapes=[
            pltpu.VMEM((tiles, block, block), BF16),
            pltpu.VMEM((source_blocks, parts, part_rows, width), BF16),
            pltpu.VMEM((node_rows // block + 1, block, 2 * width), F32),
            pltpu.VMEM((2 * width, hidden_width), BF16),
            pltpu.VMEM((node_rows, hidden_width), BF16),
            pltpu.VMEM((2 * width, hidden_width), F32),
        ]
        + [pltpu.VMEM(shape.shape, shape.dtype) for shape in shapes]
        + [
            pltpu.SemaphoreType.DMA((tiles // CHUNK,)),
            pltpu.SemaphoreType.DMA((5 + parts,)),
            pltpu.SemaphoreType.DMA((3,)),
        ],
        compiler_params=params(WHOLE),
        name="forward",
    )(targets, sources, count, weights, features, halo, *hubs, out_grad, w_self, w_nbr)


def collect(live, wanted, order):
    def look(t, found):
        order[found] = t
        return found + wanted(t).astype(jnp.int32)

    found = lax.fori_loop(0, live, look, 0)
    for u in range(CHUNK):
        order[found + u] = 0
    return found


def add_tiles(found, order, chunks, targets, held, agg, totals, place, spare, arrived):
    block = held.shape[1]

    def step(c, waited):
        at = [order[c * CHUNK + u] for u in range(CHUNK)]
        last = order[jnp.minimum(c * CHUNK + CHUNK, found) - 1]
        needed = last // CHUNK + 1

        def wait(n, carry):
            arrived(n)
            return carry

        lax.fori_loop(waited, needed, wait, 0)
        products = [
            lax.dot_general(
                held[t],
                agg[rows_at(targets[t], block)],
                (((0,), (0,)), ((), ())),
                preferred_element_type=F32,
            )
            for t in at
        ]
        for u, value in enumerate(products):
            block_at = jnp.where(c * CHUNK + u < found, place(at[u]), spare)
            totals[rows_at(block_at, block)] += value
        return needed

    waited = lax.fori_loop(0, (found + CHUNK - 1) // CHUNK, step, 0)

    def rest(n, carry):
        arrived(n)
        return carry

    lax.fori_loop(waited, chunks, rest, 0)


def backward_far_kernel(
    targets,
    sources,
    count,
    weights,
    grad_agg,
    halo,
    near,
    far,
    order,
    held,
    agg,
    totals,
    halo_all,
    near_all,
    far_all,
    weight_sems,
    sems,
):
    block = weights.shape[1]
    node_rows, width = grad_agg.shape
    own_blocks = node_rows // block
    peers, slots, _ = halo.shape
    _, groups, hubs, _ = near.shape
    agg_copy = pltpu.make_async_copy(grad_agg, agg, sems.at[0])
    agg_copy.start()
    live = count[0]
    chunks = (live + CHUNK - 1) // CHUNK
    start_weights(0, chunks, weights, held, weight_sems)
    rep = lax.axis_index("rep")
    core = lax.axis_index("core")
    totals[...] = jnp.zeros_like(totals)
    found = collect(live, lambda t: sources[t] >= own_blocks, order)
    agg_copy.wait()
    add_tiles(
        found,
        order,
        chunks,
        targets,
        held,
        agg,
        totals,
        lambda t: sources[t] - own_blocks,
        totals.shape[0] // block - 1,
        lambda n: weight_copy(n, weights, held, weight_sems).wait(),
    )
    outs = [
        pltpu.make_async_copy(x, y, sems.at[n])
        for n, (x, y) in enumerate(((far_all, far), (halo_all, halo), (near_all, near)))
    ]
    halo_base = groups * CORES * REPS * hubs

    def emit_hub(piece, to_core):
        def emit(p, carry):
            for i in range(REPS):
                to_rep = lax.rem(rep + i, REPS)
                part = (p * CORES + to_core) * REPS + to_rep
                piece[i, p] = totals[rows_at(part, hubs)].astype(BF16)
            return carry

        lax.fori_loop(0, groups, emit, 0, unroll=4)

    def emit_halo(p, carry):
        at = pl.multiple_of(halo_base + p * slots, slots)
        halo_all[p] = totals[pl.ds(at, slots)].astype(BF16)
        return carry

    emit_hub(far_all, 1 - core)
    outs[0].start()
    lax.fori_loop(0, peers, emit_halo, 0, unroll=8)
    outs[1].start()
    emit_hub(near_all, core)
    outs[2].start()
    for copy in outs:
        copy.wait()


def backward_far(targets, sources, count, weights, grad_agg, peers, slots, hubs):
    node_rows, width = grad_agg.shape
    tiles, block, _ = weights.shape
    groups = peers // CORES
    total_rows = peers * REPS * hubs + peers * slots + block
    halo = jax.ShapeDtypeStruct((peers, slots, width), BF16)
    piece = jax.ShapeDtypeStruct((REPS, groups, hubs, width), BF16)
    return pl.pallas_call(
        backward_far_kernel,
        out_shape=(halo, piece, piece),
        in_specs=[smem()] * 3 + [hbm()] * 2,
        out_specs=(hbm(),) * 3,
        scratch_shapes=[
            pltpu.SMEM((tiles + CHUNK,), jnp.int32),
            pltpu.VMEM((tiles, block, block), BF16),
            pltpu.VMEM((node_rows, width), BF16),
            pltpu.VMEM((total_rows, width), F32),
            pltpu.VMEM(halo.shape, BF16),
            pltpu.VMEM(piece.shape, BF16),
            pltpu.VMEM(piece.shape, BF16),
            pltpu.SemaphoreType.DMA((tiles // CHUNK,)),
            pltpu.SemaphoreType.DMA((3,)),
        ],
        compiler_params=params(WHOLE),
        name="backward_far",
    )(targets, sources, count, weights, grad_agg)


def own_rows_kernel(
    targets,
    sources,
    count,
    hub_rows,
    weights,
    grad_agg,
    grad_self,
    returned,
    ids_across,
    ids_down,
    out,
    near,
    order,
    held,
    agg,
    totals,
    scattered,
    rows,
    spread,
    weight_sems,
    sems,
    out_sems,
):
    block = weights.shape[1]
    node_rows, width = grad_agg.shape
    own_blocks = node_rows // block
    slots = returned.shape[0]
    folded = node_rows // FOLDS
    copies = [
        pltpu.make_async_copy(x, y, sems.at[n])
        for n, (x, y) in enumerate(
            (
                (returned, rows),
                (grad_agg, agg),
                (grad_self, totals.at[pl.ds(0, node_rows)]),
            )
        )
    ]
    for copy in copies:
        copy.start()
    live = count[0]
    chunks = (live + CHUNK - 1) // CHUNK
    start_weights(0, chunks, weights, held, weight_sems)
    totals[node_rows:] = jnp.zeros((block, width), F32)
    found = collect(live, lambda t: sources[t] < own_blocks, order)
    down = jnp.concatenate(
        [ids_down[...], jnp.zeros((block - ids_down.shape[0], block), F32)], 0
    ).T
    copies[0].wait()
    for j in range(slots // block):
        part = pl.ds(j * block, block)
        fold = jnp.broadcast_to(down[:, j : j + 1], (block, width))
        value = rows[part].astype(F32)
        for q in range(FOLDS):
            inside = (fold >= q * folded) & (fold < (q + 1) * folded)
            spread[part, pl.ds(q * width, width)] = jnp.where(inside, value, 0.0).astype(BF16)
    across = ids_across[...] % folded
    steps = folded // FOLD_ROWS

    def spots(c):
        return [pl.ds(q * folded + c * FOLD_ROWS, FOLD_ROWS) for q in range(FOLDS)]

    for c in range(steps):
        ids = lax.broadcasted_iota(jnp.int32, (FOLD_ROWS, slots), 0) + c * FOLD_ROWS
        hot = (ids == across).astype(F32).astype(BF16)
        added = jnp.dot(hot, spread[...], preferred_element_type=F32)
        for q, at in enumerate(spots(c)):
            scattered[at] = added[:, q * width : (q + 1) * width]
    for copy in copies[1:]:
        copy.wait()
    add_tiles(
        found,
        order,
        chunks,
        targets,
        held,
        agg,
        totals,
        lambda t: sources[t],
        own_blocks,
        lambda n: weight_copy(n, weights, held, weight_sems).wait(),
    )
    outs = []
    for c in range(steps):
        for q, at in enumerate(spots(c)):
            totals[at] += scattered[at]
            outs.append(pltpu.make_async_copy(totals.at[at], out.at[at], out_sems.at[c, q]))
            outs[-1].start()
    for h in range(hub_rows.shape[0]):
        near[pl.ds(h * TILE, TILE)] = totals[rows_at(hub_rows[h] // TILE, TILE)]

    for copy in outs:
        copy.wait()


def own_rows(
    targets, sources, count, hub_rows, weights, grad_agg, grad_self, returned, send_ids
):
    node_rows, width = grad_agg.shape
    tiles, block, _ = weights.shape
    hubs = hub_rows.shape[0]
    slots = returned.shape[0] * returned.shape[1]
    return pl.pallas_call(
        own_rows_kernel,
        out_shape=(
            jax.ShapeDtypeStruct((node_rows, width), F32),
            jax.ShapeDtypeStruct((hubs * TILE, width), F32),
        ),
        in_specs=[smem()] * 4 + [hbm()] * 4 + [vmem()] * 2,
        out_specs=(hbm(), vmem()),
        scratch_shapes=[
            pltpu.SMEM((tiles + CHUNK,), jnp.int32),
            pltpu.VMEM((tiles, block, block), BF16),
            pltpu.VMEM((node_rows, width), BF16),
            pltpu.VMEM((node_rows + block, width), F32),
            pltpu.VMEM((node_rows, width), F32),
            pltpu.VMEM((slots, width), BF16),
            pltpu.VMEM((slots, FOLDS * width), BF16),
            pltpu.SemaphoreType.DMA((tiles // CHUNK,)),
            pltpu.SemaphoreType.DMA((3,)),
            pltpu.SemaphoreType.DMA((node_rows // FOLDS // FOLD_ROWS, FOLDS)),
        ],
        compiler_params=params(WHOLE),
        name="own_rows",
    )(
        targets,
        sources,
        count,
        hub_rows,
        weights,
        grad_agg,
        grad_self,
        returned.reshape(slots, width),
        send_ids.reshape(1, slots),
        send_ids.reshape(slots // block, block).astype(F32),
    )


def split_pair(total):
    high = total.astype(BF16)
    return high, (total - high.astype(F32)).astype(BF16)


def fold_kernel(slices, out):
    def peer(p, total):
        return total + slices[p].astype(F32)

    total = lax.fori_loop(0, slices.shape[0], peer, jnp.zeros(slices.shape[1:], F32))
    out[0], out[1] = split_pair(total)


def fold(slices):
    return pl.pallas_call(
        fold_kernel,
        out_shape=jax.ShapeDtypeStruct((2, *slices.shape[1:]), BF16),
        in_specs=[vmem()],
        out_specs=vmem(),
        compiler_params=params(8),
        name="fold",
    )(slices)


def join_kernel(near, far, w_near, w_far, *outs):
    groups = near.shape[1]
    total = (w_near[0].astype(F32) + w_near[1].astype(F32)) + (
        w_far[0].astype(F32) + w_far[1].astype(F32)
    )
    high, low = split_pair(total)
    for out in outs:
        out[groups] = high
        out[groups + 1] = low

    def group(p, carry):
        for i, out in enumerate(outs):
            out[p] = (near[i, p].astype(F32) + far[i, p].astype(F32)).astype(BF16)
        return carry

    lax.fori_loop(0, groups, group, 0)


def join(near, far, w_near, w_far):
    reps, groups, hubs, width = near.shape
    piece = jax.ShapeDtypeStruct((groups + 2, hubs, width), BF16)
    return pl.pallas_call(
        join_kernel,
        out_shape=(piece,) * reps,
        in_specs=[vmem()] * 4,
        out_specs=(vmem(),) * reps,
        compiler_params=params(8),
        name="join",
    )(near, far, w_near, w_far)


def merge_kernel(hub0, hub1, hub2, hub3, out, w_parts):
    groups, message, width = out.shape
    hubs = hub0.shape[1]
    rep = lax.axis_index("rep")
    for i, piece in enumerate((hub0, hub1, hub2, hub3)):
        w_parts[lax.rem(rep - i + REPS, REPS)] = piece[groups].astype(F32) + piece[
            groups + 1
        ].astype(F32)
    w_total = (((w_parts[0] + w_parts[1]) + w_parts[2]) + w_parts[3]).astype(BF16)

    def group(p, carry):
        total = (hub0[p].astype(F32) + hub1[p].astype(F32)) + (
            hub2[p].astype(F32) + hub3[p].astype(F32)
        )
        out[p, :hubs] = total.astype(BF16)
        out[p, hubs:] = w_total
        return carry

    lax.fori_loop(0, groups, group, 0)


def merge(pieces):
    groups, hubs, width = pieces[0].shape
    return pl.pallas_call(
        merge_kernel,
        out_shape=jax.ShapeDtypeStruct((groups - 2, 2 * hubs, width), BF16),
        in_specs=[vmem()] * 4,
        out_specs=vmem(),
        scratch_shapes=[pltpu.VMEM((REPS, hubs, width), F32)],
        compiler_params=params(8),
        name="merge",
    )(*pieces)


def finish(hub_rows, received, around, grad_nodes, hidden_width, grad_scale):
    groups, message, width = received.shape
    hubs = hub_rows.shape[0]
    w_rows = message - hubs

    def body(
        hub_rows, received, around, grad_nodes, out, grad_self, grad_nbr, near, held, sems
    ):
        at = [hub_rows[h] // TILE for h in range(hubs)]
        near[...] = around[...]

        def place(p, total):
            held[rows_at(p, w_rows)] = received[p, hubs:].astype(F32) * grad_scale
            return total + received[p, :hubs].astype(F32)

        total = lax.fori_loop(0, groups, place, jnp.zeros((hubs, width), F32), unroll=4)
        first = []
        for h in range(hubs):
            slot = jnp.int32(h)
            for j in reversed(range(h)):
                slot = jnp.where(at[j] == at[h], j, slot)
            first.append(slot)
            row = slot * TILE + hub_rows[h] % TILE
            near[pl.ds(row, 1)] += total[h : h + 1]

        def back(h):
            return pltpu.make_async_copy(
                near.at[pl.ds(h * TILE, TILE)], out.at[rows_at(at[h], TILE)], sems.at[h]
            )

        for h in range(hubs):
            pl.when(first[h] == h)(back(h).start)
        for k in range(hidden_width // width):
            columns = pl.ds(k * width, width)
            grad_self[:, columns] = held[2 * k * width : (2 * k + 1) * width]
            grad_nbr[:, columns] = held[(2 * k + 1) * width : (2 * k + 2) * width]
        for h in range(hubs):
            pl.when(first[h] == h)(back(h).wait)

    return pl.pallas_call(
        body,
        out_shape=(
            jax.ShapeDtypeStruct(grad_nodes.shape, F32),
            jax.ShapeDtypeStruct((width, hidden_width), F32),
            jax.ShapeDtypeStruct((width, hidden_width), F32),
        ),
        in_specs=[smem(), vmem(), vmem(), hbm()],
        out_specs=(hbm(), vmem(), vmem()),
        input_output_aliases={3: 0},
        scratch_shapes=[
            pltpu.VMEM((hubs * TILE, width), F32),
            pltpu.VMEM((groups * w_rows, width), F32),
            pltpu.SemaphoreType.DMA((hubs,)),
        ],
        compiler_params=params(FINISH),
        name="finish",
    )(hub_rows, received, around, grad_nodes)


def rep_shift(value, shift):
    return lax.ppermute(value, "rep", [(j, (j + shift) % REPS) for j in range(REPS)])


def core_swap(value):
    return lax.ppermute(value, "core", [(0, 1), (1, 0)])


def swap(value, axes):
    return lax.all_to_all(value, axes, split_axis=0, concat_axis=0, tiled=True)


def shards(
    features,
    out_grad,
    w_self,
    w_nbr,
    hub_rows,
    send_rows,
    send_counts,
    tile_targets,
    tile_sources,
    tile_count,
    tile_weights,
):
    node_rows, width = features.shape
    peers, slots = send_rows.shape
    hubs = hub_rows.shape[0]
    groups = peers // CORES
    own_rep = swap(hub_pack(hub_rows, features, groups), GROUP)
    halo = swap(halo_pack(send_rows, send_counts, features), DOM)
    near = [own_rep] + [rep_shift(own_rep, i) for i in range(1, REPS)]
    far = [core_swap(piece) for piece in near]
    hidden, grad_agg, grad_self, grad_w = forward(
        tile_targets, tile_sources, tile_count, tile_weights, features, halo, near + far,
        out_grad, w_self, w_nbr,
    )
    w_slices = swap(grad_w.reshape(groups, -1, width), GROUP)
    grad_halo, near, far = backward_far(
        tile_targets, tile_sources, tile_count, tile_weights, grad_agg, peers, slots, hubs
    )
    returned = swap(grad_halo, DOM)
    w_pair = fold(w_slices)
    pieces = join(near, core_swap(far), w_pair, core_swap(w_pair))
    pieces = [pieces[0]] + [rep_shift(pieces[i], i) for i in range(1, REPS)]
    merged = swap(merge(pieces), GROUP)
    slot_live = jnp.arange(slots, dtype=jnp.int32)[None, :] < send_counts[:, None]
    send_ids = jnp.where(slot_live, send_rows, node_rows)
    grad_nodes, around = own_rows(
        tile_targets, tile_sources, tile_count, hub_rows, tile_weights, grad_agg, grad_self,
        returned, send_ids,
    )
    grad_scale = 1.0 / math.sqrt(node_rows * peers * REPS)
    grad_features, grad_w_self, grad_w_nbr = finish(
        hub_rows, merged, around, grad_nodes, w_self.shape[1], grad_scale
    )
    return (hidden, grad_features, grad_w_self, grad_w_nbr)


def solution(mesh):
    fine = Mesh(mesh.devices.reshape(-1, CORES, REPS), ("group", "core", "rep"))
    every = ("group", "core", "rep")
    return jax.shard_map(
        shards,
        mesh=fine,
        in_specs=(
            P(every, None),
            P(every, None),
            P(),
            P(),
            P(every),
            P(every, None),
            P(every),
            P(every),
            P(every),
            P(every),
            P(every, None, None),
        ),
        out_specs=(P(every, None), P(every, None), P(), P()),
        check_vma=False,
    )
```

```python
import math

import jax
import jax.numpy as jnp
from jax import lax
from jax.experimental import pallas as pl
from jax.experimental.pallas import tpu as pltpu
from jax.sharding import Mesh
from jax.sharding import PartitionSpec as P

BF16 = jnp.bfloat16
F32 = jnp.float32
CHUNK = 16
ROWS = 1024
NEAR = 16
TILE = 8
PARTS = 4
WHOLE = 60
FORWARD = 52
FAR = 52
OWN = 52
FINISH = 16
FOLDS = 4
FOLD_ROWS = 512
REPS = 4
CORES = 2
GROUP = "group"
DOM = ("group", "core")


def smem():
    return pl.BlockSpec(memory_space=pltpu.SMEM)


def vmem():
    return pl.BlockSpec(memory_space=pltpu.VMEM)


def hbm():
    return pl.BlockSpec(memory_space=pl.ANY)


def params(mebibytes):
    return pltpu.CompilerParams(vmem_limit_bytes=mebibytes * 1024 * 1024)


def rows_at(index, size):
    return pl.ds(pl.multiple_of(index * size, size), size)


def hub_pack_kernel(hub_rows, features, out, near, wide, sems):
    hubs = hub_rows.shape[0]
    copies = []
    for h in range(hubs):
        start = pl.multiple_of(hub_rows[h] // NEAR * NEAR, NEAR)
        copies.append(
            pltpu.make_async_copy(
                features.at[pl.ds(start, NEAR)], near.at[pl.ds(h * NEAR, NEAR)], sems.at[h]
            )
        )
        copies[-1].start()
    for copy in copies:
        copy.wait()
    wide[hubs:] = near[...].astype(F32)
    for h in range(hubs):
        row = hubs + h * NEAR + hub_rows[h] % NEAR
        wide[h : h + 1] = wide[pl.ds(row, 1)]
    own_hubs = wide[:hubs].astype(BF16)

    def emit(p, carry):
        out[p] = own_hubs
        return carry

    lax.fori_loop(0, out.shape[0], emit, 0)


def hub_pack(hub_rows, features, peers):
    hubs = hub_rows.shape[0]
    width = features.shape[1]
    return pl.pallas_call(
        hub_pack_kernel,
        out_shape=jax.ShapeDtypeStruct((peers, hubs, width), BF16),
        in_specs=[smem(), hbm()],
        out_specs=vmem(),
        scratch_shapes=[
            pltpu.VMEM((hubs * NEAR, width), BF16),
            pltpu.VMEM((hubs + hubs * NEAR, width), F32),
            pltpu.SemaphoreType.DMA((hubs,)),
        ],
        compiler_params=params(WHOLE),
        name="hub_pack",
    )(hub_rows, features)


def halo_pack_kernel(send_slots, send_counts, features, out, wide, staged):
    slots, peers = send_slots.shape
    wide[...] = features[...].astype(F32)

    def peer(p, carry):
        for k in range(slots):
            staged[pl.ds(p * slots + k, 1)] = wide[pl.ds(send_slots[k, p], 1)]
        return carry

    lax.fori_loop(0, peers, peer, 0)
    slot = lax.broadcasted_iota(jnp.int32, (slots, out.shape[2]), 0)

    def emit(p, carry):
        rows = staged[rows_at(p, slots)]
        out[p] = jnp.where(slot < send_counts[p], rows, 0.0).astype(BF16)
        return carry

    lax.fori_loop(0, peers, emit, 0)


def halo_pack(send_rows, send_counts, features):
    peers, slots = send_rows.shape
    node_rows, width = features.shape
    return pl.pallas_call(
        halo_pack_kernel,
        out_shape=jax.ShapeDtypeStruct((peers, slots, width), BF16),
        in_specs=[smem(), smem(), vmem()],
        out_specs=vmem(),
        scratch_shapes=[
            pltpu.VMEM((node_rows, width), F32),
            pltpu.VMEM((peers * slots, width), F32),
        ],
        compiler_params=params(WHOLE),
        name="halo_pack",
    )(send_rows.T, send_counts, features)


def weight_copy(c, weights, held, sems):
    part = rows_at(c, CHUNK)
    return pltpu.make_async_copy(weights.at[part], held.at[part], sems.at[c])


def start_weights(first, chunks, weights, held, sems):
    def start(c, carry):
        weight_copy(c, weights, held, sems).start()
        return carry

    lax.fori_loop(first, chunks, start, 0)


def forward_kernel(
    targets,
    sources,
    count,
    weights,
    features,
    halo,
    *refs,
):
    hubs, refs = refs[: REPS * CORES], refs[REPS * CORES :]
    out_grad, w_self, w_nbr, hidden, grad_agg, grad_self, grad_w, *refs = refs
    held, source_rows, totals, w_both, grads_in, grad_total, hidden_all, *refs = refs
    agg_all, self_all, w_all, weight_sems, sems, out_sems = refs
    block = weights.shape[1]
    target_blocks, parts, part_rows, width = features.shape
    hub_blocks = hubs[0].shape[0]
    halo_blocks = halo.shape[0]
    node_rows = target_blocks * block
    rep = lax.axis_index("rep")
    core = lax.axis_index("core")
    pieces = [(features, source_rows.at[pl.ds(0, target_blocks)])]
    for c in range(CORES):
        for i in range(REPS):
            from_core = lax.rem(core + c, CORES)
            from_rep = lax.rem(rep - i + REPS, REPS)
            part = from_core * REPS + from_rep
            pieces.append(
                (hubs[c * REPS + i], source_rows.at[pl.ds(target_blocks, hub_blocks), part])
            )
    pieces.append((halo, source_rows.at[pl.ds(target_blocks + hub_blocks, halo_blocks)]))
    early = [pltpu.make_async_copy(x, y, sems.at[n]) for n, (x, y) in enumerate(pieces)]
    for copy in early:
        copy.start()
    live = count[0]
    chunks = (live + CHUNK - 1) // CHUNK
    start_weights(0, chunks, weights, held, weight_sems)
    late = [
        pltpu.make_async_copy(x, y, sems.at[len(pieces) + n])
        for n, (x, y) in enumerate(
            (
                (w_self, w_both.at[pl.ds(0, width)]),
                (w_nbr, w_both.at[pl.ds(width, width)]),
                (out_grad, grads_in),
            )
        )
    ]
    for copy in late:
        copy.start()
    ones = jnp.ones((block, width), BF16)

    def product(t):
        picked = source_rows[sources[t]].reshape(block, width)
        return jnp.dot(
            held[t], jnp.concatenate([picked, ones], 1), preferred_element_type=F32
        )

    for copy in early:
        copy.wait()
    leading = target_blocks // CHUNK

    def first(c, carry):
        weight_copy(c, weights, held, weight_sems).wait()
        for u in range(CHUNK):
            totals[c * CHUNK + u] = product(c * CHUNK + u)
        return carry

    lax.fori_loop(0, leading, first, 0)

    def more(c, carry):
        weight_copy(c, weights, held, weight_sems).wait()
        products = [product(c * CHUNK + u) for u in range(CHUNK)]
        for u, value in enumerate(products):
            t = c * CHUNK + u
            target = jnp.where(t < live, targets[t], target_blocks)
            totals[target] += value
        return carry

    lax.fori_loop(leading, chunks, more, 0)
    grad_total[...] = jnp.zeros_like(grad_total)
    per_chunk = ROWS // block
    for copy in late:
        copy.wait()

    def outs(c):
        rows = rows_at(c, ROWS)
        return [
            pltpu.make_async_copy(x.at[rows], y.at[rows], out_sems.at[n])
            for n, (x, y) in enumerate(
                ((hidden_all, hidden), (agg_all, grad_agg), (self_all, grad_self))
            )
        ]

    def dense(c, carry):
        rows = rows_at(c, ROWS)
        blocks_at = pl.ds(c * per_chunk, per_chunk)
        total = totals[blocks_at].reshape(ROWS, 2 * width)
        inverse = 1.0 / jnp.maximum(total[:, width:], 1.0)
        aggregate = (total[:, :width] * inverse).astype(BF16)
        own = source_rows[blocks_at].reshape(ROWS, width)
        both = jnp.concatenate([own, aggregate], 1)
        preact = jnp.dot(both, w_both[...], preferred_element_type=F32)
        sigmoid = 0.5 * jnp.tanh(0.5 * preact) + 0.5
        activated = preact * sigmoid
        hidden_all[rows] = activated.astype(BF16)
        slope = sigmoid + activated * (1.0 - sigmoid)
        grad_preact = (grads_in[rows].astype(F32) * slope).astype(BF16)
        grad_total[...] += lax.dot_general(
            both, grad_preact, (((0,), (0,)), ((), ())), preferred_element_type=F32
        )
        back = lax.dot_general(
            grad_preact, w_both[...], (((1,), (1,)), ((), ())), preferred_element_type=F32
        )
        self_all[rows] = back[:, :width]
        agg_all[rows] = (back[:, width:] * inverse).astype(BF16)
        for copy in outs(c):
            copy.start()
        return carry

    steps = node_rows // ROWS
    lax.fori_loop(0, steps, dense, 0)
    half = grad_total.shape[1] // 2
    w_all[: grad_total.shape[0]] = grad_total[:, :half].astype(BF16)
    w_all[grad_total.shape[0] :] = grad_total[:, half:].astype(BF16)
    w_copy = pltpu.make_async_copy(w_all, grad_w, sems.at[0])
    w_copy.start()

    def drain(c, carry):
        for copy in outs(c):
            copy.wait()
        return carry

    lax.fori_loop(0, steps, drain, 0)
    w_copy.wait()


def forward(targets, sources, count, weights, features, halo, hubs, out_grad, w_self, w_nbr):
    node_rows, width = features.shape
    tiles, block, _ = weights.shape
    hidden_width = w_self.shape[1]
    parts = REPS * CORES
    part_rows = block // parts
    in_blocks = lambda value: value.reshape(-1, parts, part_rows, width)
    features = in_blocks(features)
    halo = in_blocks(halo)
    source_blocks = features.shape[0] + hubs[0].shape[0] + halo.shape[0]
    shapes = (
        jax.ShapeDtypeStruct((node_rows, hidden_width), BF16),
        jax.ShapeDtypeStruct((node_rows, width), BF16),
        jax.ShapeDtypeStruct((node_rows, width), F32),
        jax.ShapeDtypeStruct((4 * width, hidden_width // 2), BF16),
    )
    return pl.pallas_call(
        forward_kernel,
        out_shape=shapes,
        in_specs=[smem()] * 3 + [hbm()] * (6 + parts),
        out_specs=(hbm(),) * 4,
        scratch_shapes=[
            pltpu.VMEM((tiles, block, block), BF16),
            pltpu.VMEM((source_blocks, parts, part_rows, width), BF16),
            pltpu.VMEM((node_rows // block + 1, block, 2 * width), F32),
            pltpu.VMEM((2 * width, hidden_width), BF16),
            pltpu.VMEM((node_rows, hidden_width), BF16),
            pltpu.VMEM((2 * width, hidden_width), F32),
        ]
        + [pltpu.VMEM(shape.shape, shape.dtype) for shape in shapes]
        + [
            pltpu.SemaphoreType.DMA((tiles // CHUNK,)),
            pltpu.SemaphoreType.DMA((5 + parts,)),
            pltpu.SemaphoreType.DMA((3,)),
        ],
        compiler_params=params(FORWARD),
        name="forward",
    )(targets, sources, count, weights, features, halo, *hubs, out_grad, w_self, w_nbr)


def collect(live, wanted, order):
    def look(t, found):
        order[found] = t
        return found + wanted(t).astype(jnp.int32)

    found = lax.fori_loop(0, live, look, 0)
    for u in range(CHUNK):
        order[found + u] = 0
    return found


def add_tiles(found, order, chunks, targets, held, agg, totals, place, spare, arrived):
    block = held.shape[1]

    def step(c, waited):
        at = [order[c * CHUNK + u] for u in range(CHUNK)]
        last = order[jnp.minimum(c * CHUNK + CHUNK, found) - 1]
        needed = last // CHUNK + 1

        def wait(n, carry):
            arrived(n)
            return carry

        lax.fori_loop(waited, needed, wait, 0)
        products = [
            lax.dot_general(
                held[t],
                agg[rows_at(targets[t], block)],
                (((0,), (0,)), ((), ())),
                preferred_element_type=F32,
            )
            for t in at
        ]
        for u, value in enumerate(products):
            block_at = jnp.where(c * CHUNK + u < found, place(at[u]), spare)
            totals[rows_at(block_at, block)] += value
        return needed

    waited = lax.fori_loop(0, (found + CHUNK - 1) // CHUNK, step, 0)

    def rest(n, carry):
        arrived(n)
        return carry

    lax.fori_loop(waited, chunks, rest, 0)


def backward_far_kernel(
    targets,
    sources,
    count,
    weights,
    grad_agg,
    halo,
    near,
    far,
    order,
    held,
    agg,
    totals,
    halo_all,
    near_all,
    far_all,
    weight_sems,
    sems,
):
    block = weights.shape[1]
    node_rows, width = grad_agg.shape
    own_blocks = node_rows // block
    peers, slots, _ = halo.shape
    _, groups, hubs, _ = near.shape
    agg_copy = pltpu.make_async_copy(grad_agg, agg, sems.at[0])
    agg_copy.start()
    live = count[0]
    chunks = (live + CHUNK - 1) // CHUNK
    start_weights(0, chunks, weights, held, weight_sems)
    rep = lax.axis_index("rep")
    core = lax.axis_index("core")
    totals[...] = jnp.zeros_like(totals)
    found = collect(live, lambda t: sources[t] >= own_blocks, order)
    agg_copy.wait()
    add_tiles(
        found,
        order,
        chunks,
        targets,
        held,
        agg,
        totals,
        lambda t: sources[t] - own_blocks,
        totals.shape[0] // block - 1,
        lambda n: weight_copy(n, weights, held, weight_sems).wait(),
    )
    outs = [
        pltpu.make_async_copy(x, y, sems.at[n])
        for n, (x, y) in enumerate(((far_all, far), (halo_all, halo), (near_all, near)))
    ]
    halo_base = groups * CORES * REPS * hubs

    def emit_hub(piece, to_core):
        def emit(p, carry):
            for i in range(REPS):
                to_rep = lax.rem(rep + i, REPS)
                part = (p * CORES + to_core) * REPS + to_rep
                piece[i, p] = totals[rows_at(part, hubs)].astype(BF16)
            return carry

        lax.fori_loop(0, groups, emit, 0, unroll=4)

    def emit_halo(p, carry):
        at = pl.multiple_of(halo_base + p * slots, slots)
        halo_all[p] = totals[pl.ds(at, slots)].astype(BF16)
        return carry

    emit_hub(far_all, 1 - core)
    outs[0].start()
    lax.fori_loop(0, peers, emit_halo, 0, unroll=8)
    outs[1].start()
    emit_hub(near_all, core)
    outs[2].start()
    for copy in outs:
        copy.wait()


def backward_far(targets, sources, count, weights, grad_agg, peers, slots, hubs):
    node_rows, width = grad_agg.shape
    tiles, block, _ = weights.shape
    groups = peers // CORES
    total_rows = peers * REPS * hubs + peers * slots + block
    halo = jax.ShapeDtypeStruct((peers, slots, width), BF16)
    piece = jax.ShapeDtypeStruct((REPS, groups, hubs, width), BF16)
    return pl.pallas_call(
        backward_far_kernel,
        out_shape=(halo, piece, piece),
        in_specs=[smem()] * 3 + [hbm()] * 2,
        out_specs=(hbm(),) * 3,
        scratch_shapes=[
            pltpu.SMEM((tiles + CHUNK,), jnp.int32),
            pltpu.VMEM((tiles, block, block), BF16),
            pltpu.VMEM((node_rows, width), BF16),
            pltpu.VMEM((total_rows, width), F32),
            pltpu.VMEM(halo.shape, BF16),
            pltpu.VMEM(piece.shape, BF16),
            pltpu.VMEM(piece.shape, BF16),
            pltpu.SemaphoreType.DMA((tiles // CHUNK,)),
            pltpu.SemaphoreType.DMA((3,)),
        ],
        compiler_params=params(FAR),
        name="backward_far",
    )(targets, sources, count, weights, grad_agg)


def own_rows_kernel(
    targets,
    sources,
    count,
    hub_rows,
    weights,
    grad_agg,
    grad_self,
    returned,
    ids_across,
    ids_down,
    out,
    near,
    order,
    held,
    agg,
    totals,
    scattered,
    rows,
    spread,
    weight_sems,
    sems,
    out_sems,
):
    block = weights.shape[1]
    node_rows, width = grad_agg.shape
    own_blocks = node_rows // block
    slots = returned.shape[0]
    folded = node_rows // FOLDS
    copies = [
        pltpu.make_async_copy(x, y, sems.at[n])
        for n, (x, y) in enumerate(
            (
                (returned, rows),
                (grad_agg, agg),
                (grad_self, totals.at[pl.ds(0, node_rows)]),
            )
        )
    ]
    for copy in copies:
        copy.start()
    live = count[0]
    chunks = (live + CHUNK - 1) // CHUNK
    start_weights(0, chunks, weights, held, weight_sems)
    totals[node_rows:] = jnp.zeros((block, width), F32)
    found = collect(live, lambda t: sources[t] < own_blocks, order)
    down = jnp.concatenate(
        [ids_down[...], jnp.zeros((block - ids_down.shape[0], block), F32)], 0
    ).T
    copies[0].wait()
    for j in range(slots // block):
        part = pl.ds(j * block, block)
        fold = jnp.broadcast_to(down[:, j : j + 1], (block, width))
        value = rows[part].astype(F32)
        for q in range(FOLDS):
            inside = (fold >= q * folded) & (fold < (q + 1) * folded)
            spread[part, pl.ds(q * width, width)] = jnp.where(inside, value, 0.0).astype(BF16)
    across = ids_across[...] % folded
    steps = folded // FOLD_ROWS

    def spots(c):
        return [pl.ds(q * folded + c * FOLD_ROWS, FOLD_ROWS) for q in range(FOLDS)]

    for c in range(steps):
        ids = lax.broadcasted_iota(jnp.int32, (FOLD_ROWS, slots), 0) + c * FOLD_ROWS
        hot = (ids == across).astype(F32).astype(BF16)
        added = jnp.dot(hot, spread[...], preferred_element_type=F32)
        for q, at in enumerate(spots(c)):
            scattered[at] = added[:, q * width : (q + 1) * width]
    for copy in copies[1:]:
        copy.wait()
    add_tiles(
        found,
        order,
        chunks,
        targets,
        held,
        agg,
        totals,
        lambda t: sources[t],
        own_blocks,
        lambda n: weight_copy(n, weights, held, weight_sems).wait(),
    )
    outs = []
    for c in range(steps):
        for q, at in enumerate(spots(c)):
            totals[at] += scattered[at]
            outs.append(pltpu.make_async_copy(totals.at[at], out.at[at], out_sems.at[c, q]))
            outs[-1].start()
    for h in range(hub_rows.shape[0]):
        near[pl.ds(h * TILE, TILE)] = totals[rows_at(hub_rows[h] // TILE, TILE)]

    for copy in outs:
        copy.wait()


def own_rows(
    targets, sources, count, hub_rows, weights, grad_agg, grad_self, returned, send_ids
):
    node_rows, width = grad_agg.shape
    tiles, block, _ = weights.shape
    hubs = hub_rows.shape[0]
    slots = returned.shape[0] * returned.shape[1]
    return pl.pallas_call(
        own_rows_kernel,
        out_shape=(
            jax.ShapeDtypeStruct((node_rows, width), F32),
            jax.ShapeDtypeStruct((hubs * TILE, width), F32),
        ),
        in_specs=[smem()] * 4 + [hbm()] * 4 + [vmem()] * 2,
        out_specs=(hbm(), vmem()),
        scratch_shapes=[
            pltpu.SMEM((tiles + CHUNK,), jnp.int32),
            pltpu.VMEM((tiles, block, block), BF16),
            pltpu.VMEM((node_rows, width), BF16),
            pltpu.VMEM((node_rows + block, width), F32),
            pltpu.VMEM((node_rows, width), F32),
            pltpu.VMEM((slots, width), BF16),
            pltpu.VMEM((slots, FOLDS * width), BF16),
            pltpu.SemaphoreType.DMA((tiles // CHUNK,)),
            pltpu.SemaphoreType.DMA((3,)),
            pltpu.SemaphoreType.DMA((node_rows // FOLDS // FOLD_ROWS, FOLDS)),
        ],
        compiler_params=params(OWN),
        name="own_rows",
    )(
        targets,
        sources,
        count,
        hub_rows,
        weights,
        grad_agg,
        grad_self,
        returned.reshape(slots, width),
        send_ids.reshape(1, slots),
        send_ids.reshape(slots // block, block).astype(F32),
    )


def split_pair(total):
    high = total.astype(BF16)
    return high, (total - high.astype(F32)).astype(BF16)


def fold_kernel(slices, out):
    def peer(p, total):
        return total + slices[p].astype(F32)

    total = lax.fori_loop(0, slices.shape[0], peer, jnp.zeros(slices.shape[1:], F32))
    out[0], out[1] = split_pair(total)


def fold(slices):
    return pl.pallas_call(
        fold_kernel,
        out_shape=jax.ShapeDtypeStruct((2, *slices.shape[1:]), BF16),
        in_specs=[vmem()],
        out_specs=vmem(),
        compiler_params=params(8),
        name="fold",
    )(slices)


def join_kernel(near, far, w_near, w_far, *outs):
    groups = near.shape[1]
    total = (w_near[0].astype(F32) + w_near[1].astype(F32)) + (
        w_far[0].astype(F32) + w_far[1].astype(F32)
    )
    high, low = split_pair(total)
    for out in outs:
        out[groups] = high
        out[groups + 1] = low

    def group(p, carry):
        for i, out in enumerate(outs):
            out[p] = (near[i, p].astype(F32) + far[i, p].astype(F32)).astype(BF16)
        return carry

    lax.fori_loop(0, groups, group, 0)


def join(near, far, w_near, w_far):
    reps, groups, hubs, width = near.shape
    piece = jax.ShapeDtypeStruct((groups + 2, hubs, width), BF16)
    return pl.pallas_call(
        join_kernel,
        out_shape=(piece,) * reps,
        in_specs=[vmem()] * 4,
        out_specs=(vmem(),) * reps,
        compiler_params=params(8),
        name="join",
    )(near, far, w_near, w_far)


def merge_kernel(hub0, hub1, hub2, hub3, out, w_parts):
    groups, message, width = out.shape
    hubs = hub0.shape[1]
    rep = lax.axis_index("rep")
    for i, piece in enumerate((hub0, hub1, hub2, hub3)):
        w_parts[lax.rem(rep - i + REPS, REPS)] = piece[groups].astype(F32) + piece[
            groups + 1
        ].astype(F32)
    w_total = (((w_parts[0] + w_parts[1]) + w_parts[2]) + w_parts[3]).astype(BF16)

    def group(p, carry):
        total = (hub0[p].astype(F32) + hub1[p].astype(F32)) + (
            hub2[p].astype(F32) + hub3[p].astype(F32)
        )
        out[p, :hubs] = total.astype(BF16)
        out[p, hubs:] = w_total
        return carry

    lax.fori_loop(0, groups, group, 0)


def merge(pieces):
    groups, hubs, width = pieces[0].shape
    return pl.pallas_call(
        merge_kernel,
        out_shape=jax.ShapeDtypeStruct((groups - 2, 2 * hubs, width), BF16),
        in_specs=[vmem()] * 4,
        out_specs=vmem(),
        scratch_shapes=[pltpu.VMEM((REPS, hubs, width), F32)],
        compiler_params=params(8),
        name="merge",
    )(*pieces)


def finish(hub_rows, received, around, grad_nodes, hidden_width, grad_scale):
    groups, message, width = received.shape
    hubs = hub_rows.shape[0]
    w_rows = message - hubs

    def body(
        hub_rows, received, around, grad_nodes, out, grad_self, grad_nbr, near, held, sems
    ):
        at = [hub_rows[h] // TILE for h in range(hubs)]
        near[...] = around[...]

        def place(p, total):
            held[rows_at(p, w_rows)] = received[p, hubs:].astype(F32) * grad_scale
            return total + received[p, :hubs].astype(F32)

        total = lax.fori_loop(0, groups, place, jnp.zeros((hubs, width), F32), unroll=4)
        first = []
        for h in range(hubs):
            slot = jnp.int32(h)
            for j in reversed(range(h)):
                slot = jnp.where(at[j] == at[h], j, slot)
            first.append(slot)
            row = slot * TILE + hub_rows[h] % TILE
            near[pl.ds(row, 1)] += total[h : h + 1]

        def back(h):
            return pltpu.make_async_copy(
                near.at[pl.ds(h * TILE, TILE)], out.at[rows_at(at[h], TILE)], sems.at[h]
            )

        for h in range(hubs):
            pl.when(first[h] == h)(back(h).start)
        for k in range(hidden_width // width):
            columns = pl.ds(k * width, width)
            grad_self[:, columns] = held[2 * k * width : (2 * k + 1) * width]
            grad_nbr[:, columns] = held[(2 * k + 1) * width : (2 * k + 2) * width]
        for h in range(hubs):
            pl.when(first[h] == h)(back(h).wait)

    return pl.pallas_call(
        body,
        out_shape=(
            jax.ShapeDtypeStruct(grad_nodes.shape, F32),
            jax.ShapeDtypeStruct((width, hidden_width), F32),
            jax.ShapeDtypeStruct((width, hidden_width), F32),
        ),
        in_specs=[smem(), vmem(), vmem(), hbm()],
        out_specs=(hbm(), vmem(), vmem()),
        input_output_aliases={3: 0},
        scratch_shapes=[
            pltpu.VMEM((hubs * TILE, width), F32),
            pltpu.VMEM((groups * w_rows, width), F32),
            pltpu.SemaphoreType.DMA((hubs,)),
        ],
        compiler_params=params(FINISH),
        name="finish",
    )(hub_rows, received, around, grad_nodes)


def rep_shift(value, shift):
    return lax.ppermute(value, "rep", [(j, (j + shift) % REPS) for j in range(REPS)])


def core_swap(value):
    return lax.ppermute(value, "core", [(0, 1), (1, 0)])


def swap(value, axes):
    return lax.all_to_all(value, axes, split_axis=0, concat_axis=0, tiled=True)


def shards(
    features,
    out_grad,
    w_self,
    w_nbr,
    hub_rows,
    send_rows,
    send_counts,
    tile_targets,
    tile_sources,
    tile_count,
    tile_weights,
):
    node_rows, width = features.shape
    peers, slots = send_rows.shape
    hubs = hub_rows.shape[0]
    groups = peers // CORES
    own_rep = swap(hub_pack(hub_rows, features, groups), GROUP)
    halo = swap(halo_pack(send_rows, send_counts, features), DOM)
    near = [own_rep] + [rep_shift(own_rep, i) for i in range(1, REPS)]
    far = [core_swap(piece) for piece in near]
    hidden, grad_agg, grad_self, grad_w = forward(
        tile_targets, tile_sources, tile_count, tile_weights, features, halo, near + far,
        out_grad, w_self, w_nbr,
    )
    w_slices = swap(grad_w.reshape(groups, -1, width), GROUP)
    grad_halo, near, far = backward_far(
        tile_targets, tile_sources, tile_count, tile_weights, grad_agg, peers, slots, hubs
    )
    returned = swap(grad_halo, DOM)
    w_pair = fold(w_slices)
    pieces = join(near, core_swap(far), w_pair, core_swap(w_pair))
    pieces = [pieces[0]] + [rep_shift(pieces[i], i) for i in range(1, REPS)]
    merged = swap(merge(pieces), GROUP)
    slot_live = jnp.arange(slots, dtype=jnp.int32)[None, :] < send_counts[:, None]
    send_ids = jnp.where(slot_live, send_rows, node_rows)
    grad_nodes, around = own_rows(
        tile_targets, tile_sources, tile_count, hub_rows, tile_weights, grad_agg, grad_self,
        returned, send_ids,
    )
    grad_scale = 1.0 / math.sqrt(node_rows * peers * REPS)
    grad_features, grad_w_self, grad_w_nbr = finish(
        hub_rows, merged, around, grad_nodes, w_self.shape[1], grad_scale
    )
    return (hidden, grad_features, grad_w_self, grad_w_nbr)


def solution(mesh):
    fine = Mesh(mesh.devices.reshape(-1, CORES, REPS), ("group", "core", "rep"))
    every = ("group", "core", "rep")
    return jax.shard_map(
        shards,
        mesh=fine,
        in_specs=(
            P(every, None),
            P(every, None),
            P(),
            P(),
            P(every),
            P(every, None),
            P(every),
            P(every),
            P(every),
            P(every),
            P(every, None, None),
        ),
        out_specs=(P(every, None), P(every, None), P(), P()),
        check_vma=False,
    )
```

```python
import math

import jax
import jax.numpy as jnp
from jax import lax
from jax.experimental import pallas as pl
from jax.experimental.pallas import tpu as pltpu
from jax.sharding import Mesh
from jax.sharding import PartitionSpec as P

BF16 = jnp.bfloat16
F32 = jnp.float32
CHUNK = 32
ROWS = 1024
NEAR = 16
TILE = 8
PARTS = 4
WHOLE = 60
FORWARD = 52
FAR = 52
OWN = 52
FINISH = 16
FOLDS = 4
FOLD_ROWS = 512
REPS = 4
CORES = 2
GROUP = "group"
DOM = ("group", "core")


def smem():
    return pl.BlockSpec(memory_space=pltpu.SMEM)


def vmem():
    return pl.BlockSpec(memory_space=pltpu.VMEM)


def hbm():
    return pl.BlockSpec(memory_space=pl.ANY)


def params(mebibytes):
    return pltpu.CompilerParams(vmem_limit_bytes=mebibytes * 1024 * 1024)


def rows_at(index, size):
    return pl.ds(pl.multiple_of(index * size, size), size)


def hub_pack_kernel(hub_rows, features, out, near, wide, sems):
    hubs = hub_rows.shape[0]
    copies = []
    for h in range(hubs):
        start = pl.multiple_of(hub_rows[h] // NEAR * NEAR, NEAR)
        copies.append(
            pltpu.make_async_copy(
                features.at[pl.ds(start, NEAR)], near.at[pl.ds(h * NEAR, NEAR)], sems.at[h]
            )
        )
        copies[-1].start()
    for copy in copies:
        copy.wait()
    wide[hubs:] = near[...].astype(F32)
    for h in range(hubs):
        row = hubs + h * NEAR + hub_rows[h] % NEAR
        wide[h : h + 1] = wide[pl.ds(row, 1)]
    own_hubs = wide[:hubs].astype(BF16)

    def emit(p, carry):
        out[p] = own_hubs
        return carry

    lax.fori_loop(0, out.shape[0], emit, 0)


def hub_pack(hub_rows, features, peers):
    hubs = hub_rows.shape[0]
    width = features.shape[1]
    return pl.pallas_call(
        hub_pack_kernel,
        out_shape=jax.ShapeDtypeStruct((peers, hubs, width), BF16),
        in_specs=[smem(), hbm()],
        out_specs=vmem(),
        scratch_shapes=[
            pltpu.VMEM((hubs * NEAR, width), BF16),
            pltpu.VMEM((hubs + hubs * NEAR, width), F32),
            pltpu.SemaphoreType.DMA((hubs,)),
        ],
        compiler_params=params(WHOLE),
        name="hub_pack",
    )(hub_rows, features)


def halo_pack_kernel(send_slots, send_counts, features, out, wide, staged):
    slots, peers = send_slots.shape
    wide[...] = features[...].astype(F32)

    def peer(p, carry):
        for k in range(slots):
            staged[pl.ds(p * slots + k, 1)] = wide[pl.ds(send_slots[k, p], 1)]
        return carry

    lax.fori_loop(0, peers, peer, 0)
    slot = lax.broadcasted_iota(jnp.int32, (slots, out.shape[2]), 0)

    def emit(p, carry):
        rows = staged[rows_at(p, slots)]
        out[p] = jnp.where(slot < send_counts[p], rows, 0.0).astype(BF16)
        return carry

    lax.fori_loop(0, peers, emit, 0)


def halo_pack(send_rows, send_counts, features):
    peers, slots = send_rows.shape
    node_rows, width = features.shape
    return pl.pallas_call(
        halo_pack_kernel,
        out_shape=jax.ShapeDtypeStruct((peers, slots, width), BF16),
        in_specs=[smem(), smem(), vmem()],
        out_specs=vmem(),
        scratch_shapes=[
            pltpu.VMEM((node_rows, width), F32),
            pltpu.VMEM((peers * slots, width), F32),
        ],
        compiler_params=params(WHOLE),
        name="halo_pack",
    )(send_rows.T, send_counts, features)


def weight_copy(c, weights, held, sems):
    part = rows_at(c, CHUNK)
    return pltpu.make_async_copy(weights.at[part], held.at[part], sems.at[c])


def start_weights(first, chunks, weights, held, sems):
    def start(c, carry):
        weight_copy(c, weights, held, sems).start()
        return carry

    lax.fori_loop(first, chunks, start, 0)


def forward_kernel(
    targets,
    sources,
    count,
    weights,
    features,
    halo,
    *refs,
):
    hubs, refs = refs[: REPS * CORES], refs[REPS * CORES :]
    out_grad, w_self, w_nbr, hidden, grad_agg, grad_self, grad_w, *refs = refs
    held, source_rows, totals, w_both, grads_in, grad_total, hidden_all, *refs = refs
    agg_all, self_all, w_all, weight_sems, sems, out_sems = refs
    block = weights.shape[1]
    target_blocks, parts, part_rows, width = features.shape
    hub_blocks = hubs[0].shape[0]
    halo_blocks = halo.shape[0]
    node_rows = target_blocks * block
    rep = lax.axis_index("rep")
    core = lax.axis_index("core")
    pieces = [(features, source_rows.at[pl.ds(0, target_blocks)])]
    for c in range(CORES):
        for i in range(REPS):
            from_core = lax.rem(core + c, CORES)
            from_rep = lax.rem(rep - i + REPS, REPS)
            part = from_core * REPS + from_rep
            pieces.append(
                (hubs[c * REPS + i], source_rows.at[pl.ds(target_blocks, hub_blocks), part])
            )
    pieces.append((halo, source_rows.at[pl.ds(target_blocks + hub_blocks, halo_blocks)]))
    early = [pltpu.make_async_copy(x, y, sems.at[n]) for n, (x, y) in enumerate(pieces)]
    for copy in early:
        copy.start()
    live = count[0]
    chunks = (live + CHUNK - 1) // CHUNK
    start_weights(0, chunks, weights, held, weight_sems)
    late = [
        pltpu.make_async_copy(x, y, sems.at[len(pieces) + n])
        for n, (x, y) in enumerate(
            (
                (w_self, w_both.at[pl.ds(0, width)]),
                (w_nbr, w_both.at[pl.ds(width, width)]),
                (out_grad, grads_in),
            )
        )
    ]
    for copy in late:
        copy.start()
    ones = jnp.ones((block, width), BF16)

    def product(t):
        picked = source_rows[sources[t]].reshape(block, width)
        return jnp.dot(
            held[t], jnp.concatenate([picked, ones], 1), preferred_element_type=F32
        )

    for copy in early:
        copy.wait()
    leading = target_blocks // CHUNK

    def first(c, carry):
        weight_copy(c, weights, held, weight_sems).wait()
        for u in range(CHUNK):
            totals[c * CHUNK + u] = product(c * CHUNK + u)
        return carry

    lax.fori_loop(0, leading, first, 0)

    def more(c, carry):
        weight_copy(c, weights, held, weight_sems).wait()
        products = [product(c * CHUNK + u) for u in range(CHUNK)]
        for u, value in enumerate(products):
            t = c * CHUNK + u
            target = jnp.where(t < live, targets[t], target_blocks)
            totals[target] += value
        return carry

    lax.fori_loop(leading, chunks, more, 0)
    grad_total[...] = jnp.zeros_like(grad_total)
    per_chunk = ROWS // block
    for copy in late:
        copy.wait()

    def outs(c):
        rows = rows_at(c, ROWS)
        return [
            pltpu.make_async_copy(x.at[rows], y.at[rows], out_sems.at[n])
            for n, (x, y) in enumerate(
                ((hidden_all, hidden), (agg_all, grad_agg), (self_all, grad_self))
            )
        ]

    def dense(c, carry):
        rows = rows_at(c, ROWS)
        blocks_at = pl.ds(c * per_chunk, per_chunk)
        total = totals[blocks_at].reshape(ROWS, 2 * width)
        inverse = 1.0 / jnp.maximum(total[:, width:], 1.0)
        aggregate = (total[:, :width] * inverse).astype(BF16)
        own = source_rows[blocks_at].reshape(ROWS, width)
        both = jnp.concatenate([own, aggregate], 1)
        preact = jnp.dot(both, w_both[...], preferred_element_type=F32)
        sigmoid = 0.5 * jnp.tanh(0.5 * preact) + 0.5
        activated = preact * sigmoid
        hidden_all[rows] = activated.astype(BF16)
        slope = sigmoid + activated * (1.0 - sigmoid)
        grad_preact = (grads_in[rows].astype(F32) * slope).astype(BF16)
        grad_total[...] += lax.dot_general(
            both, grad_preact, (((0,), (0,)), ((), ())), preferred_element_type=F32
        )
        back = lax.dot_general(
            grad_preact, w_both[...], (((1,), (1,)), ((), ())), preferred_element_type=F32
        )
        self_all[rows] = back[:, :width]
        agg_all[rows] = (back[:, width:] * inverse).astype(BF16)
        for copy in outs(c):
            copy.start()
        return carry

    steps = node_rows // ROWS
    for c in range(steps):
        dense(c, 0)
    half = grad_total.shape[1] // 2
    w_all[: grad_total.shape[0]] = grad_total[:, :half].astype(BF16)
    w_all[grad_total.shape[0] :] = grad_total[:, half:].astype(BF16)
    w_copy = pltpu.make_async_copy(w_all, grad_w, sems.at[0])
    w_copy.start()

    def drain(c, carry):
        for copy in outs(c):
            copy.wait()
        return carry

    lax.fori_loop(0, steps, drain, 0)
    w_copy.wait()


def forward(targets, sources, count, weights, features, halo, hubs, out_grad, w_self, w_nbr):
    node_rows, width = features.shape
    tiles, block, _ = weights.shape
    hidden_width = w_self.shape[1]
    parts = REPS * CORES
    part_rows = block // parts
    in_blocks = lambda value: value.reshape(-1, parts, part_rows, width)
    features = in_blocks(features)
    halo = in_blocks(halo)
    source_blocks = features.shape[0] + hubs[0].shape[0] + halo.shape[0]
    shapes = (
        jax.ShapeDtypeStruct((node_rows, hidden_width), BF16),
        jax.ShapeDtypeStruct((node_rows, width), BF16),
        jax.ShapeDtypeStruct((node_rows, width), F32),
        jax.ShapeDtypeStruct((4 * width, hidden_width // 2), BF16),
    )
    return pl.pallas_call(
        forward_kernel,
        out_shape=shapes,
        in_specs=[smem()] * 3 + [hbm()] * (6 + parts),
        out_specs=(hbm(),) * 4,
        scratch_shapes=[
            pltpu.VMEM((tiles, block, block), BF16),
            pltpu.VMEM((source_blocks, parts, part_rows, width), BF16),
            pltpu.VMEM((node_rows // block + 1, block, 2 * width), F32),
            pltpu.VMEM((2 * width, hidden_width), BF16),
            pltpu.VMEM((node_rows, hidden_width), BF16),
            pltpu.VMEM((2 * width, hidden_width), F32),
        ]
        + [pltpu.VMEM(shape.shape, shape.dtype) for shape in shapes]
        + [
            pltpu.SemaphoreType.DMA((tiles // CHUNK,)),
            pltpu.SemaphoreType.DMA((5 + parts,)),
            pltpu.SemaphoreType.DMA((3,)),
        ],
        compiler_params=params(FORWARD),
        name="forward",
    )(targets, sources, count, weights, features, halo, *hubs, out_grad, w_self, w_nbr)


def collect(live, wanted, order):
    def look(t, found):
        order[found] = t
        return found + wanted(t).astype(jnp.int32)

    found = lax.fori_loop(0, live, look, 0)
    for u in range(CHUNK):
        order[found + u] = 0
    return found


def add_tiles(found, order, chunks, targets, held, agg, totals, place, spare, arrived):
    block = held.shape[1]

    def step(c, waited):
        at = [order[c * CHUNK + u] for u in range(CHUNK)]
        last = order[jnp.minimum(c * CHUNK + CHUNK, found) - 1]
        needed = last // CHUNK + 1

        def wait(n, carry):
            arrived(n)
            return carry

        lax.fori_loop(waited, needed, wait, 0)
        products = [
            lax.dot_general(
                held[t],
                agg[rows_at(targets[t], block)],
                (((0,), (0,)), ((), ())),
                preferred_element_type=F32,
            )
            for t in at
        ]
        for u, value in enumerate(products):
            block_at = jnp.where(c * CHUNK + u < found, place(at[u]), spare)
            totals[rows_at(block_at, block)] += value
        return needed

    waited = lax.fori_loop(0, (found + CHUNK - 1) // CHUNK, step, 0)

    def rest(n, carry):
        arrived(n)
        return carry

    lax.fori_loop(waited, chunks, rest, 0)


def backward_far_kernel(
    targets,
    sources,
    count,
    weights,
    grad_agg,
    halo,
    near,
    far,
    order,
    held,
    agg,
    totals,
    halo_all,
    near_all,
    far_all,
    weight_sems,
    sems,
):
    block = weights.shape[1]
    node_rows, width = grad_agg.shape
    own_blocks = node_rows // block
    peers, slots, _ = halo.shape
    _, groups, hubs, _ = near.shape
    agg_copy = pltpu.make_async_copy(grad_agg, agg, sems.at[0])
    agg_copy.start()
    live = count[0]
    chunks = (live + CHUNK - 1) // CHUNK
    start_weights(0, chunks, weights, held, weight_sems)
    rep = lax.axis_index("rep")
    core = lax.axis_index("core")
    totals[...] = jnp.zeros_like(totals)
    found = collect(live, lambda t: sources[t] >= own_blocks, order)
    agg_copy.wait()
    add_tiles(
        found,
        order,
        chunks,
        targets,
        held,
        agg,
        totals,
        lambda t: sources[t] - own_blocks,
        totals.shape[0] // block - 1,
        lambda n: weight_copy(n, weights, held, weight_sems).wait(),
    )
    outs = [
        pltpu.make_async_copy(x, y, sems.at[n])
        for n, (x, y) in enumerate(((far_all, far), (halo_all, halo), (near_all, near)))
    ]
    halo_base = groups * CORES * REPS * hubs

    def emit_hub(piece, to_core):
        def emit(p, carry):
            for i in range(REPS):
                to_rep = lax.rem(rep + i, REPS)
                part = (p * CORES + to_core) * REPS + to_rep
                piece[i, p] = totals[rows_at(part, hubs)].astype(BF16)
            return carry

        lax.fori_loop(0, groups, emit, 0, unroll=4)

    def emit_halo(p, carry):
        at = pl.multiple_of(halo_base + p * slots, slots)
        halo_all[p] = totals[pl.ds(at, slots)].astype(BF16)
        return carry

    emit_hub(far_all, 1 - core)
    outs[0].start()
    lax.fori_loop(0, peers, emit_halo, 0, unroll=8)
    outs[1].start()
    emit_hub(near_all, core)
    outs[2].start()
    for copy in outs:
        copy.wait()


def backward_far(targets, sources, count, weights, grad_agg, peers, slots, hubs):
    node_rows, width = grad_agg.shape
    tiles, block, _ = weights.shape
    groups = peers // CORES
    total_rows = peers * REPS * hubs + peers * slots + block
    halo = jax.ShapeDtypeStruct((peers, slots, width), BF16)
    piece = jax.ShapeDtypeStruct((REPS, groups, hubs, width), BF16)
    return pl.pallas_call(
        backward_far_kernel,
        out_shape=(halo, piece, piece),
        in_specs=[smem()] * 3 + [hbm()] * 2,
        out_specs=(hbm(),) * 3,
        scratch_shapes=[
            pltpu.SMEM((tiles + CHUNK,), jnp.int32),
            pltpu.VMEM((tiles, block, block), BF16),
            pltpu.VMEM((node_rows, width), BF16),
            pltpu.VMEM((total_rows, width), F32),
            pltpu.VMEM(halo.shape, BF16),
            pltpu.VMEM(piece.shape, BF16),
            pltpu.VMEM(piece.shape, BF16),
            pltpu.SemaphoreType.DMA((tiles // CHUNK,)),
            pltpu.SemaphoreType.DMA((3,)),
        ],
        compiler_params=params(FAR),
        name="backward_far",
    )(targets, sources, count, weights, grad_agg)


def own_rows_kernel(
    targets,
    sources,
    count,
    hub_rows,
    weights,
    grad_agg,
    grad_self,
    returned,
    ids_across,
    ids_down,
    out,
    near,
    order,
    held,
    agg,
    totals,
    scattered,
    rows,
    spread,
    weight_sems,
    sems,
    out_sems,
):
    block = weights.shape[1]
    node_rows, width = grad_agg.shape
    own_blocks = node_rows // block
    slots = returned.shape[0]
    folded = node_rows // FOLDS
    copies = [
        pltpu.make_async_copy(x, y, sems.at[n])
        for n, (x, y) in enumerate(
            (
                (returned, rows),
                (grad_agg, agg),
                (grad_self, totals.at[pl.ds(0, node_rows)]),
            )
        )
    ]
    for copy in copies:
        copy.start()
    live = count[0]
    chunks = (live + CHUNK - 1) // CHUNK
    start_weights(0, chunks, weights, held, weight_sems)
    totals[node_rows:] = jnp.zeros((block, width), F32)
    found = collect(live, lambda t: sources[t] < own_blocks, order)
    down = jnp.concatenate(
        [ids_down[...], jnp.zeros((block - ids_down.shape[0], block), F32)], 0
    ).T
    copies[0].wait()
    for j in range(slots // block):
        part = pl.ds(j * block, block)
        fold = jnp.broadcast_to(down[:, j : j + 1], (block, width))
        value = rows[part].astype(F32)
        for q in range(FOLDS):
            inside = (fold >= q * folded) & (fold < (q + 1) * folded)
            spread[part, pl.ds(q * width, width)] = jnp.where(inside, value, 0.0).astype(BF16)
    across = ids_across[...] % folded
    steps = folded // FOLD_ROWS

    def spots(c):
        return [pl.ds(q * folded + c * FOLD_ROWS, FOLD_ROWS) for q in range(FOLDS)]

    for c in range(steps):
        ids = lax.broadcasted_iota(jnp.int32, (FOLD_ROWS, slots), 0) + c * FOLD_ROWS
        hot = (ids == across).astype(F32).astype(BF16)
        added = jnp.dot(hot, spread[...], preferred_element_type=F32)
        for q, at in enumerate(spots(c)):
            scattered[at] = added[:, q * width : (q + 1) * width]
    for copy in copies[1:]:
        copy.wait()
    add_tiles(
        found,
        order,
        chunks,
        targets,
        held,
        agg,
        totals,
        lambda t: sources[t],
        own_blocks,
        lambda n: weight_copy(n, weights, held, weight_sems).wait(),
    )
    outs = []
    for c in range(steps):
        for q, at in enumerate(spots(c)):
            totals[at] += scattered[at]
            outs.append(pltpu.make_async_copy(totals.at[at], out.at[at], out_sems.at[c, q]))
            outs[-1].start()
    for h in range(hub_rows.shape[0]):
        near[pl.ds(h * TILE, TILE)] = totals[rows_at(hub_rows[h] // TILE, TILE)]

    for copy in outs:
        copy.wait()


def own_rows(
    targets, sources, count, hub_rows, weights, grad_agg, grad_self, returned, send_ids
):
    node_rows, width = grad_agg.shape
    tiles, block, _ = weights.shape
    hubs = hub_rows.shape[0]
    slots = returned.shape[0] * returned.shape[1]
    return pl.pallas_call(
        own_rows_kernel,
        out_shape=(
            jax.ShapeDtypeStruct((node_rows, width), F32),
            jax.ShapeDtypeStruct((hubs * TILE, width), F32),
        ),
        in_specs=[smem()] * 4 + [hbm()] * 4 + [vmem()] * 2,
        out_specs=(hbm(), vmem()),
        scratch_shapes=[
            pltpu.SMEM((tiles + CHUNK,), jnp.int32),
            pltpu.VMEM((tiles, block, block), BF16),
            pltpu.VMEM((node_rows, width), BF16),
            pltpu.VMEM((node_rows + block, width), F32),
            pltpu.VMEM((node_rows, width), F32),
            pltpu.VMEM((slots, width), BF16),
            pltpu.VMEM((slots, FOLDS * width), BF16),
            pltpu.SemaphoreType.DMA((tiles // CHUNK,)),
            pltpu.SemaphoreType.DMA((3,)),
            pltpu.SemaphoreType.DMA((node_rows // FOLDS // FOLD_ROWS, FOLDS)),
        ],
        compiler_params=params(OWN),
        name="own_rows",
    )(
        targets,
        sources,
        count,
        hub_rows,
        weights,
        grad_agg,
        grad_self,
        returned.reshape(slots, width),
        send_ids.reshape(1, slots),
        send_ids.reshape(slots // block, block).astype(F32),
    )


def split_pair(total):
    high = total.astype(BF16)
    return high, (total - high.astype(F32)).astype(BF16)


def fold_kernel(slices, out):
    def peer(p, total):
        return total + slices[p].astype(F32)

    total = lax.fori_loop(0, slices.shape[0], peer, jnp.zeros(slices.shape[1:], F32))
    out[0], out[1] = split_pair(total)


def fold(slices):
    return pl.pallas_call(
        fold_kernel,
        out_shape=jax.ShapeDtypeStruct((2, *slices.shape[1:]), BF16),
        in_specs=[vmem()],
        out_specs=vmem(),
        compiler_params=params(8),
        name="fold",
    )(slices)


def join_kernel(near, far, w_near, w_far, *outs):
    groups = near.shape[1]
    total = (w_near[0].astype(F32) + w_near[1].astype(F32)) + (
        w_far[0].astype(F32) + w_far[1].astype(F32)
    )
    high, low = split_pair(total)
    for out in outs:
        out[groups] = high
        out[groups + 1] = low

    def group(p, carry):
        for i, out in enumerate(outs):
            out[p] = (near[i, p].astype(F32) + far[i, p].astype(F32)).astype(BF16)
        return carry

    lax.fori_loop(0, groups, group, 0)


def join(near, far, w_near, w_far):
    reps, groups, hubs, width = near.shape
    piece = jax.ShapeDtypeStruct((groups + 2, hubs, width), BF16)
    return pl.pallas_call(
        join_kernel,
        out_shape=(piece,) * reps,
        in_specs=[vmem()] * 4,
        out_specs=(vmem(),) * reps,
        compiler_params=params(8),
        name="join",
    )(near, far, w_near, w_far)


def merge_kernel(hub0, hub1, hub2, hub3, out, w_parts):
    groups, message, width = out.shape
    hubs = hub0.shape[1]
    rep = lax.axis_index("rep")
    for i, piece in enumerate((hub0, hub1, hub2, hub3)):
        w_parts[lax.rem(rep - i + REPS, REPS)] = piece[groups].astype(F32) + piece[
            groups + 1
        ].astype(F32)
    w_total = (((w_parts[0] + w_parts[1]) + w_parts[2]) + w_parts[3]).astype(BF16)

    def group(p, carry):
        total = (hub0[p].astype(F32) + hub1[p].astype(F32)) + (
            hub2[p].astype(F32) + hub3[p].astype(F32)
        )
        out[p, :hubs] = total.astype(BF16)
        out[p, hubs:] = w_total
        return carry

    lax.fori_loop(0, groups, group, 0)


def merge(pieces):
    groups, hubs, width = pieces[0].shape
    return pl.pallas_call(
        merge_kernel,
        out_shape=jax.ShapeDtypeStruct((groups - 2, 2 * hubs, width), BF16),
        in_specs=[vmem()] * 4,
        out_specs=vmem(),
        scratch_shapes=[pltpu.VMEM((REPS, hubs, width), F32)],
        compiler_params=params(8),
        name="merge",
    )(*pieces)


def finish(hub_rows, received, around, grad_nodes, hidden_width, grad_scale):
    groups, message, width = received.shape
    hubs = hub_rows.shape[0]
    w_rows = message - hubs

    def body(
        hub_rows, received, around, grad_nodes, out, grad_self, grad_nbr, near, held, wide, sems
    ):
        at = [hub_rows[h] // TILE for h in range(hubs)]
        near[...] = around[...]

        def place(p, total):
            held[rows_at(p, w_rows)] = received[p, hubs:].astype(F32) * grad_scale
            return total + received[p, :hubs].astype(F32)

        total = lax.fori_loop(0, groups, place, jnp.zeros((hubs, width), F32), unroll=4)
        for k in range(hidden_width // width):
            columns = pl.ds(k * width, width)
            for n in range(2):
                wide[n, :, columns] = held[pl.ds((2 * k + n) * width, width)]
        w_outs = [
            pltpu.make_async_copy(wide.at[n], grad, sems.at[hubs + n])
            for n, grad in enumerate((grad_self, grad_nbr))
        ]
        for copy in w_outs:
            copy.start()
        first = []
        for h in range(hubs):
            slot = jnp.int32(h)
            for j in reversed(range(h)):
                slot = jnp.where(at[j] == at[h], j, slot)
            first.append(slot)
            row = slot * TILE + hub_rows[h] % TILE
            near[pl.ds(row, 1)] += total[h : h + 1]

        def back(h):
            return pltpu.make_async_copy(
                near.at[pl.ds(h * TILE, TILE)], out.at[rows_at(at[h], TILE)], sems.at[h]
            )

        for h in range(hubs):
            pl.when(first[h] == h)(back(h).start)
        for h in range(hubs):
            pl.when(first[h] == h)(back(h).wait)
        for copy in w_outs:
            copy.wait()

    return pl.pallas_call(
        body,
        out_shape=(
            jax.ShapeDtypeStruct(grad_nodes.shape, F32),
            jax.ShapeDtypeStruct((width, hidden_width), F32),
            jax.ShapeDtypeStruct((width, hidden_width), F32),
        ),
        in_specs=[smem(), vmem(), vmem(), hbm()],
        out_specs=(hbm(),) * 3,
        input_output_aliases={3: 0},
        scratch_shapes=[
            pltpu.VMEM((hubs * TILE, width), F32),
            pltpu.VMEM((groups * w_rows, width), F32),
            pltpu.VMEM((2, width, hidden_width), F32),
            pltpu.SemaphoreType.DMA((hubs + 2,)),
        ],
        compiler_params=params(FINISH),
        name="finish",
    )(hub_rows, received, around, grad_nodes)


def rep_shift(value, shift):
    return lax.ppermute(value, "rep", [(j, (j + shift) % REPS) for j in range(REPS)])


def core_swap(value):
    return lax.ppermute(value, "core", [(0, 1), (1, 0)])


def swap(value, axes):
    return lax.all_to_all(value, axes, split_axis=0, concat_axis=0, tiled=True)


def shards(
    features,
    out_grad,
    w_self,
    w_nbr,
    hub_rows,
    send_rows,
    send_counts,
    tile_targets,
    tile_sources,
    tile_count,
    tile_weights,
):
    node_rows, width = features.shape
    peers, slots = send_rows.shape
    hubs = hub_rows.shape[0]
    groups = peers // CORES
    own_rep = swap(hub_pack(hub_rows, features, groups), GROUP)
    halo = swap(halo_pack(send_rows, send_counts, features), DOM)
    near = [own_rep] + [rep_shift(own_rep, i) for i in range(1, REPS)]
    far = [core_swap(piece) for piece in near]
    hidden, grad_agg, grad_self, grad_w = forward(
        tile_targets, tile_sources, tile_count, tile_weights, features, halo, near + far,
        out_grad, w_self, w_nbr,
    )
    w_slices = swap(grad_w.reshape(groups, -1, width), GROUP)
    grad_halo, near, far = backward_far(
        tile_targets, tile_sources, tile_count, tile_weights, grad_agg, peers, slots, hubs
    )
    returned = swap(grad_halo, DOM)
    w_pair = fold(w_slices)
    pieces = join(near, core_swap(far), w_pair, core_swap(w_pair))
    pieces = [pieces[0]] + [rep_shift(pieces[i], i) for i in range(1, REPS)]
    merged = swap(merge(pieces), GROUP)
    slot_live = jnp.arange(slots, dtype=jnp.int32)[None, :] < send_counts[:, None]
    send_ids = jnp.where(slot_live, send_rows, node_rows)
    grad_nodes, around = own_rows(
        tile_targets, tile_sources, tile_count, hub_rows, tile_weights, grad_agg, grad_self,
        returned, send_ids,
    )
    grad_scale = 1.0 / math.sqrt(node_rows * peers * REPS)
    grad_features, grad_w_self, grad_w_nbr = finish(
        hub_rows, merged, around, grad_nodes, w_self.shape[1], grad_scale
    )
    return (hidden, grad_features, grad_w_self, grad_w_nbr)


def solution(mesh):
    fine = Mesh(mesh.devices.reshape(-1, CORES, REPS), ("group", "core", "rep"))
    every = ("group", "core", "rep")
    return jax.shard_map(
        shards,
        mesh=fine,
        in_specs=(
            P(every, None),
            P(every, None),
            P(),
            P(),
            P(every),
            P(every, None),
            P(every),
            P(every),
            P(every),
            P(every),
            P(every, None, None),
        ),
        out_specs=(P(every, None), P(every, None), P(), P()),
        check_vma=False,
    )
```

```python
import math

import jax
import jax.numpy as jnp
from jax import lax
from jax.experimental import pallas as pl
from jax.experimental.pallas import tpu as pltpu
from jax.sharding import Mesh
from jax.sharding import PartitionSpec as P

BF16 = jnp.bfloat16
F32 = jnp.float32
CHUNK = 32
SIZES = (1024, 1024, 1024, 512, 512)
NEAR = 16
TILE = 8
PARTS = 4
WHOLE = 60
FORWARD = 52
FAR = 52
OWN = 52
FINISH = 16
FOLDS = 4
FOLD_ROWS = 512
REPS = 4
CORES = 2
GROUP = "group"
DOM = ("group", "core")


def smem():
    return pl.BlockSpec(memory_space=pltpu.SMEM)


def vmem():
    return pl.BlockSpec(memory_space=pltpu.VMEM)


def hbm():
    return pl.BlockSpec(memory_space=pl.ANY)


def params(mebibytes):
    return pltpu.CompilerParams(vmem_limit_bytes=mebibytes * 1024 * 1024)


def rows_at(index, size):
    return pl.ds(pl.multiple_of(index * size, size), size)


def hub_pack_kernel(hub_rows, features, out, near, wide, sems):
    hubs = hub_rows.shape[0]
    copies = []
    for h in range(hubs):
        start = pl.multiple_of(hub_rows[h] // NEAR * NEAR, NEAR)
        copies.append(
            pltpu.make_async_copy(
                features.at[pl.ds(start, NEAR)], near.at[pl.ds(h * NEAR, NEAR)], sems.at[h]
            )
        )
        copies[-1].start()
    for copy in copies:
        copy.wait()
    wide[hubs:] = near[...].astype(F32)
    for h in range(hubs):
        row = hubs + h * NEAR + hub_rows[h] % NEAR
        wide[h : h + 1] = wide[pl.ds(row, 1)]
    own_hubs = wide[:hubs].astype(BF16)

    def emit(p, carry):
        out[p] = own_hubs
        return carry

    lax.fori_loop(0, out.shape[0], emit, 0)


def hub_pack(hub_rows, features, peers):
    hubs = hub_rows.shape[0]
    width = features.shape[1]
    return pl.pallas_call(
        hub_pack_kernel,
        out_shape=jax.ShapeDtypeStruct((peers, hubs, width), BF16),
        in_specs=[smem(), hbm()],
        out_specs=vmem(),
        scratch_shapes=[
            pltpu.VMEM((hubs * NEAR, width), BF16),
            pltpu.VMEM((hubs + hubs * NEAR, width), F32),
            pltpu.SemaphoreType.DMA((hubs,)),
        ],
        compiler_params=params(WHOLE),
        name="hub_pack",
    )(hub_rows, features)


def halo_pack_kernel(send_slots, send_counts, features, out, wide, staged):
    slots, peers = send_slots.shape
    wide[...] = features[...].astype(F32)

    def peer(p, carry):
        for k in range(slots):
            staged[pl.ds(p * slots + k, 1)] = wide[pl.ds(send_slots[k, p], 1)]
        return carry

    lax.fori_loop(0, peers, peer, 0)
    slot = lax.broadcasted_iota(jnp.int32, (slots, out.shape[2]), 0)

    def emit(p, carry):
        rows = staged[rows_at(p, slots)]
        out[p] = jnp.where(slot < send_counts[p], rows, 0.0).astype(BF16)
        return carry

    lax.fori_loop(0, peers, emit, 0)


def halo_pack(send_rows, send_counts, features):
    peers, slots = send_rows.shape
    node_rows, width = features.shape
    return pl.pallas_call(
        halo_pack_kernel,
        out_shape=jax.ShapeDtypeStruct((peers, slots, width), BF16),
        in_specs=[smem(), smem(), vmem()],
        out_specs=vmem(),
        scratch_shapes=[
            pltpu.VMEM((node_rows, width), F32),
            pltpu.VMEM((peers * slots, width), F32),
        ],
        compiler_params=params(WHOLE),
        name="halo_pack",
    )(send_rows.T, send_counts, features)


def weight_copy(c, weights, held, sems):
    part = rows_at(c, CHUNK)
    return pltpu.make_async_copy(weights.at[part], held.at[part], sems.at[c])


def start_weights(first, chunks, weights, held, sems):
    def start(c, carry):
        weight_copy(c, weights, held, sems).start()
        return carry

    lax.fori_loop(first, chunks, start, 0)


def forward_kernel(
    targets,
    sources,
    count,
    weights,
    features,
    halo,
    *refs,
):
    hubs, refs = refs[: REPS * CORES], refs[REPS * CORES :]
    out_grad, w_self, w_nbr, hidden, grad_agg, grad_self, grad_w, *refs = refs
    held, source_rows, totals, w_both, grads_in, grad_total, hidden_all, *refs = refs
    agg_all, self_all, w_all, weight_sems, sems, out_sems = refs
    block = weights.shape[1]
    target_blocks, parts, part_rows, width = features.shape
    hub_blocks = hubs[0].shape[0]
    halo_blocks = halo.shape[0]
    node_rows = target_blocks * block
    rep = lax.axis_index("rep")
    core = lax.axis_index("core")
    pieces = [(features, source_rows.at[pl.ds(0, target_blocks)])]
    for c in range(CORES):
        for i in range(REPS):
            from_core = lax.rem(core + c, CORES)
            from_rep = lax.rem(rep - i + REPS, REPS)
            part = from_core * REPS + from_rep
            pieces.append(
                (hubs[c * REPS + i], source_rows.at[pl.ds(target_blocks, hub_blocks), part])
            )
    pieces.append((halo, source_rows.at[pl.ds(target_blocks + hub_blocks, halo_blocks)]))
    early = [pltpu.make_async_copy(x, y, sems.at[n]) for n, (x, y) in enumerate(pieces)]
    for copy in early:
        copy.start()
    live = count[0]
    chunks = (live + CHUNK - 1) // CHUNK
    start_weights(0, chunks, weights, held, weight_sems)
    late = [
        pltpu.make_async_copy(x, y, sems.at[len(pieces) + n])
        for n, (x, y) in enumerate(
            (
                (w_self, w_both.at[pl.ds(0, width)]),
                (w_nbr, w_both.at[pl.ds(width, width)]),
                (out_grad, grads_in),
            )
        )
    ]
    for copy in late:
        copy.start()
    ones = jnp.ones((block, width), BF16)

    def product(t):
        picked = source_rows[sources[t]].reshape(block, width)
        return jnp.dot(
            held[t], jnp.concatenate([picked, ones], 1), preferred_element_type=F32
        )

    for copy in early:
        copy.wait()
    leading = target_blocks // CHUNK

    def first(c, carry):
        weight_copy(c, weights, held, weight_sems).wait()
        for u in range(CHUNK):
            totals[c * CHUNK + u] = product(c * CHUNK + u)
        return carry

    lax.fori_loop(0, leading, first, 0)

    def more(c, carry):
        weight_copy(c, weights, held, weight_sems).wait()
        products = [product(c * CHUNK + u) for u in range(CHUNK)]
        for u, value in enumerate(products):
            t = c * CHUNK + u
            target = jnp.where(t < live, targets[t], target_blocks)
            totals[target] += value
        return carry

    lax.fori_loop(leading, chunks, more, 0)
    for copy in late:
        copy.wait()

    def outs(rows):
        return [
            pltpu.make_async_copy(x.at[rows], y.at[rows], out_sems.at[n])
            for n, (x, y) in enumerate(
                ((hidden_all, hidden), (agg_all, grad_agg), (self_all, grad_self))
            )
        ]

    def dense(start, size):
        rows = pl.ds(start, size)
        blocks_at = pl.ds(start // block, size // block)
        total = totals[blocks_at].reshape(size, 2 * width)
        inverse = 1.0 / jnp.maximum(total[:, width:], 1.0)
        aggregate = (total[:, :width] * inverse).astype(BF16)
        own = source_rows[blocks_at].reshape(size, width)
        both = jnp.concatenate([own, aggregate], 1)
        preact = jnp.dot(both, w_both[...], preferred_element_type=F32)
        sigmoid = 0.5 * jnp.tanh(0.5 * preact) + 0.5
        activated = preact * sigmoid
        hidden_all[rows] = activated.astype(BF16)
        slope = sigmoid + activated * (1.0 - sigmoid)
        grad_preact = (grads_in[rows].astype(F32) * slope).astype(BF16)
        term = lax.dot_general(
            both, grad_preact, (((0,), (0,)), ((), ())), preferred_element_type=F32
        )
        grad_total[...] = term if start == 0 else grad_total[...] + term
        back = lax.dot_general(
            grad_preact, w_both[...], (((1,), (1,)), ((), ())), preferred_element_type=F32
        )
        self_all[rows] = back[:, :width]
        agg_all[rows] = (back[:, width:] * inverse).astype(BF16)
        for copy in outs(rows):
            copy.start()

    parts_at = []
    start = 0
    for size in SIZES:
        parts_at.append((start, size))
        start += size
    for start, size in parts_at:
        dense(start, size)
    half = grad_total.shape[1] // 2
    w_all[: grad_total.shape[0]] = grad_total[:, :half].astype(BF16)
    w_all[grad_total.shape[0] :] = grad_total[:, half:].astype(BF16)
    w_copy = pltpu.make_async_copy(w_all, grad_w, sems.at[0])
    w_copy.start()

    for start, size in parts_at:
        for copy in outs(pl.ds(start, size)):
            copy.wait()
    w_copy.wait()


def forward(targets, sources, count, weights, features, halo, hubs, out_grad, w_self, w_nbr):
    node_rows, width = features.shape
    tiles, block, _ = weights.shape
    hidden_width = w_self.shape[1]
    parts = REPS * CORES
    part_rows = block // parts
    in_blocks = lambda value: value.reshape(-1, parts, part_rows, width)
    features = in_blocks(features)
    halo = in_blocks(halo)
    source_blocks = features.shape[0] + hubs[0].shape[0] + halo.shape[0]
    shapes = (
        jax.ShapeDtypeStruct((node_rows, hidden_width), BF16),
        jax.ShapeDtypeStruct((node_rows, width), BF16),
        jax.ShapeDtypeStruct((node_rows, width), F32),
        jax.ShapeDtypeStruct((4 * width, hidden_width // 2), BF16),
    )
    return pl.pallas_call(
        forward_kernel,
        out_shape=shapes,
        in_specs=[smem()] * 3 + [hbm()] * (6 + parts),
        out_specs=(hbm(),) * 4,
        scratch_shapes=[
            pltpu.VMEM((tiles, block, block), BF16),
            pltpu.VMEM((source_blocks, parts, part_rows, width), BF16),
            pltpu.VMEM((node_rows // block + 1, block, 2 * width), F32),
            pltpu.VMEM((2 * width, hidden_width), BF16),
            pltpu.VMEM((node_rows, hidden_width), BF16),
            pltpu.VMEM((2 * width, hidden_width), F32),
        ]
        + [pltpu.VMEM(shape.shape, shape.dtype) for shape in shapes]
        + [
            pltpu.SemaphoreType.DMA((tiles // CHUNK,)),
            pltpu.SemaphoreType.DMA((5 + parts,)),
            pltpu.SemaphoreType.DMA((3,)),
        ],
        compiler_params=params(FORWARD),
        name="forward",
    )(targets, sources, count, weights, features, halo, *hubs, out_grad, w_self, w_nbr)


def collect(live, wanted, order):
    def look(t, found):
        order[found] = t
        return found + wanted(t).astype(jnp.int32)

    found = lax.fori_loop(0, live, look, 0)
    for u in range(CHUNK):
        order[found + u] = 0
    return found


def add_tiles(found, order, chunks, targets, held, agg, totals, place, spare, arrived):
    block = held.shape[1]

    def step(c, waited):
        at = [order[c * CHUNK + u] for u in range(CHUNK)]
        last = order[jnp.minimum(c * CHUNK + CHUNK, found) - 1]
        needed = last // CHUNK + 1

        def wait(n, carry):
            arrived(n)
            return carry

        lax.fori_loop(waited, needed, wait, 0)
        products = [
            lax.dot_general(
                held[t],
                agg[rows_at(targets[t], block)],
                (((0,), (0,)), ((), ())),
                preferred_element_type=F32,
            )
            for t in at
        ]
        for u, value in enumerate(products):
            block_at = jnp.where(c * CHUNK + u < found, place(at[u]), spare)
            totals[rows_at(block_at, block)] += value
        return needed

    waited = lax.fori_loop(0, (found + CHUNK - 1) // CHUNK, step, 0)

    def rest(n, carry):
        arrived(n)
        return carry

    lax.fori_loop(waited, chunks, rest, 0)


def backward_far_kernel(
    targets,
    sources,
    count,
    weights,
    grad_agg,
    halo,
    near,
    far,
    order,
    held,
    agg,
    totals,
    halo_all,
    near_all,
    far_all,
    weight_sems,
    sems,
):
    block = weights.shape[1]
    node_rows, width = grad_agg.shape
    own_blocks = node_rows // block
    peers, slots, _ = halo.shape
    _, groups, hubs, _ = near.shape
    agg_copy = pltpu.make_async_copy(grad_agg, agg, sems.at[0])
    agg_copy.start()
    live = count[0]
    chunks = (live + CHUNK - 1) // CHUNK
    start_weights(0, chunks, weights, held, weight_sems)
    rep = lax.axis_index("rep")
    core = lax.axis_index("core")
    totals[...] = jnp.zeros_like(totals)
    found = collect(live, lambda t: sources[t] >= own_blocks, order)
    agg_copy.wait()
    add_tiles(
        found,
        order,
        chunks,
        targets,
        held,
        agg,
        totals,
        lambda t: sources[t] - own_blocks,
        totals.shape[0] // block - 1,
        lambda n: weight_copy(n, weights, held, weight_sems).wait(),
    )
    outs = [
        pltpu.make_async_copy(x, y, sems.at[n])
        for n, (x, y) in enumerate(((far_all, far), (halo_all, halo), (near_all, near)))
    ]
    halo_base = groups * CORES * REPS * hubs

    def emit_hub(piece, to_core):
        def emit(p, carry):
            for i in range(REPS):
                to_rep = lax.rem(rep + i, REPS)
                part = (p * CORES + to_core) * REPS + to_rep
                piece[i, p] = totals[rows_at(part, hubs)].astype(BF16)
            return carry

        lax.fori_loop(0, groups, emit, 0, unroll=4)

    def emit_halo(p, carry):
        at = pl.multiple_of(halo_base + p * slots, slots)
        halo_all[p] = totals[pl.ds(at, slots)].astype(BF16)
        return carry

    emit_hub(far_all, 1 - core)
    outs[0].start()
    lax.fori_loop(0, peers, emit_halo, 0, unroll=8)
    outs[1].start()
    emit_hub(near_all, core)
    outs[2].start()
    for copy in outs:
        copy.wait()


def backward_far(targets, sources, count, weights, grad_agg, peers, slots, hubs):
    node_rows, width = grad_agg.shape
    tiles, block, _ = weights.shape
    groups = peers // CORES
    total_rows = peers * REPS * hubs + peers * slots + block
    halo = jax.ShapeDtypeStruct((peers, slots, width), BF16)
    piece = jax.ShapeDtypeStruct((REPS, groups, hubs, width), BF16)
    return pl.pallas_call(
        backward_far_kernel,
        out_shape=(halo, piece, piece),
        in_specs=[smem()] * 3 + [hbm()] * 2,
        out_specs=(hbm(),) * 3,
        scratch_shapes=[
            pltpu.SMEM((tiles + CHUNK,), jnp.int32),
            pltpu.VMEM((tiles, block, block), BF16),
            pltpu.VMEM((node_rows, width), BF16),
            pltpu.VMEM((total_rows, width), F32),
            pltpu.VMEM(halo.shape, BF16),
            pltpu.VMEM(piece.shape, BF16),
            pltpu.VMEM(piece.shape, BF16),
            pltpu.SemaphoreType.DMA((tiles // CHUNK,)),
            pltpu.SemaphoreType.DMA((3,)),
        ],
        compiler_params=params(FAR),
        name="backward_far",
    )(targets, sources, count, weights, grad_agg)


def own_rows_kernel(
    targets,
    sources,
    count,
    hub_rows,
    weights,
    grad_agg,
    grad_self,
    returned,
    ids_across,
    ids_down,
    out,
    near,
    order,
    held,
    agg,
    totals,
    scattered,
    rows,
    spread,
    weight_sems,
    sems,
    out_sems,
):
    block = weights.shape[1]
    node_rows, width = grad_agg.shape
    own_blocks = node_rows // block
    slots = returned.shape[0]
    folded = node_rows // FOLDS
    copies = [
        pltpu.make_async_copy(x, y, sems.at[n])
        for n, (x, y) in enumerate(
            (
                (returned, rows),
                (grad_agg, agg),
                (grad_self, totals.at[pl.ds(0, node_rows)]),
            )
        )
    ]
    for copy in copies:
        copy.start()
    live = count[0]
    chunks = (live + CHUNK - 1) // CHUNK
    start_weights(0, chunks, weights, held, weight_sems)
    totals[node_rows:] = jnp.zeros((block, width), F32)
    found = collect(live, lambda t: sources[t] < own_blocks, order)
    down = jnp.concatenate(
        [ids_down[...], jnp.zeros((block - ids_down.shape[0], block), F32)], 0
    ).T
    copies[0].wait()
    for j in range(slots // block):
        part = pl.ds(j * block, block)
        fold = jnp.broadcast_to(down[:, j : j + 1], (block, width))
        value = rows[part].astype(F32)
        for q in range(FOLDS):
            inside = (fold >= q * folded) & (fold < (q + 1) * folded)
            spread[part, pl.ds(q * width, width)] = jnp.where(inside, value, 0.0).astype(BF16)
    across = ids_across[...] % folded
    steps = folded // FOLD_ROWS

    def spots(c):
        return [pl.ds(q * folded + c * FOLD_ROWS, FOLD_ROWS) for q in range(FOLDS)]

    for c in range(steps):
        ids = lax.broadcasted_iota(jnp.int32, (FOLD_ROWS, slots), 0) + c * FOLD_ROWS
        hot = (ids == across).astype(F32).astype(BF16)
        added = jnp.dot(hot, spread[...], preferred_element_type=F32)
        for q, at in enumerate(spots(c)):
            scattered[at] = added[:, q * width : (q + 1) * width]
    for copy in copies[1:]:
        copy.wait()
    add_tiles(
        found,
        order,
        chunks,
        targets,
        held,
        agg,
        totals,
        lambda t: sources[t],
        own_blocks,
        lambda n: weight_copy(n, weights, held, weight_sems).wait(),
    )
    outs = []
    for c in range(steps):
        for q, at in enumerate(spots(c)):
            totals[at] += scattered[at]
            outs.append(pltpu.make_async_copy(totals.at[at], out.at[at], out_sems.at[c, q]))
            outs[-1].start()
    for h in range(hub_rows.shape[0]):
        near[pl.ds(h * TILE, TILE)] = totals[rows_at(hub_rows[h] // TILE, TILE)]

    for copy in outs:
        copy.wait()


def own_rows(
    targets, sources, count, hub_rows, weights, grad_agg, grad_self, returned, send_ids
):
    node_rows, width = grad_agg.shape
    tiles, block, _ = weights.shape
    hubs = hub_rows.shape[0]
    slots = returned.shape[0] * returned.shape[1]
    return pl.pallas_call(
        own_rows_kernel,
        out_shape=(
            jax.ShapeDtypeStruct((node_rows, width), F32),
            jax.ShapeDtypeStruct((hubs * TILE, width), F32),
        ),
        in_specs=[smem()] * 4 + [hbm()] * 4 + [vmem()] * 2,
        out_specs=(hbm(), vmem()),
        scratch_shapes=[
            pltpu.SMEM((tiles + CHUNK,), jnp.int32),
            pltpu.VMEM((tiles, block, block), BF16),
            pltpu.VMEM((node_rows, width), BF16),
            pltpu.VMEM((node_rows + block, width), F32),
            pltpu.VMEM((node_rows, width), F32),
            pltpu.VMEM((slots, width), BF16),
            pltpu.VMEM((slots, FOLDS * width), BF16),
            pltpu.SemaphoreType.DMA((tiles // CHUNK,)),
            pltpu.SemaphoreType.DMA((3,)),
            pltpu.SemaphoreType.DMA((node_rows // FOLDS // FOLD_ROWS, FOLDS)),
        ],
        compiler_params=params(OWN),
        name="own_rows",
    )(
        targets,
        sources,
        count,
        hub_rows,
        weights,
        grad_agg,
        grad_self,
        returned.reshape(slots, width),
        send_ids.reshape(1, slots),
        send_ids.reshape(slots // block, block).astype(F32),
    )


def split_pair(total):
    high = total.astype(BF16)
    return high, (total - high.astype(F32)).astype(BF16)


def fold_kernel(slices, out):
    def peer(p, total):
        return total + slices[p].astype(F32)

    total = lax.fori_loop(0, slices.shape[0], peer, jnp.zeros(slices.shape[1:], F32))
    out[0], out[1] = split_pair(total)


def fold(slices):
    return pl.pallas_call(
        fold_kernel,
        out_shape=jax.ShapeDtypeStruct((2, *slices.shape[1:]), BF16),
        in_specs=[vmem()],
        out_specs=vmem(),
        compiler_params=params(8),
        name="fold",
    )(slices)


def join_kernel(near, far, w_near, w_far, *outs):
    groups = near.shape[1]
    total = (w_near[0].astype(F32) + w_near[1].astype(F32)) + (
        w_far[0].astype(F32) + w_far[1].astype(F32)
    )
    high, low = split_pair(total)
    for out in outs:
        out[groups] = high
        out[groups + 1] = low

    def group(p, carry):
        for i, out in enumerate(outs):
            out[p] = (near[i, p].astype(F32) + far[i, p].astype(F32)).astype(BF16)
        return carry

    lax.fori_loop(0, groups, group, 0)


def join(near, far, w_near, w_far):
    reps, groups, hubs, width = near.shape
    piece = jax.ShapeDtypeStruct((groups + 2, hubs, width), BF16)
    return pl.pallas_call(
        join_kernel,
        out_shape=(piece,) * reps,
        in_specs=[vmem()] * 4,
        out_specs=(vmem(),) * reps,
        compiler_params=params(8),
        name="join",
    )(near, far, w_near, w_far)


def merge_kernel(hub0, hub1, hub2, hub3, out, w_parts):
    groups, message, width = out.shape
    hubs = hub0.shape[1]
    rep = lax.axis_index("rep")
    for i, piece in enumerate((hub0, hub1, hub2, hub3)):
        w_parts[lax.rem(rep - i + REPS, REPS)] = piece[groups].astype(F32) + piece[
            groups + 1
        ].astype(F32)
    w_total = (((w_parts[0] + w_parts[1]) + w_parts[2]) + w_parts[3]).astype(BF16)

    def group(p, carry):
        total = (hub0[p].astype(F32) + hub1[p].astype(F32)) + (
            hub2[p].astype(F32) + hub3[p].astype(F32)
        )
        out[p, :hubs] = total.astype(BF16)
        out[p, hubs:] = w_total
        return carry

    lax.fori_loop(0, groups, group, 0)


def merge(pieces):
    groups, hubs, width = pieces[0].shape
    return pl.pallas_call(
        merge_kernel,
        out_shape=jax.ShapeDtypeStruct((groups - 2, 2 * hubs, width), BF16),
        in_specs=[vmem()] * 4,
        out_specs=vmem(),
        scratch_shapes=[pltpu.VMEM((REPS, hubs, width), F32)],
        compiler_params=params(8),
        name="merge",
    )(*pieces)


def finish(hub_rows, received, around, grad_nodes, hidden_width, grad_scale):
    groups, message, width = received.shape
    hubs = hub_rows.shape[0]
    w_rows = message - hubs

    def body(
        hub_rows, received, around, grad_nodes, out, grad_self, grad_nbr, near, held, wide, sems
    ):
        at = [hub_rows[h] // TILE for h in range(hubs)]
        near[...] = around[...]

        def place(p, total):
            held[rows_at(p, w_rows)] = received[p, hubs:].astype(F32) * grad_scale
            return total + received[p, :hubs].astype(F32)

        total = lax.fori_loop(0, groups, place, jnp.zeros((hubs, width), F32), unroll=4)
        for k in range(hidden_width // width):
            columns = pl.ds(k * width, width)
            for n in range(2):
                wide[n, :, columns] = held[pl.ds((2 * k + n) * width, width)]
        w_outs = [
            pltpu.make_async_copy(wide.at[n], grad, sems.at[hubs + n])
            for n, grad in enumerate((grad_self, grad_nbr))
        ]
        for copy in w_outs:
            copy.start()
        first = []
        for h in range(hubs):
            slot = jnp.int32(h)
            for j in reversed(range(h)):
                slot = jnp.where(at[j] == at[h], j, slot)
            first.append(slot)
            row = slot * TILE + hub_rows[h] % TILE
            near[pl.ds(row, 1)] += total[h : h + 1]

        def back(h):
            return pltpu.make_async_copy(
                near.at[pl.ds(h * TILE, TILE)], out.at[rows_at(at[h], TILE)], sems.at[h]
            )

        for h in range(hubs):
            pl.when(first[h] == h)(back(h).start)
        for h in range(hubs):
            pl.when(first[h] == h)(back(h).wait)
        for copy in w_outs:
            copy.wait()

    return pl.pallas_call(
        body,
        out_shape=(
            jax.ShapeDtypeStruct(grad_nodes.shape, F32),
            jax.ShapeDtypeStruct((width, hidden_width), F32),
            jax.ShapeDtypeStruct((width, hidden_width), F32),
        ),
        in_specs=[smem(), vmem(), vmem(), hbm()],
        out_specs=(hbm(),) * 3,
        input_output_aliases={3: 0},
        scratch_shapes=[
            pltpu.VMEM((hubs * TILE, width), F32),
            pltpu.VMEM((groups * w_rows, width), F32),
            pltpu.VMEM((2, width, hidden_width), F32),
            pltpu.SemaphoreType.DMA((hubs + 2,)),
        ],
        compiler_params=params(FINISH),
        name="finish",
    )(hub_rows, received, around, grad_nodes)


def rep_shift(value, shift):
    return lax.ppermute(value, "rep", [(j, (j + shift) % REPS) for j in range(REPS)])


def core_swap(value):
    return lax.ppermute(value, "core", [(0, 1), (1, 0)])


def swap(value, axes):
    return lax.all_to_all(value, axes, split_axis=0, concat_axis=0, tiled=True)


def shards(
    features,
    out_grad,
    w_self,
    w_nbr,
    hub_rows,
    send_rows,
    send_counts,
    tile_targets,
    tile_sources,
    tile_count,
    tile_weights,
):
    node_rows, width = features.shape
    peers, slots = send_rows.shape
    hubs = hub_rows.shape[0]
    groups = peers // CORES
    own_rep = swap(hub_pack(hub_rows, features, groups), GROUP)
    halo = swap(halo_pack(send_rows, send_counts, features), DOM)
    near = [own_rep] + [rep_shift(own_rep, i) for i in range(1, REPS)]
    far = [core_swap(piece) for piece in near]
    hidden, grad_agg, grad_self, grad_w = forward(
        tile_targets, tile_sources, tile_count, tile_weights, features, halo, near + far,
        out_grad, w_self, w_nbr,
    )
    w_slices = swap(grad_w.reshape(groups, -1, width), GROUP)
    grad_halo, near, far = backward_far(
        tile_targets, tile_sources, tile_count, tile_weights, grad_agg, peers, slots, hubs
    )
    returned = swap(grad_halo, DOM)
    w_pair = fold(w_slices)
    pieces = join(near, core_swap(far), w_pair, core_swap(w_pair))
    pieces = [pieces[0]] + [rep_shift(pieces[i], i) for i in range(1, REPS)]
    merged = swap(merge(pieces), GROUP)
    slot_live = jnp.arange(slots, dtype=jnp.int32)[None, :] < send_counts[:, None]
    send_ids = jnp.where(slot_live, send_rows, node_rows)
    grad_nodes, around = own_rows(
        tile_targets, tile_sources, tile_count, hub_rows, tile_weights, grad_agg, grad_self,
        returned, send_ids,
    )
    grad_scale = 1.0 / math.sqrt(node_rows * peers * REPS)
    grad_features, grad_w_self, grad_w_nbr = finish(
        hub_rows, merged, around, grad_nodes, w_self.shape[1], grad_scale
    )
    return (hidden, grad_features, grad_w_self, grad_w_nbr)


def solution(mesh):
    fine = Mesh(mesh.devices.reshape(-1, CORES, REPS), ("group", "core", "rep"))
    every = ("group", "core", "rep")
    return jax.shard_map(
        shards,
        mesh=fine,
        in_specs=(
            P(every, None),
            P(every, None),
            P(),
            P(),
            P(every),
            P(every, None),
            P(every),
            P(every),
            P(every),
            P(every),
            P(every, None, None),
        ),
        out_specs=(P(every, None), P(every, None), P(), P()),
        check_vma=False,
    )
```
